32 devices in a mesh: rep: 8 (over z, y), shard: 4 (over x, core).
Axes of the slice: x: 2, y: 2, z: 4, core: 2. Of those that a mesh axis runs over, the one named last changes fastest.
Arguments:
- tokens: bfloat16 [8, 1024, 768], P('rep', 'shard'), may hold values from -6 to 6
- encoded: bfloat16 [8, 1024, 768], P('rep', 'shard'), may hold values from -6 to 6
- block_ids: int32 [8, 1024], P('rep', 'shard'), may hold values from 0 to 7, never falling along the last dimension, each value on 1 to 256 neighbouring positions
- buckets: int32 [2047], replicated, may hold values from 0 to 31
- cotangent: bfloat16 [8, 1024, 768], P('rep', 'shard'), may hold values from -6 to 6
- norm_self: bfloat16 [768], P('shard'), may hold values from 0.25 to 1.75
- self_query: bfloat16 [768, 768], P('shard'), may hold values from -0.02734375 to 0.02734375
- self_keyval: bfloat16 [2, 768, 768], P(None, 'shard'), may hold values from -0.21875 to 0.21875
- self_output: bfloat16 [768, 768], P('shard'), may hold values from -1.75 to 1.75
- bucket_bias: bfloat16 [12, 32], P(None, 'shard'), may hold values from -4 to 4
- norm_cross: bfloat16 [768], P('shard'), may hold values from 0.25 to 1.75
- cross_query: bfloat16 [768, 768], P('shard'), may hold values from -0.02734375 to 0.02734375
- cross_keyval: bfloat16 [2, 768, 768], P(None, 'shard'), may hold values from -0.21875 to 0.21875
- cross_output: bfloat16 [768, 768], P('shard'), may hold values from -1.75 to 1.75
- norm_feed: bfloat16 [768], P('shard'), may hold values from 0.25 to 1.75
- feed_in: bfloat16 [768, 3072], P('shard'), may hold values from -0.21875 to 0.21875
- feed_out: bfloat16 [3072, 768], P('shard'), may hold values from -0.15625 to 0.15625
Outputs:
- result: bfloat16 [8, 1024, 768], P('rep', 'shard')
- d_tokens: float32 [8, 1024, 768], P('rep', 'shard')
- d_encoded: float32 [8, 1024, 768], P('rep', 'shard')
- d_norm_self: float32 [768], P('shard')
- d_self_query: float32 [768, 768], P('shard')
- d_self_keyval: float32 [2, 768, 768], P(None, 'shard')
- d_self_output: float32 [768, 768], P('shard')
- d_bucket_bias: float32 [12, 32], P(None, 'shard')
- d_norm_cross: float32 [768], P('shard')
- d_cross_query: float32 [768, 768], P('shard')
- d_cross_keyval: float32 [2, 768, 768], P(None, 'shard')
- d_cross_output: float32 [768, 768], P('shard')
- d_norm_feed: float32 [768], P('shard')
- d_feed_in: float32 [768, 3072], P('shard')
- d_feed_out: float32 [3072, 768], P('shard')
The draws below stay inside these ranges and needn't reach their ends.
Inputs may be any that keep to these rules, and one draw needn't show every extreme that they name: `block_ids`: never falls along a sequence; at most 256 positions of a sequence share a number. `buckets`: entry 1023 + k serves a key k positions after its query.
All inputs are finite; a program needn't handle non-finite values.
Results may differ from the reference program's by a relative error of at most 0.025.
Values may be sent and summed in bfloat16 or wider, within the bound.
A program may use at most 192 MiB of HBM per device.

```python
import math
import jax
import jax.numpy as jnp
import numpy as np
from jax import lax

D = 768
H = 12
HD = 64
FF = 3072
NB = 32
BLOCK = 256
ENC = 1024
LEN = 1024
SEQS = 8


def set_ends(entries, own_key, low, largest):
    shape = entries.shape
    index_at = [jax.random.randint(jax.random.fold_in(own_key, axis), (), 0, shape[axis]) for axis in range(len(shape))]
    entries = entries.at[tuple(index_at)].set(low)
    longest = shape.index(max(shape))
    index_at[longest] = (index_at[longest] + 1) % shape[longest]
    return entries.at[tuple(index_at)].set(largest)


def level_of(rng, extent, split, smallest, high):
    factor_of = 1.0
    for dim, shards_of in split:
        draws = jax.random.uniform(jax.random.fold_in(jax.random.fold_in(rng, 6), dim), (shards_of,), jnp.float32, smallest / len(split), high / len(split))
        factor_of = factor_of * jnp.repeat(jnp.exp(draws), extent[dim] // shards_of).reshape((-1,) + (1,) * (len(extent) - 1 - dim))
    return factor_of


def profile(count, total, limit, lean):
    portions = [(1 << 20) // math.isqrt(grade ** lean) + 1 for grade in range(2, count + 1)]
    surplus, holding = total - limit - (count - 1), [1] * (count - 1)
    while surplus > 0:
        movable = [i for i in range(count - 1) if holding[i] < limit]
        whole, remaining = sum([portions[i] for i in movable]), surplus
        for i in movable:
            more = min(limit - holding[i], max(1, remaining * portions[i] // whole), surplus)
            holding[i] = holding[i] + more
            surplus = surplus - more
    return np.array([limit] + holding)


def uneven_parts(stream_key, number_of, total, bound, slope):
    if number_of == 2:
        one = jax.random.randint(stream_key, (), max(1, total - bound), min(bound, total - 1) + 1)
        return jnp.stack([one, total - one])
    lengths = jnp.asarray(profile(number_of, total, bound, slope), jnp.int32)
    twos = (number_of - 1) // 2
    donor, receiver = lengths[1:1 + 2 * twos:2], lengths[2:2 + 2 * twos:2]
    margin = jnp.minimum(donor - 1, bound - receiver)
    moved = jax.random.randint(jax.random.fold_in(stream_key, 1), (twos,), 0, 1 << 20) % (margin + 1)
    lengths = lengths.at[1:1 + 2 * twos:2].set(donor - moved).at[2:2 + 2 * twos:2].set(receiver + moved)
    return lengths[jax.random.permutation(jax.random.fold_in(stream_key, 2), number_of)]


def scatter_about(stream_key, shape, spread, reach, pieces=(), kind=jnp.bfloat16):
    array = jax.random.normal(stream_key, shape, jnp.float32) * spread
    if len(pieces) > 0:
        array = level_of(stream_key, shape, pieces, -0.22, 0.18) * array
    return jnp.clip(array, min=-reach, max=reach).astype(kind)


def setup_inputs(seed: int = 0) -> dict:
    arg_keys = jax.random.split(jax.random.key(seed), 18)
    return {
        "tokens": scatter_about(arg_keys[0], (SEQS, LEN, D), 1.0, 6.0, ((0, 8), (1, 4))),
        "encoded": scatter_about(arg_keys[1], (SEQS, ENC, D), 1.0, 6.0, ((0, 8), (1, 4))),
        "block_ids": jax.vmap(lambda own: jnp.searchsorted(jnp.cumsum(uneven_parts(own, 2 * LEN // BLOCK, LEN, BLOCK, 0)), jnp.arange(LEN), side="right"))(jax.random.split(arg_keys[2], SEQS)).reshape((SEQS, LEN)).astype(jnp.int32),
        "buckets": set_ends(jax.random.randint(arg_keys[3], (2 * LEN - 1,), 0, NB), jax.random.fold_in(arg_keys[3], 1), 0, NB - 1).astype(jnp.int32),
        "cotangent": scatter_about(arg_keys[4], (SEQS, LEN, D), 1.0, 6.0, ((0, 8), (1, 4))),
        "norm_self": jnp.clip(1.0 + 0.15 * jax.random.normal(arg_keys[5], (D,), jnp.float32), 0.25, 1.75).astype(jnp.bfloat16),
        "self_query": scatter_about(arg_keys[6], (D, D), (D * HD) ** -0.5, 0.02734375, ((0, 4),)),
        "self_keyval": scatter_about(arg_keys[7], (2, D, D), D ** -0.5, 0.21875, ((1, 4),)),
        "self_output": scatter_about(arg_keys[8], (D, D), (D // 64) ** -0.5, 1.75, ((0, 4),)),
        "bucket_bias": scatter_about(arg_keys[9], (H, NB), 0.7, 4.0, ((1, 4),)),
        "norm_cross": jnp.clip(1.0 + 0.15 * jax.random.normal(arg_keys[10], (D,), jnp.float32), 0.25, 1.75).astype(jnp.bfloat16),
        "cross_query": scatter_about(arg_keys[11], (D, D), (D * HD) ** -0.5, 0.02734375, ((0, 4),)),
        "cross_keyval": scatter_about(arg_keys[12], (2, D, D), D ** -0.5, 0.21875, ((1, 4),)),
        "cross_output": scatter_about(arg_keys[13], (D, D), (D // 64) ** -0.5, 1.75, ((0, 4),)),
        "norm_feed": jnp.clip(1.0 + 0.15 * jax.random.normal(arg_keys[14], (D,), jnp.float32), 0.25, 1.75).astype(jnp.bfloat16),
        "feed_in": scatter_about(arg_keys[15], (D, FF), D ** -0.5, 0.21875, ((0, 4),)),
        "feed_out": scatter_about(arg_keys[16], (FF, D), (FF // 2) ** -0.5, 0.15625, ((0, 4),)),
    }


EPSILON = 1e-06
MASKED = -1e+30
TOP_PRECISION = lax.Precision.HIGHEST

@jax.custom_vjp
def low(v):
    return lax.optimization_barrier(v.astype(jnp.bfloat16)).astype(jnp.float32)

@jax.custom_vjp
def low_back(v):
    return v

def low_keep(v):
    return (low(v), None)

def low_pass(kept, grad):
    return (grad,)

def back_keep(v):
    return (v, None)

def back_low(kept, grad):
    return (low(grad),)
low.defvjp(low_keep, low_pass)
low_back.defvjp(back_keep, back_low)

def rounded_both(values):
    return low(low_back(values))

def normalize(values, gain):
    return values * lax.rsqrt(lax.optimization_barrier(jnp.mean(values * values, axis=-1, keepdims=True)) + EPSILON) * gain

def split_heads(values):
    return values.reshape(values.shape[0], values.shape[1], H, HD)

def project(values, weight):
    return jnp.einsum('gld,de->gle', values, weight, precision=TOP_PRECISION)

def attention(query, key_rows, value_rows, score_correction, step_rows):
    groups, length = (query.shape[0], query.shape[1])

    def query_block(anchor):
        picked = lax.dynamic_slice_in_dim(query, anchor, step_rows, 1)
        scores = low_back(jnp.einsum('gqhd,gkhd->ghqk', picked, key_rows, precision=TOP_PRECISION))
        weights = low(jax.nn.softmax(score_correction(scores, anchor), axis=-1))
        return jnp.einsum('ghqk,gkhd->gqhd', weights, value_rows, precision=TOP_PRECISION)
    anchors = jnp.arange(length // step_rows, dtype=jnp.int32) * step_rows
    blocks_out = lax.map(jax.checkpoint(query_block), anchors)
    return jnp.moveaxis(blocks_out, 0, 1).reshape(groups, length, H * HD)

def layer(params, tokens, encoded, block_ids, buckets):
    norm_self, self_query, self_keyval, self_output, bucket_bias, norm_cross, cross_query, cross_keyval, cross_output, norm_feed, feed_in, feed_out = params
    length = tokens.shape[1]
    step_rows = min(512, length)
    positions = jnp.arange(length, dtype=jnp.int32)

    def self_adjust(scores, anchor):
        row_pos = anchor + jnp.arange(step_rows, dtype=jnp.int32)
        offsets = positions[None, :] - row_pos[:, None] + (length - 1)
        bias_block = jnp.take(bucket_bias, jnp.take(buckets, offsets), axis=1)
        row_blocks = lax.dynamic_slice_in_dim(block_ids, anchor, step_rows, 1)
        allowed = block_ids[:, None, :] <= row_blocks[:, :, None]
        return jnp.where(allowed[:, None], scores + bias_block[None], MASKED)

    def plain_adjust(scores, anchor):
        return scores
    normed = low(normalize(tokens, norm_self))
    query = rounded_both(project(normed, self_query))
    keyval = rounded_both(jnp.einsum('gld,cde->cgle', normed, self_keyval, precision=TOP_PRECISION))
    attended = rounded_both(attention(split_heads(query), split_heads(keyval[0]), split_heads(keyval[1]), self_adjust, step_rows))
    first = tokens + low_back(project(attended, self_output))
    normed = low(normalize(first, norm_cross))
    query = rounded_both(project(normed, cross_query))
    keyval = rounded_both(jnp.einsum('gmd,cde->cgme', encoded, cross_keyval, precision=TOP_PRECISION))
    attended = rounded_both(attention(split_heads(query), split_heads(keyval[0]), split_heads(keyval[1]), plain_adjust, step_rows))
    second = first + low_back(project(attended, cross_output))
    normed = low(normalize(second, norm_feed))
    hidden = low(jax.nn.gelu(low_back(project(normed, feed_in))))
    return second + low_back(project(hidden, feed_out))

def reference(tokens, encoded, block_ids, buckets, cotangent, norm_self, self_query, self_keyval, self_output, bucket_bias, norm_cross, cross_query, cross_keyval, cross_output, norm_feed, feed_in, feed_out):
    params = tuple((weight.astype(jnp.float32) for weight in (norm_self, self_query, self_keyval, self_output, bucket_bias, norm_cross, cross_query, cross_keyval, cross_output, norm_feed, feed_in, feed_out)))
    sequences, length = (tokens.shape[0], tokens.shape[1])
    per_step = math.gcd(sequences, max(1, 4096 // length))
    steps_count = sequences // per_step

    def grouped(values):
        return values.reshape((steps_count, per_step) + values.shape[1:])

    def visit(totals, batch_slice):
        inputs, memory, blocks_here, cotangent_here = batch_slice

        def forward(weights_here, inputs_here, memory_here):
            return layer(weights_here, inputs_here, memory_here, blocks_here, buckets)
        outcome, pullback = jax.vjp(forward, params, inputs, memory)
        d_params, d_inputs, d_memory = pullback(cotangent_here)
        totals = jax.tree.map(jnp.add, totals, d_params)
        return (totals, (outcome.astype(jnp.bfloat16), d_inputs, d_memory))
    zeros_start = jax.tree.map(jnp.zeros_like, params)
    totals, (outcome, d_tokens, d_encoded) = lax.scan(visit, zeros_start, (grouped(tokens.astype(jnp.float32)), grouped(encoded.astype(jnp.float32)), grouped(block_ids), grouped(cotangent.astype(jnp.float32))))
    return (outcome.reshape(tokens.shape), d_tokens.reshape(tokens.shape), d_encoded.reshape(encoded.shape), totals[0], totals[1], totals[2], totals[3], totals[4], totals[5], totals[6], totals[7], totals[8], totals[9], totals[10], totals[11])
```

```python
import functools
import types

import jax
import jax.numpy as jnp
from jax import lax
from jax.experimental import pallas as pl
from jax.experimental.pallas import tpu as pltpu
from jax.sharding import PartitionSpec as P

H = 12
HD = 64
LANES = 2 * HD
EPSILON = 1e-06
MASKED = -1e30
F32 = jnp.float32
BF16 = jnp.bfloat16
VMEM_LIMIT = 56 * 2**20
FUSED_LIMIT = 62 * 2**20
AHEAD = 2
SLOTS = 4
MESH = pl.DeviceIdType.MESH


def dot(a, b):
    return lax.dot_general(a, b, (((1,), (0,)), ((), ())), preferred_element_type=F32)


def dot_nt(a, b):
    return lax.dot_general(a, b, (((1,), (1,)), ((), ())), preferred_element_type=F32)


def dot_tn(a, b):
    return lax.dot_general(a, b, (((0,), (0,)), ((), ())), preferred_element_type=F32)


def rms_scale(values):
    return lax.rsqrt(jnp.mean(values * values, axis=-1, keepdims=True) + EPSILON)


def rms_back(values, gain, grad):
    scale = rms_scale(values)
    scaled = gain * grad
    mean = jnp.mean(scaled * values, axis=-1, keepdims=True)
    d_values = scale * scaled - values * (scale * scale * scale) * mean
    d_gain = jnp.sum(grad * values * scale, axis=0, keepdims=True)
    return d_values, d_gain


def gelu_parts(x):
    c = 0.7978845608028654
    t = jnp.tanh(c * (x + 0.044715 * (x * x * x)))
    value = 0.5 * x * (1.0 + t)
    slope = 0.5 * (1.0 + t) + 0.5 * x * (1.0 - t * t) * (c * (1.0 + 3.0 * 0.044715 * (x * x)))
    return value, slope


def own_lanes(first):
    lane = lax.broadcasted_iota(jnp.int32, (1, LANES), 1)
    mine = (lane < HD) if first else (lane >= HD)
    return jnp.where(mine, 1.0, 0.0)


def stack_heads(pair):
    one, two = own_lanes(True).astype(pair.dtype), own_lanes(False).astype(pair.dtype)
    return jnp.concatenate([pair * one, pair * two], axis=0)


def merge_heads(stacked):
    rows = stacked.shape[0] // 2
    return stacked[:rows] * own_lanes(True) + stacked[rows:] * own_lanes(False)


def skew(window, width):
    sub = lax.broadcasted_iota(jnp.int32, (8, width), 0)
    rows = jnp.broadcast_to(window, (8, width))
    for bit in (1, 2, 4):
        rows = jnp.where((sub & bit) != 0, pltpu.roll(rows, bit, 1), rows)
    return jnp.concatenate(
        [pltpu.roll(rows, (8 * g + width - 128) % width, 1) for g in range(16)], axis=0
    )


def unskew(total, width):
    sub = lax.broadcasted_iota(jnp.int32, (8, width), 0)
    rows = jnp.zeros((8, width), F32)
    for g in range(16):
        rows = rows + pltpu.roll(total[8 * g : 8 * g + 8], 128 - 8 * g, 1)
    for bit in (1, 2, 4):
        rows = jnp.where((sub & bit) != 0, pltpu.roll(rows, width - bit, 1), rows)
    return jnp.sum(rows, axis=0, keepdims=True)


def attend_kernel(biased, q_ref, k_ref, v_ref, *refs):
    if biased:
        row_ids, key_ids, window_ref, out_ref, p_ref = refs
    else:
        out_ref, p_ref = refs
    rows, length = q_ref.shape[0], k_ref.shape[0]
    blocks = rows // 128
    scores = dot_nt(stack_heads(q_ref[...]), k_ref[...])
    for head in range(2):
        if biased:
            width = window_ref.shape[2]
            table = skew(window_ref[0, head : head + 1, :], width)
        for b in range(blocks):
            at = head * rows + b * 128
            part = scores[at : at + 128]
            if biased:
                shift = (blocks - 1 - b) * 128
                allowed = key_ids[...] <= row_ids[b * 128 : b * 128 + 128, :]
                part = jnp.where(allowed, part + table[:, shift : shift + length], MASKED)
            top = jnp.max(part, axis=-1, keepdims=True)
            raised = jnp.exp(part - top)
            share = 1.0 / jnp.sum(raised, axis=-1, keepdims=True)
            p_ref[0, at : at + 128, :] = (raised * share).astype(BF16)
    out_ref[...] = merge_heads(dot(p_ref[0], v_ref[...]))


def attend_back_kernel(folded, q_ref, k_ref, v_ref, p_ref, out_ref, grad_ref, *refs):
    if folded:
        dq_ref, dk_ref, dv_ref, window_ref, ds_ref = refs
    else:
        dq_ref, dk_ref, dv_ref, ds_ref = refs
    rows, length = q_ref.shape[0], k_ref.shape[0]
    blocks = rows // 128
    grad = grad_ref[...]
    grads = stack_heads(grad)
    delta_wide = grad.astype(F32) * out_ref[...]
    d_weights = dot_nt(grads, v_ref[...])
    for head in range(2):
        if folded:
            width = window_ref.shape[2]
            total = jnp.zeros((128, width), F32)
        delta = jnp.sum(delta_wide * own_lanes(head == 0), axis=-1, keepdims=True)
        for b in range(blocks):
            at = head * rows + b * 128
            part = p_ref[0, at : at + 128, :].astype(F32) * (
                d_weights[at : at + 128] - delta[b * 128 : b * 128 + 128]
            )
            ds_ref[at : at + 128, :] = part.astype(BF16)
            if folded:
                shift = (blocks - 1 - b) * 128
                pieces = [part]
                if shift:
                    pieces = [jnp.zeros((128, shift), F32)] + pieces
                if width - shift - length:
                    pieces = pieces + [jnp.zeros((128, width - shift - length), F32)]
                total = total + jnp.concatenate(pieces, axis=1)
        if folded:
            window_ref[0, head : head + 1, :] = unskew(total, width)
    queries = stack_heads(q_ref[...])
    dq_ref[...] = merge_heads(dot(ds_ref[...], k_ref[...])).astype(BF16)
    dk_ref[...] = dot(queries.T, ds_ref[...]).T.astype(BF16)
    dv_ref[...] = dot(grads.T, p_ref[0]).T.astype(BF16)


def attend(query, keys, values, bias=None):
    rows, width = query.shape
    length = keys.shape[0]
    pairs = width // LANES
    column = lambda n: pl.BlockSpec((n, LANES), lambda i: (0, i))
    whole = lambda a: pl.BlockSpec(a.shape, lambda i: (0,) * a.ndim)
    operands, specs = [query, keys, values], [column(rows), column(length), column(length)]
    if bias is not None:
        row_ids, key_ids, window = bias
        operands += [row_ids, key_ids, window]
        specs += [
            whole(row_ids),
            whole(key_ids),
            pl.BlockSpec((1,) + window.shape[1:], lambda i: (i, 0, 0)),
        ]
    return pl.pallas_call(
        functools.partial(attend_kernel, bias is not None),
        grid=(pairs,),
        in_specs=specs,
        out_specs=[
            column(rows),
            pl.BlockSpec((1, 2 * rows, length), lambda i: (i, 0, 0)),
        ],
        out_shape=[
            jax.ShapeDtypeStruct((rows, width), F32),
            jax.ShapeDtypeStruct((pairs, 2 * rows, length), BF16),
        ],
        compiler_params=pltpu.CompilerParams(vmem_limit_bytes=VMEM_LIMIT),
        cost_estimate=pl.CostEstimate(
            flops=16 * rows * length * width,
            bytes_accessed=2 * pairs * 2 * rows * length,
            transcendentals=pairs * 2 * rows * length,
        ),
    )(*operands)


def attend_back(query, keys, values, weights, output, grad, window_shape=None):
    rows, width = query.shape
    length = keys.shape[0]
    pairs = width // LANES
    column = lambda n: pl.BlockSpec((n, LANES), lambda i: (0, i))
    out_specs = [column(rows), column(length), column(length)]
    out_shape = [
        jax.ShapeDtypeStruct((rows, width), BF16),
        jax.ShapeDtypeStruct((length, width), BF16),
        jax.ShapeDtypeStruct((length, width), BF16),
    ]
    if window_shape is not None:
        out_specs.append(pl.BlockSpec((1,) + window_shape[1:], lambda i: (i, 0, 0)))
        out_shape.append(jax.ShapeDtypeStruct(window_shape, F32))
    return pl.pallas_call(
        functools.partial(attend_back_kernel, window_shape is not None),
        grid=(pairs,),
        in_specs=[
            column(rows),
            column(length),
            column(length),
            pl.BlockSpec((1, 2 * rows, length), lambda i: (i, 0, 0)),
            column(rows),
            column(rows),
        ],
        out_specs=out_specs,
        out_shape=out_shape,
        scratch_shapes=[pltpu.VMEM((2 * rows, length), BF16)],
        compiler_params=pltpu.CompilerParams(vmem_limit_bytes=VMEM_LIMIT),
        cost_estimate=pl.CostEstimate(
            flops=32 * rows * length * width,
            bytes_accessed=2 * pairs * 2 * rows * length,
            transcendentals=0,
        ),
    )(query, keys, values, weights, output, grad)


def gather(values, axis=0):
    return lax.all_gather(values, "shard", axis=axis, tiled=True)


def scatter(values, axis=0):
    return lax.psum_scatter(values.astype(BF16), "shard", scatter_dimension=axis, tiled=True)


class Place:
    def __init__(self, reps, shards):
        self.nx, self.nz = shards // 2, reps // 2
        rep, shard = lax.axis_index("rep"), lax.axis_index("shard")
        self.rep, self.shard = rep, shard
        self.core, self.x = lax.rem(shard, 2), lax.div(shard, 2)
        self.y, self.z = lax.rem(rep, 2), lax.div(rep, 2)

    def other_core(self):
        return (self.rep, self.x * 2 + 1 - self.core)

    def x_at(self, step):
        x = lax.rem(self.x + step, self.nx)
        return x, (self.rep, x * 2 + self.core)

    def other_y(self):
        return (self.z * 2 + 1 - self.y, self.shard)

    def z_at(self, step):
        z = lax.rem(self.z + step, self.nz)
        return z, (z * 2 + self.y, self.shard)

    def partners(self):
        found = [self.other_core(), self.other_y()]
        found += [self.x_at(d)[1] for d in range(1, self.nx)]
        found += [self.z_at(d)[1] for d in range(1, self.nz)]
        return found


def enter(place):
    barrier = pltpu.get_barrier_semaphore()
    partners = place.partners()
    for device in partners:
        pl.semaphore_signal(barrier, inc=1, device_id=device, device_id_type=MESH)
    pl.semaphore_wait(barrier, len(partners))


def remote(src, dst, send, recv, device):
    return pltpu.make_async_remote_copy(
        src_ref=src, dst_ref=dst, send_sem=send, recv_sem=recv, device_id=device, device_id_type=MESH
    )


def added(*parts):
    total = parts[0].astype(F32)
    for part in parts[1:]:
        total = total + part.astype(F32)
    return total


class Reduction:
    def __init__(self, place, recv_a, recv_b, recv_c, recv_d, fin, send, recv, own_sem):
        self.place, self.recv_a, self.recv_b = place, recv_a, recv_b
        self.recv_c, self.recv_d, self.fin = recv_c, recv_d, fin
        self.send, self.recv, self.own_sem = send, recv, own_sem
        self.rows = recv_c.shape[1] // place.nz

    @staticmethod
    def scratch(n, nx, nz, q, half):
        copies = 3 + (nx - 1) + 2 * (nz - 1)
        return [
            pltpu.VMEM((n, nx, 2, q, half), BF16),
            pltpu.VMEM((n, nx - 1, 2, q, half), BF16),
            pltpu.VMEM((n, q, half), BF16),
            pltpu.VMEM((n, nz - 1, q // nz, half), BF16),
            pltpu.SemaphoreType.DMA((n, copies)),
            pltpu.SemaphoreType.DMA((n, copies)),
            pltpu.SemaphoreType.DMA((n,)),
        ]

    def copy(self, u, which, src, dst, device):
        return remote(src, dst, self.send.at[u, which], self.recv.at[u, which], device)

    def copies_a(self, u, src):
        return [self.copy(u, 0, src, self.recv_a.at[u], self.place.other_core())]

    def copies_b(self, u):
        p = self.place
        out = []
        for d in range(1, p.nx):
            x, device = p.x_at(d)
            out.append(self.copy(u, 2 + d, self.recv_a.at[u, x], self.recv_b.at[u, d - 1], device))
        return out

    def copies_c(self, u):
        p = self.place
        return [self.copy(u, 1, self.recv_b.at[u, 0, 1 - p.y], self.recv_c.at[u], p.other_y())]

    def copies_d(self, u):
        p, out = self.place, []
        for d in range(1, p.nz):
            z, device = p.z_at(d)
            src = self.recv_c.at[u, pl.ds(pl.multiple_of(z * self.rows, self.rows), self.rows)]
            out.append(self.copy(u, 1 + p.nx + d, src, self.recv_d.at[u, d - 1], device))
        return out

    def piece(self, u):
        p = self.place
        rows = pl.ds(pl.multiple_of(p.z * self.rows, self.rows), self.rows)
        return self.recv_c.at[u, rows], self.fin.at[u, p.y, rows]

    def copies_e(self, u):
        p, out = self.place, []
        for d in range(1, p.nz):
            out.append(self.copy(u, p.nx + p.nz + d, *self.piece(u), p.z_at(d)[1]))
        return out

    def keep(self, u):
        return pltpu.make_async_copy(*self.piece(u), self.own_sem.at[u])

    def copies_f(self, u):
        p = self.place
        return [self.copy(u, 2, self.fin.at[u, p.y], self.fin.at[u, p.y], p.other_y())]

    def start(self, copies):
        for copy in copies:
            copy.start()

    def arrived(self, copies):
        for copy in copies:
            copy.wait_recv()

    def begin(self, u, src):
        self.start(self.copies_a(u, src))

    def collect(self, u, src, own):
        self.arrived(self.copies_a(u, src))
        self.recv_a[u] = added(self.recv_a[u], own[...]).astype(BF16)

    def step_c(self, u):
        p = self.place
        self.arrived(self.copies_b(u))
        parts = [self.recv_a[u, p.x]] + [self.recv_b[u, d] for d in range(p.nx - 1)]
        self.recv_b[u, 0] = added(*parts).astype(BF16)
        self.start(self.copies_c(u))

    def step_d(self, u):
        self.arrived(self.copies_c(u))
        self.recv_c[u] = added(self.recv_b[u, 0, self.place.y], self.recv_c[u]).astype(BF16)
        self.start(self.copies_d(u))

    def step_e(self, u):
        p = self.place
        self.arrived(self.copies_d(u))
        rows = pl.ds(pl.multiple_of(p.z * self.rows, self.rows), self.rows)
        parts = [self.recv_c[u, rows]] + [self.recv_d[u, d] for d in range(p.nz - 1)]
        self.recv_c[u, rows] = added(*parts).astype(BF16)
        self.start(self.copies_e(u))
        self.keep(u).start()

    def step_f(self, u):
        self.arrived(self.copies_e(u))
        self.keep(u).wait()
        self.start(self.copies_f(u))

    def step_g(self, u):
        self.arrived(self.copies_f(u))

    def sent_rest(self, u):
        for copies in (self.copies_b(u), self.copies_c(u), self.copies_d(u), self.copies_e(u), self.copies_f(u)):
            for copy in copies:
                copy.wait_send()


class SmallSum:
    def __init__(self, place, held, landed, send, recv):
        self.place, self.held, self.landed = place, held, landed
        self.send, self.recv = send, recv

    @staticmethod
    def scratch(nx, nz, shape):
        copies = 2 + nx - 1 + nz - 1
        return [
            pltpu.VMEM((5,) + shape, F32),
            pltpu.VMEM((copies,) + shape, F32),
            pltpu.SemaphoreType.DMA((copies,)),
            pltpu.SemaphoreType.DMA((copies,)),
        ]

    def copies(self, stage):
        p = self.place
        first, devices = {
            0: (0, [p.other_core()]),
            1: (2, [p.x_at(d)[1] for d in range(1, p.nx)]),
            2: (1, [p.other_y()]),
            3: (1 + p.nx, [p.z_at(d)[1] for d in range(1, p.nz)]),
        }[stage]
        return [
            remote(self.held.at[stage], self.landed.at[first + i], self.send.at[first + i], self.recv.at[first + i], device)
            for i, device in enumerate(devices)
        ], list(range(first, first + len(devices)))

    def begin(self, value):
        self.held[0] = value
        self.launch()

    def launch(self):
        for copy in self.copies(0)[0]:
            copy.start()

    def step(self, stage, stages=4):
        copies, slots = self.copies(stage)
        for copy in copies:
            copy.wait_recv()
        total = self.held[stage]
        for slot in slots:
            total = total + self.landed[slot]
        self.held[stage + 1] = total
        if stage + 1 < stages:
            for copy in self.copies(stage + 1)[0]:
                copy.start()
        return total

    def sent(self, stages=4):
        for stage in range(stages):
            for copy in self.copies(stage)[0]:
                copy.wait_send()


class Gather:
    def __init__(self, place, whole, own, hidden_rows, send, recv, own_sem):
        self.place, self.whole, self.own = place, whole, own
        self.send, self.recv, self.own_sem = send, recv, own_sem
        self.width = whole.shape[1]
        self.q = self.width // (2 * place.nx)
        self.square = len(own) - hidden_rows // self.q
        self.hidden_rows = hidden_rows

    @staticmethod
    def scratch(units, nx):
        copies = 1 + 4 * (nx - 1)
        return [
            pltpu.SemaphoreType.DMA((units, copies)),
            pltpu.SemaphoreType.DMA((units, copies)),
            pltpu.SemaphoreType.DMA((units,)),
        ]

    def rows(self, u, shard, half=None):
        if isinstance(u, int) and u >= self.square:
            at = self.square * self.width + shard * self.hidden_rows + (u - self.square) * self.q
        else:
            at = u * self.width + shard * self.q
        if half is None:
            return pl.ds(pl.multiple_of(at, 16), self.q)
        return pl.ds(pl.multiple_of(at + half * (self.q // 2), 16), self.q // 2)

    def part(self, u, shard, half=None):
        return self.whole.at[self.rows(u, shard, half)]

    def copy(self, u, which, src, dst, device):
        return remote(src, dst, self.send.at[u, which], self.recv.at[u, which], device)

    def to_core(self, u):
        shard = self.place.shard
        return self.copy(u, 0, self.own[u], self.part(u, shard), self.place.other_core())

    def keep(self, u):
        return pltpu.make_async_copy(
            self.own[u], self.part(u, self.place.shard), self.own_sem.at[u]
        )

    def over_x(self, u, d):
        p = self.place
        half = self.own[u].at[pl.ds(pl.multiple_of(p.y * (self.q // 2), 16), self.q // 2)]
        return self.copy(u, 4 * d - 3, half, self.part(u, p.shard, p.y), p.x_at(d)[1])

    def came(self, d):
        p = self.place
        return lax.rem(p.x + p.nx - d, p.nx) * 2 + p.core

    def on_y(self, u, d):
        p = self.place
        here = self.part(u, self.came(d), p.y)
        return self.copy(u, 4 * d - 2, here, here, p.other_y())

    def on_core(self, u, d):
        p = self.place
        here = self.part(u, self.came(d), p.y)
        return self.copy(u, 4 * d - 1, here, here, p.other_core())

    def last_core(self, u, d):
        p = self.place
        here = self.part(u, self.came(d), 1 - p.y)
        return self.copy(u, 4 * d, here, here, p.other_core())

    def issue(self, u):
        for d in range(1, self.place.nx):
            self.over_x(u, d).start()
        self.to_core(u).start()
        self.keep(u).start()

    def relay_x(self, u):
        for d in range(1, self.place.nx):
            self.arrive_x(u, d)
            self.on_y(u, d).start()
            self.on_core(u, d).start()

    def arrive_x(self, u, d):
        p = self.place
        here = self.part(u, self.came(d), p.y)
        self.copy(u, 4 * d - 3, here, here, p.x_at(d)[1]).wait_recv()

    def relay_y(self, u):
        for d in range(1, self.place.nx):
            self.on_y(u, d).wait_recv()
            self.last_core(u, d).start()

    def ready(self, u):
        p = self.place
        here = self.part(u, p.shard)
        pltpu.make_async_copy(here, here, self.own_sem.at[u]).wait()
        self.copy(u, 0, here, here, p.other_core()).wait_recv()
        for d in range(1, p.nx):
            self.on_core(u, d).wait_recv()
            self.last_core(u, d).wait_recv()

    def sent(self, u):
        p = self.place
        here = self.part(u, p.shard)
        self.copy(u, 0, here, here, p.other_core()).wait_send()
        for d in range(1, p.nx):
            here = self.part(u, self.came(d), p.y)
            self.copy(u, 4 * d - 3, here, here, p.x_at(d)[1]).wait_send()
            self.on_y(u, d).wait_send()
            self.on_core(u, d).wait_send()
            self.last_core(u, d).wait_send()


class Spread:
    def __init__(self, place, own, whole, send, recv, own_sem):
        self.place, self.own, self.whole = place, own, whole
        self.send, self.recv, self.own_sem = send, recv, own_sem
        self.count = own.shape[0]

    @staticmethod
    def scratch(nx):
        copies = 1 + 2 * (nx - 1)
        return [
            pltpu.SemaphoreType.DMA((copies,)),
            pltpu.SemaphoreType.DMA((copies,)),
            pltpu.SemaphoreType.DMA(()),
        ]

    def part(self, shard):
        return self.whole.at[pl.ds(pl.multiple_of(shard * self.count, 16), self.count)]

    def copy(self, which, src, dst, device):
        return remote(src, dst, self.send.at[which], self.recv.at[which], device)

    def to_core(self):
        return self.copy(0, self.own, self.part(self.place.shard), self.place.other_core())

    def over_x(self, d):
        p = self.place
        return self.copy(2 * d - 1, self.own, self.part(p.shard), p.x_at(d)[1])

    def on_core(self, d):
        p = self.place
        here = self.part(lax.rem(p.x + p.nx - d, p.nx) * 2 + p.core)
        return self.copy(2 * d, here, here, p.other_core())

    def keep(self):
        return pltpu.make_async_copy(self.own, self.part(self.place.shard), self.own_sem)

    def issue(self):
        for d in range(1, self.place.nx):
            self.over_x(d).start()
        self.to_core().start()
        self.keep().start()

    def relay_x(self):
        for d in range(1, self.place.nx):
            self.over_x(d).wait_recv()
            self.on_core(d).start()

    def ready(self):
        self.keep().wait()
        self.to_core().wait_recv()
        for d in range(1, self.place.nx):
            self.on_core(d).wait_recv()

    def sent(self):
        self.to_core().wait_send()
        for d in range(1, self.place.nx):
            self.over_x(d).wait_send()
            self.on_core(d).wait_send()


def attend_pair(query, keys, values_ref, p_ref, bias=None):
    rows, length = query.shape[0], keys.shape[0]
    blocks = rows // 128
    scores = dot_nt(stack_heads(query), keys)
    for head in range(2):
        if bias is not None:
            row_ids, key_ids, window = bias
            table = skew(window[head : head + 1], window.shape[1])
        for b in range(blocks):
            at = head * rows + b * 128
            part = scores[at : at + 128]
            if bias is not None:
                shift = (blocks - 1 - b) * 128
                allowed = key_ids <= row_ids[b * 128 : b * 128 + 128]
                part = jnp.where(allowed, part + table[:, shift : shift + length], MASKED)
            top = jnp.max(part, axis=-1, keepdims=True)
            raised = jnp.exp(part - top)
            share = 1.0 / jnp.sum(raised, axis=-1, keepdims=True)
            p_ref[at : at + 128, :] = (raised * share).astype(BF16)
    return merge_heads(dot(p_ref[...], values_ref[...]))


def forward_kernel(reps, shards, names, *refs):
    r = types.SimpleNamespace(**dict(zip(names, refs)))
    place = Place(reps, shards)
    rows, width = r.tok_in.shape
    length = r.tok.shape[0]
    pairs = width // LANES
    q = width // shards
    part = r.feed_in.shape[1] // width
    own = [r.self_query, r.self_keyval.at[0], r.self_keyval.at[1], r.self_output]
    own += [r.cross_query, r.cross_keyval.at[0], r.cross_keyval.at[1], r.cross_output]
    own += [r.feed_in.at[:, pl.ds(j * width, width)] for j in range(part)]
    own += [r.feed_out.at[pl.ds(j * q, q)] for j in range(part)]
    units = len(own)
    small = SmallSum(place, r.small_held, r.small_landed, r.small_send, r.small_recv)
    gather = Gather(place, r.whole, own, r.feed_out.shape[0], r.w_send, r.w_recv, r.w_own)
    tokens = Spread(place, r.tok_in, r.tok, r.t_send, r.t_recv, r.t_own)
    memories = Spread(place, r.enc_in, r.enc, r.e_send, r.e_recv, r.e_own)

    def weight(u):
        return r.whole[pl.ds(pl.multiple_of(u * width, width), width), :]

    def emit_weights(u, count):
        block = pl.ds(u * width, count * width)
        return pltpu.make_async_copy(r.whole.at[block], r.w_out.at[block], r.out_sem.at[u])

    def emit_kv(i):
        return pltpu.make_async_copy(r.kv.at[i], r.kv_out.at[i], r.out_sem.at[units + i])

    emit_tok = pltpu.make_async_copy(r.tok_t, r.tok_out, r.out_sem.at[units + 4])
    emit_enc = pltpu.make_async_copy(r.enc_t, r.enc_out, r.out_sem.at[units + 5])

    def emit_p(which, i):
        slot = lax.rem(i, 2)
        return pltpu.make_async_copy(r.probs.at[slot], r.p_out.at[which, i], r.p_sem.at[slot])

    def gain(i):
        return r.small_held[2, i : i + 1, :width]

    enter(place)
    small.begin(r.small_in[...])
    line = [(gather, (u,)) for u in (1, 2, 0)] + [(tokens, ()), (memories, ())]
    line += [(gather, (u,)) for u in [3, 5, 6, 4, 7] + list(range(8, units))]

    def issue(at):
        if at < len(line):
            line[at][0].issue(*line[at][1])

    def relay(owner, *u):
        owner.relay_x(*u)
        issue(line.index((owner, u)) + AHEAD)

    for at in range(AHEAD):
        issue(at)
    small.step(0, 2)
    gathered = small.step(1, 2)
    r.small_out[...] = gathered
    table = gathered[8:24, :LANES].astype(BF16)
    biases = dot(table, r.onehot[...])
    for i in range(pairs):
        r.window[i] = biases[2 * i : 2 * i + 2]
    for u in (1, 2, 0):
        relay(gather, u)
    for u in (1, 2, 0):
        gather.relay_y(u)
    relay(tokens)
    tokens.ready()
    tokens.sent()

    def norm_rows(i, carry):
        at = pl.ds(pl.multiple_of(i * rows, 16), rows)
        values = r.tok[at, :].astype(F32)
        normed = (values * rms_scale(values) * gain(0)).astype(BF16)
        r.tok[at, :] = normed
        r.tok_t[:, pl.ds(pl.multiple_of(i * rows, LANES), rows)] = normed.T
        return carry

    lax.fori_loop(0, length // rows, norm_rows, 0)
    emit_tok.start()

    def project_pair(source, target, base):
        def step(i, carry):
            at = pl.ds(pl.multiple_of(i * rows, 16), rows)
            block = source[at, :]
            for which in range(2):
                out = dot(block, weight(base + which)).astype(BF16)
                for j in range(pairs):
                    r.kv[target + which, j, at, :] = out[:, j * LANES : (j + 1) * LANES]
            return carry

        lax.fori_loop(0, source.shape[0] // rows, step, 0)
        emit_kv(target).start()
        emit_kv(target + 1).start()

    def project_query(normed, u, which):
        out = dot(normed, weight(u)).astype(BF16)
        for j in range(pairs):
            r.q_out[which, j] = out[:, j * LANES : (j + 1) * LANES]

    def attention(which, bias, relays):
        def pair(i, carry):
            @pl.when(i >= 2)
            def _():
                emit_p(which, i).wait()

            slot = lax.rem(i, 2)
            more = None
            if bias:
                more = (r.row_ids[...], r.small_held[2, 3:4, :length], r.window[i])
            r.low_out[which, i] = attend_pair(
                r.q_out[which, i],
                r.kv[2 * which, i],
                r.kv.at[2 * which + 1, i],
                r.probs.at[slot],
                more,
            )
            emit_p(which, i).start()
            for step, relay, u in relays:
                @pl.when(i == step)
                def _():
                    relay(*u)

            return carry

        lax.fori_loop(0, pairs, pair, 0)
        emit_p(which, 0).wait()
        emit_p(which, 1).wait()
        low = [r.low_out[which, j].astype(BF16) for j in range(pairs)]
        low = jnp.concatenate(low, axis=1)
        r.low_t[which] = low.T
        return low

    gather.ready(1)
    gather.ready(2)
    project_pair(r.tok, 0, 1)
    gather.ready(0)
    emit_weights(0, 3).start()
    mine = pl.ds(pl.multiple_of(place.shard * rows, 16), rows)
    project_query(r.tok[mine, :], 0, 0)
    over_y = gather.relay_y

    def over_x(u):
        relay(gather, u)

    low = attention(
        0,
        True,
        [
            (0, relay, (memories,)),
            (1, over_x, (3,)),
            (2, over_x, (5,)),
            (3, over_x, (6,)),
            (3, over_y, (3,)),
            (4, over_x, (4,)),
            (4, over_y, (5,)),
            (5, over_y, (6,)),
        ],
    )
    gather.ready(3)
    r.first_out[...] = r.tok_in[...].astype(F32) + dot(low, weight(3))
    over_x(7)
    over_y(4)
    memories.ready()

    def turn_rows(i, carry):
        at = pl.ds(pl.multiple_of(i * rows, LANES), rows)
        r.enc_t[:, at] = r.enc[at, :].T
        return carry

    lax.fori_loop(0, length // rows, turn_rows, 0)
    emit_enc.start()
    gather.ready(5)
    gather.ready(6)
    project_pair(r.enc, 2, 5)
    gather.ready(4)
    first = r.first_out[...]
    normed = (first * rms_scale(first) * gain(1)).astype(BF16)
    r.normed2_t[...] = normed.T
    project_query(normed, 4, 1)
    over_x(8)
    over_y(7)
    low = attention(
        1,
        False,
        [
            (1, over_x, (9,)),
            (1, over_y, (8,)),
            (2, over_x, (10,)),
            (3, over_y, (9,)),
            (4, over_x, (11,)),
            (5, over_y, (10,)),
        ],
    )
    gather.ready(7)
    emit_weights(3, 5).start()
    r.second_out[...] = r.first_out[...] + dot(low, weight(7))
    over_x(12)
    over_y(11)
    second = r.second_out[...]
    normed = (second * rms_scale(second) * gain(2)).astype(BF16)
    r.normed[...] = normed
    r.normed3_t[...] = normed.T
    for j in range(part):
        gather.ready(8 + j)
        value, slope = gelu_parts(dot(r.normed[...], weight(8 + j)))
        value = value.astype(BF16)
        r.hidden[j] = value
        r.hidden_t[j * width : (j + 1) * width, :] = value.T
        r.slope_out[j] = slope
        if j + 1 < part:
            over_x(13 + j)
            over_y(12 + j)
    over_y(units - 1)
    for j in range(part):
        gather.ready(8 + part + j)
    emit_weights(8, units - 8).start()
    total = second
    for j in range(part):
        total = total + dot(r.hidden[j], weight(8 + part + j))
    r.result[...] = total.astype(BF16)
    for u in range(units):
        gather.sent(u)
    memories.sent()
    small.sent(2)
    for u, count in ((0, 3), (3, 5), (8, units - 8)):
        emit_weights(u, count).wait()
    for i in range(4):
        emit_kv(i).wait()
    emit_tok.wait()
    emit_enc.wait()


def forward(tokens, encoded, row_ids, small, onehot, shards_of, reps, shards):
    rows, width = tokens.shape
    length, memory = rows * shards, encoded.shape[0] * shards
    nx = shards // 2
    feed_in, feed_out = shards_of[-2:]
    hidden = feed_in.shape[1]
    units = 8 + 2 * (hidden // width)
    pairs = width // LANES
    kept = lambda *shape, dtype=BF16: (pl.BlockSpec(memory_space=pl.ANY), jax.ShapeDtypeStruct(shape, dtype))
    near = lambda *shape, dtype=F32: (pl.BlockSpec(memory_space=pltpu.VMEM), jax.ShapeDtypeStruct(shape, dtype))
    outs = dict(
        result=near(rows, width, dtype=BF16),
        first_out=near(rows, width),
        second_out=near(rows, width),
        low_out=near(2, pairs, rows, LANES),
        q_out=near(2, pairs, rows, LANES, dtype=BF16),
        small_out=near(*small.shape),
        low_t=near(2, width, rows, dtype=BF16),
        normed2_t=near(width, rows, dtype=BF16),
        normed3_t=near(width, rows, dtype=BF16),
        hidden_t=near(hidden, rows, dtype=BF16),
        slope_out=near(hidden // width, rows, width),
        w_out=kept(units * width, width),
        kv_out=kept(4, pairs, length, LANES),
        tok_out=kept(width, length),
        enc_out=kept(width, memory),
        p_out=kept(2, pairs, 2 * rows, length),
    )
    scratch = dict(
        whole=pltpu.VMEM((units * width, width), BF16),
        tok=pltpu.VMEM((length, width), BF16),
        enc=pltpu.VMEM((memory, width), BF16),
        kv=pltpu.VMEM((4, pairs, length, LANES), BF16),
        window=pltpu.VMEM((pairs, 2, onehot.shape[1]), F32),
        probs=pltpu.VMEM((2, 2 * rows, length), BF16),
        normed=pltpu.VMEM((rows, width), BF16),
        hidden=pltpu.VMEM((hidden // width, rows, width), BF16),
        tok_t=pltpu.VMEM((width, length), BF16),
        enc_t=pltpu.VMEM((width, memory), BF16),
        p_sem=pltpu.SemaphoreType.DMA((2,)),
        out_sem=pltpu.SemaphoreType.DMA((units + 6,)),
    )
    scratch.update(zip(("small_held", "small_landed", "small_send", "small_recv"), SmallSum.scratch(nx, reps // 2, small.shape)))
    scratch.update(zip(("w_send", "w_recv", "w_own"), Gather.scratch(units, nx)))
    scratch.update(zip(("t_send", "t_recv", "t_own"), Spread.scratch(nx)))
    scratch.update(zip(("e_send", "e_recv", "e_own"), Spread.scratch(nx)))
    shard_names = ["self_query", "self_keyval", "self_output", "cross_query", "cross_keyval", "cross_output", "feed_in", "feed_out"]
    names = ["tok_in", "enc_in", "row_ids", "small_in", "onehot"] + shard_names + list(outs) + list(scratch)
    made = pl.pallas_call(
        functools.partial(forward_kernel, reps, shards, tuple(names)),
        in_specs=[pl.BlockSpec(memory_space=pltpu.VMEM)] * 5 + [pl.BlockSpec(memory_space=pl.ANY)] * 8,
        out_specs=[spec for spec, _ in outs.values()],
        out_shape=[shape for _, shape in outs.values()],
        scratch_shapes=list(scratch.values()),
        compiler_params=pltpu.CompilerParams(
            collective_id=2, has_side_effects=True, vmem_limit_bytes=FUSED_LIMIT
        ),
    )(tokens, encoded, row_ids, small, onehot, *shards_of)
    return types.SimpleNamespace(**dict(zip(outs, made)))


class RowSum:
    def __init__(self, place, parts, recv_a, recv_b, send, recv):
        self.place, self.parts, self.recv_a, self.recv_b = place, parts, recv_a, recv_b
        self.send, self.recv = send, recv

    @staticmethod
    def scratch(nx, width, rows):
        return [
            pltpu.VMEM((2, nx, width, rows), BF16),
            pltpu.VMEM((nx, width, rows), BF16),
            pltpu.VMEM((nx - 1, width, rows), BF16),
            pltpu.SemaphoreType.DMA((nx,)),
            pltpu.SemaphoreType.DMA((nx,)),
        ]

    def copy(self, which, src, dst, device):
        return remote(src, dst, self.send.at[which], self.recv.at[which], device)

    def to_core(self):
        p = self.place
        return self.copy(0, self.parts.at[1 - p.core], self.recv_a, p.other_core())

    def over_x(self, d):
        x, device = self.place.x_at(d)
        return self.copy(d, self.recv_a.at[x], self.recv_b.at[d - 1], device)

    def begin(self, total):
        rows = self.parts.shape[3]
        for s in range(2 * self.place.nx):
            self.parts[s % 2, s // 2] = total[:, s * rows : (s + 1) * rows].astype(BF16)
        self.to_core().start()

    def pass_x(self):
        self.to_core().wait_recv()
        self.recv_a[...] = added(self.recv_a[...], self.parts[self.place.core]).astype(BF16)
        for d in range(1, self.place.nx):
            self.over_x(d).start()

    def finish(self):
        p = self.place
        for d in range(1, p.nx):
            self.over_x(d).wait_recv()
        return added(self.recv_a[p.x], *[self.recv_b[d] for d in range(p.nx - 1)])

    def sent(self):
        for d in range(1, self.place.nx):
            self.over_x(d).wait_send()


def attend_back_pair(query, keys, values, p_ref, output, grad, ds_ref, width=None):
    rows, length = query.shape[0], keys.shape[0]
    blocks = rows // 128
    grads, queries = stack_heads(grad), stack_heads(query)
    delta_wide = grad.astype(F32) * output
    d_weights = dot_nt(grads, values)
    windows = []
    for head in range(2):
        delta = jnp.sum(delta_wide * own_lanes(head == 0), axis=-1, keepdims=True)
        total = None
        for b in range(blocks):
            at = head * rows + b * 128
            part = p_ref[at : at + 128, :].astype(F32) * (
                d_weights[at : at + 128] - delta[b * 128 : b * 128 + 128]
            )
            ds_ref[at : at + 128, :] = part.astype(BF16)
            if width is not None:
                shift = (blocks - 1 - b) * 128
                pieces = [jnp.zeros((128, shift), F32)] if shift else []
                pieces.append(part)
                if width - shift - length:
                    pieces.append(jnp.zeros((128, width - shift - length), F32))
                placed = jnp.concatenate(pieces, axis=1)
                total = placed if total is None else total + placed
        if width is not None:
            windows.append(unskew(total, width))
    d_query = merge_heads(dot(ds_ref[...], keys)).astype(BF16)
    d_keys = dot(queries.T, ds_ref[...]).astype(BF16)
    d_values = dot(grads.T, p_ref[...]).astype(BF16)
    return d_query, d_keys, d_values, windows


def backward_kernel(reps, shards, names, *refs):
    r = types.SimpleNamespace(**dict(zip(names, refs)))
    place = Place(reps, shards)
    rows, width = r.cotangent.shape
    length = r.enc_t.shape[1]
    pairs = width // LANES
    q = width // shards
    part = r.hidden_t.shape[0] // width
    units = 8 + 2 * part
    red = Reduction(place, r.recv_a, r.recv_b, r.recv_c, r.recv_d, r.fin, r.r_send, r.r_recv, r.r_own)
    small = SmallSum(place, r.small_held, r.small_landed, r.small_send, r.small_recv)
    sum_memory = RowSum(place, r.m_parts, r.m_a, r.m_b, r.m_send, r.m_recv)
    sum_tokens = RowSum(place, r.m_parts, r.t_a, r.t_b, r.t_send, r.t_recv)

    def gain(i):
        return r.gains[i : i + 1, :width]

    def load_weight(u, slot):
        block = pl.ds(u * width, width)
        return pltpu.make_async_copy(r.w_in.at[block], r.w.at[slot], r.w_sem.at[slot])

    def load_slope(j):
        slot = lax.rem(j, 2)
        return pltpu.make_async_copy(r.slope.at[j], r.slopes.at[slot], r.s_sem.at[slot])

    def load_kv(i, slot):
        return pltpu.make_async_copy(r.kv_in.at[i], r.kv.at[slot], r.kv_sem.at[slot])

    def load_p(which, i):
        slot = lax.rem(i, 2)
        return pltpu.make_async_copy(r.p_in.at[which, i], r.probs.at[slot], r.p_sem.at[slot])

    def load_t(source, which):
        return pltpu.make_async_copy(source, r.rows_t, r.t_sem.at[which])

    def away(n):
        return r.made.at[lax.rem(n, SLOTS), 1 - place.core]

    def fill(n, value):
        slot = lax.rem(n, SLOTS)
        rest = value.shape[0] // shards
        half = width // 2
        for s in range(shards):
            for h in range(2):
                r.made[slot, s % 2, s // 2, h] = value[
                    s * rest : (s + 1) * rest, h * half : (h + 1) * half
                ].astype(BF16)
        red.begin(n, away(n))

    def free(n):
        red.copies_a(n - SLOTS, away(n))[0].wait_send()

    def take(n):
        red.collect(n, away(n), r.made.at[lax.rem(n, SLOTS), place.core])

    def advance(n):
        if n < units:
            red.step_c(n)
            if n + AHEAD < units:
                red.start(red.copies_b(n + AHEAD))
        for late, step in ((1, red.step_d), (2, red.step_e), (3, red.step_f), (4, red.step_g)):
            if 0 <= n - late < units:
                step(n - late)

    enter(place)
    load_slope(0).start()
    for slot, u in enumerate((8, 8 + part)):
        load_weight(u, slot).start()
    for slot in range(2):
        load_kv(2 + slot, slot).start()
        load_p(1, slot).start()
    load_t(r.enc_t, 0).start()
    r.acc[...] = jnp.zeros((rows, width), F32)

    def feed(j, carry):
        slot = 2 * lax.rem(j, 2)
        load_weight(8, slot).wait()
        load_weight(8 + part, slot + 1).wait()
        load_slope(j).wait()

        @pl.when(j + 1 < part)
        def _():
            load_slope(j + 1).start()
            load_weight(8 + j + 1, 2 - slot).start()
            load_weight(8 + part + j + 1, 3 - slot).start()

        grad_hidden = dot_nt(r.cotangent[...], r.w[slot + 1])
        grad = (grad_hidden * r.slopes[lax.rem(j, 2)]).astype(BF16)
        fill(j, dot(r.normed3_t[...], grad))
        r.acc[...] += dot_nt(grad, r.w[slot])

        @pl.when(j >= 1)
        def _():
            take(j - 1)

        return carry

    lax.fori_loop(0, part, feed, 0)
    for slot, u in ((0, 7), (1, 5), (2, 6), (3, 4)):
        load_weight(u, slot).start()
    take(part - 1)
    for n in range(AHEAD):
        red.start(red.copies_b(n))

    def feed_out(m, carry):
        n = part + m
        free(n)
        value = jnp.concatenate(
            [
                dot(
                    r.hidden_t[pl.ds(pl.multiple_of(s * width + m * q, 16), q), :],
                    r.cotangent[...],
                )
                for s in range(shards)
            ],
            axis=0,
        )
        fill(n, value)

        @pl.when(m >= 1)
        def _():
            take(n - 1)

        return carry

    lax.fori_loop(0, part, feed_out, 0)
    back, d_gain3 = rms_back(r.second[...], gain(2), r.acc[...])
    r.grad[...] = r.cotangent[...].astype(F32) + back
    take(2 * part - 1)

    def attention(which, fold, steps):
        def pair(i, carry):
            slot = lax.rem(i, 2)
            load_p(which, i).wait()
            d_query, d_keys, d_values, windows = attend_back_pair(
                r.queries[which, i],
                r.kv[0, i],
                r.kv[1, i],
                r.probs.at[slot],
                r.low[which, i],
                r.grad_att[i],
                r.ds,
                r.onehot.shape[1] if fold else None,
            )
            r.d_query[i] = d_query
            at = pl.ds(pl.multiple_of(i * LANES, LANES), LANES)
            r.dk_t[at, :] = d_keys
            r.dv_t[at, :] = d_values
            if fold:
                r.d_window[i] = jnp.concatenate(windows, axis=0)

            @pl.when(i + 2 < pairs)
            def _():
                load_p(which, i + 2).start()

            for step, n in steps:
                @pl.when(i == step)
                def _():
                    advance(n)

            return carry

        lax.fori_loop(0, pairs, pair, 0)

    def spread_grad(value):
        for i in range(pairs):
            r.grad_att[i] = value[:, i * LANES : (i + 1) * LANES].astype(BF16)

    def joined_query():
        return jnp.concatenate([r.d_query[i] for i in range(pairs)], axis=1)

    n = 2 * part
    grad_low = r.grad[...].astype(BF16)
    free(n)
    fill(n, dot(r.low_t[1], grad_low))
    load_weight(7, 0).wait()
    spread_grad(dot_nt(grad_low, r.w[0]))
    load_weight(3, 0).start()
    take(n)
    for slot in range(2):
        load_kv(2 + slot, slot).wait()
    attention(1, False, [(0, 0), (4, 1)])
    for slot in range(2):
        load_kv(slot, slot).start()
        load_p(0, slot).start()
    load_weight(5, 1).wait()
    load_weight(6, 2).wait()
    sum_memory.begin(dot(r.w[1], r.dk_t[...]) + dot(r.w[2], r.dv_t[...]))
    load_weight(1, 1).start()
    load_weight(2, 2).start()
    load_t(r.enc_t, 0).wait()
    free(n + 1)
    fill(n + 1, dot_nt(r.rows_t[...], r.dk_t[...]))
    sum_memory.pass_x()
    free(n + 2)
    fill(n + 2, dot_nt(r.rows_t[...], r.dv_t[...]))
    take(n + 1)
    load_t(r.tok_t, 1).start()
    d_query = joined_query()
    load_weight(4, 3).wait()
    back, d_gain2 = rms_back(r.first[...], gain(1), dot_nt(d_query, r.w[3]))
    load_weight(0, 3).start()
    free(n + 3)
    fill(n + 3, dot(r.normed2_t[...], d_query))
    take(n + 2)
    r.grad[...] = r.grad[...] + back
    advance(2)

    grad_low = r.grad[...].astype(BF16)
    take(n + 3)
    free(n + 4)
    fill(n + 4, dot(r.low_t[0], grad_low))
    load_weight(3, 0).wait()
    spread_grad(dot_nt(grad_low, r.w[0]))
    take(n + 4)
    for slot in range(2):
        load_kv(slot, slot).wait()
    attention(0, True, [(1, 3), (4, 4)])
    load_weight(1, 1).wait()
    load_weight(2, 2).wait()
    sum_memory.to_core().wait_send()
    sum_tokens.begin(dot(r.w[1], r.dk_t[...]) + dot(r.w[2], r.dv_t[...]))
    load_t(r.tok_t, 1).wait()
    free(n + 5)
    fill(n + 5, dot_nt(r.rows_t[...], r.dk_t[...]))
    sum_tokens.pass_x()
    free(n + 6)
    fill(n + 6, dot_nt(r.rows_t[...], r.dv_t[...]))
    take(n + 5)
    r.d_memory[...] = sum_memory.finish().T
    advance(5)
    d_query = joined_query()
    free(n + 7)
    mine = pl.ds(pl.multiple_of(place.shard * rows, LANES), rows)
    fill(n + 7, dot(r.rows_t[:, mine], d_query))
    take(n + 6)
    load_weight(0, 3).wait()
    r.acc[...] = dot_nt(d_query, r.w[3])
    windows = jnp.concatenate([r.d_window[i] for i in range(pairs)], axis=0)
    d_table = lax.dot_general(
        windows,
        r.onehot[...].astype(F32),
        (((1,), (1,)), ((), ())),
        precision=lax.Precision.HIGHEST,
        preferred_element_type=F32,
    )
    take(n + 7)
    advance(6)
    values = r.tokens[...].astype(F32)
    back, d_gain1 = rms_back(values, gain(0), r.acc[...] + sum_tokens.finish().T)
    r.d_tokens[...] = r.grad[...] + back
    r.small_held[0] = jnp.zeros(r.small_held.shape[1:], F32)
    for i, d_gain in enumerate((d_gain1, d_gain2, d_gain3)):
        r.small_held[0, i : i + 1, :width] = d_gain
    r.small_held[0, 8 : 8 + 2 * pairs, :LANES] = d_table
    small.launch()
    for n in range(7, units + 4):
        advance(n)
        if n < 11:
            small.step(n - 7)
    r.small_out[...] = r.small_held[4]
    for n in range(units):
        if n >= units - SLOTS:
            red.copies_a(n, away(n))[0].wait_send()
        red.sent_rest(n)
    small.sent()
    sum_tokens.to_core().wait_send()
    sum_memory.sent()
    sum_tokens.sent()


def backward(tokens, cotangent, onehot, held, reps, shards):
    rows, width = tokens.shape
    length = held.enc_out.shape[1]
    nx, nz = shards // 2, reps // 2
    pairs = width // LANES
    q, half = width // shards, width // 2
    units = held.w_out.shape[0] // width
    small = (24, width)
    kept = pl.BlockSpec(memory_space=pl.ANY)
    near = pl.BlockSpec(memory_space=pltpu.VMEM)
    ins = dict(
        tokens=(near, tokens),
        cotangent=(near, cotangent),
        onehot=(near, onehot),
        gains=(near, held.small_out),
        first=(near, held.first_out),
        second=(near, held.second_out),
        low=(near, held.low_out),
        low_t=(near, held.low_t),
        queries=(near, held.q_out),
        normed2_t=(near, held.normed2_t),
        normed3_t=(near, held.normed3_t),
        hidden_t=(near, held.hidden_t),
        slope=(kept, held.slope_out),
        tok_t=(kept, held.tok_out),
        enc_t=(kept, held.enc_out),
        w_in=(kept, held.w_out),
        kv_in=(kept, held.kv_out),
        p_in=(kept, held.p_out),
    )
    outs = dict(
        d_tokens=(near, jax.ShapeDtypeStruct((rows, width), F32)),
        d_memory=(near, jax.ShapeDtypeStruct((rows, width), F32)),
        small_out=(near, jax.ShapeDtypeStruct(small, F32)),
        fin=(kept, jax.ShapeDtypeStruct((units, 2, q, half), BF16)),
    )
    scratch = dict(
        w=pltpu.VMEM((4, width, width), BF16),
        kv=pltpu.VMEM((2, pairs, length, LANES), BF16),
        probs=pltpu.VMEM((2, 2 * rows, length), BF16),
        ds=pltpu.VMEM((2 * rows, length), BF16),
        rows_t=pltpu.VMEM((width, length), BF16),
        dk_t=pltpu.VMEM((width, length), BF16),
        dv_t=pltpu.VMEM((width, length), BF16),
        d_query=pltpu.VMEM((pairs, rows, LANES), BF16),
        grad_att=pltpu.VMEM((pairs, rows, LANES), BF16),
        d_window=pltpu.VMEM((pairs, 2, onehot.shape[1]), F32),
        acc=pltpu.VMEM((rows, width), F32),
        grad=pltpu.VMEM((rows, width), F32),
        made=pltpu.VMEM((SLOTS, 2, nx, 2, q, half), BF16),
        slopes=pltpu.VMEM((2, rows, width), F32),
        s_sem=pltpu.SemaphoreType.DMA((2,)),
        w_sem=pltpu.SemaphoreType.DMA((4,)),
        kv_sem=pltpu.SemaphoreType.DMA((2,)),
        p_sem=pltpu.SemaphoreType.DMA((2,)),
        t_sem=pltpu.SemaphoreType.DMA((2,)),
    )
    scratch.update(
        zip(
            ("recv_a", "recv_b", "recv_c", "recv_d", "r_send", "r_recv", "r_own"),
            Reduction.scratch(units, nx, nz, q, half),
        )
    )
    scratch.update(
        zip(("small_held", "small_landed", "small_send", "small_recv"), SmallSum.scratch(nx, nz, small))
    )
    for name in "mt":
        keys = (name + end for end in ("_parts", "_a", "_b", "_send", "_recv"))
        scratch.update(zip(keys, RowSum.scratch(nx, width, rows)))
    del scratch["t_parts"]
    names = tuple(list(ins) + list(outs) + list(scratch))
    made = pl.pallas_call(
        functools.partial(backward_kernel, reps, shards, names),
        in_specs=[spec for spec, _ in ins.values()],
        out_specs=[spec for spec, _ in outs.values()],
        out_shape=[shape for _, shape in outs.values()],
        scratch_shapes=list(scratch.values()),
        compiler_params=pltpu.CompilerParams(
            collective_id=3, has_side_effects=True, vmem_limit_bytes=FUSED_LIMIT
        ),
    )(*[value for _, value in ins.values()])
    return types.SimpleNamespace(**dict(zip(outs, made)))


def tiles_evenly(reps, shards, width):
    if reps % 2 or shards % 2 or width % shards:
        return False
    return (width // shards) % (8 * reps) == 0 and width % (4 * HD) == 0


def layer(
    tokens,
    encoded,
    block_ids,
    buckets,
    cotangent,
    norm_self,
    self_query,
    self_keyval,
    self_output,
    bucket_bias,
    norm_cross,
    cross_query,
    cross_keyval,
    cross_output,
    norm_feed,
    feed_in,
    feed_out,
):
    groups, positions, model_width = tokens.shape
    reps, shards = lax.axis_size("rep"), lax.axis_size("shard")
    length = (buckets.shape[0] + 1) // 2
    memory_local = encoded.shape[1]
    row_anchor = lax.axis_index("shard") * positions
    heads, bucket_count = bucket_bias.shape[0], bucket_bias.shape[1] * shards
    window_width = length + positions
    window_buckets = lax.dynamic_slice_in_dim(
        jnp.pad(buckets, (1, 0)), length - row_anchor - positions, window_width
    )
    fused = tiles_evenly(reps, shards, model_width) and encoded.shape == tokens.shape
    fused = fused and feed_out.shape[0] == model_width and positions % LANES == 0
    if fused:
        onehot = window_buckets[None, :] == jnp.arange(LANES, dtype=jnp.int32)[:, None]
        small = jnp.zeros((24, max(length, model_width)), F32)
        shard = lax.axis_index("shard")
        place = lambda a, block, row: lax.dynamic_update_slice(
            a, block.astype(F32), (row, shard * block.shape[1])
        )
        small = place(small, jnp.stack([norm_self, norm_cross, norm_feed]), 0)
        small = place(small, block_ids, 3)
        small = place(small, bucket_bias, 8)
        held = forward(
            tokens[0],
            encoded[0],
            block_ids[0].astype(F32)[:, None],
            small,
            onehot.astype(BF16),
            (self_query, self_keyval, self_output, cross_query, cross_keyval, cross_output, feed_in, feed_out),
            reps,
            shards,
        )
        made = backward(tokens[0], cotangent[0], onehot.astype(BF16), held, reps, shards)
        sums = made.fin.transpose(0, 2, 1, 3).reshape(-1, model_width // shards, model_width)
        sums = sums.astype(F32)
        parts = feed_in.shape[1] // model_width
        inner = jnp.concatenate([sums[j] for j in range(parts)], axis=1)
        outer = sums[parts : 2 * parts].reshape(-1, model_width)
        co, ck, cv, cq, so, sk, sv, sq = (sums[2 * parts + i] for i in range(8))
        mine = lambda a, size: lax.dynamic_slice_in_dim(a, shard * size, size, a.ndim - 1)
        gains = mine(made.small_out[:3, :model_width], model_width // shards)
        table = mine(made.small_out[8 : 8 + heads, :bucket_count], bucket_count // shards)
        totals = (gains[0], sq, jnp.stack([sk, sv]), so, table)
        totals += (gains[1], cq, jnp.stack([ck, cv]), co, gains[2], inner, outer)
        return (held.result[None], made.d_tokens[None], made.d_memory[None]) + totals

    inputs = tokens[0].astype(F32)
    encoded_whole = gather(encoded[0])
    ids_whole = gather(block_ids[0])
    gains = gather(jnp.stack([norm_self, norm_cross, norm_feed]), 1).astype(F32)
    gain_first, gain_second, gain_third = gains[0:1], gains[1:2], gains[2:3]
    query_first, keyval_first, output_first, table = (
        gather(self_query),
        gather(self_keyval, 1),
        gather(self_output),
        gather(bucket_bias, 1),
    )
    query_second, keyval_second, output_second = (
        gather(cross_query),
        gather(cross_keyval, 1),
        gather(cross_output),
    )
    inner, outer = gather(feed_in), gather(feed_out)

    onehot = window_buckets[None, :] == jnp.arange(bucket_count, dtype=jnp.int32)[:, None]
    window = dot(table, onehot.astype(BF16)).reshape(heads // 2, 2, window_width)

    normed_first = (inputs * rms_scale(inputs) * gain_first).astype(BF16)
    normed_whole = gather(normed_first)
    query = dot(normed_first, query_first).astype(BF16)
    keys = dot(normed_whole, keyval_first[0]).astype(BF16)
    values = dot(normed_whole, keyval_first[1]).astype(BF16)
    attended, weights = attend(
        query, keys, values, (block_ids[0][:, None], ids_whole[None, :], window)
    )
    low_first = attended.astype(BF16)
    first = inputs + dot(low_first, output_first)

    memory_keys = dot(encoded_whole, keyval_second[0]).astype(BF16)
    memory_values = dot(encoded_whole, keyval_second[1]).astype(BF16)
    normed_second = (first * rms_scale(first) * gain_second).astype(BF16)
    query_cross = dot(normed_second, query_second).astype(BF16)
    attended_cross, weights_cross = attend(query_cross, memory_keys, memory_values)
    low_second = attended_cross.astype(BF16)
    second = first + dot(low_second, output_second)

    normed_third = (second * rms_scale(second) * gain_third).astype(BF16)
    preact = dot(normed_third, inner)
    value, slope = gelu_parts(preact)
    hidden = value.astype(BF16)
    result = (second + dot(hidden, outer)).astype(BF16)

    grad_result = cotangent[0]
    d_outer = dot_tn(hidden, grad_result)
    grad_preact = (dot_nt(grad_result, outer) * slope).astype(BF16)
    d_inner = dot_tn(normed_third, grad_preact)
    back, d_gain_third = rms_back(second, gain_third, dot_nt(grad_preact, inner))
    grad_second = grad_result.astype(F32) + back

    grad_second_low = grad_second.astype(BF16)
    d_output_second = dot_tn(low_second, grad_second_low)
    grad_att = dot_nt(grad_second_low, output_second).astype(BF16)
    d_query, d_keys, d_values = attend_back(
        query_cross, memory_keys, memory_values, weights_cross, attended_cross, grad_att
    )
    d_keyval_second = jnp.stack(
        [dot_tn(encoded_whole, d_keys), dot_tn(encoded_whole, d_values)]
    )
    d_memory = scatter(dot_nt(d_keys, keyval_second[0]) + dot_nt(d_values, keyval_second[1]))
    d_query_second = dot_tn(normed_second, d_query)
    back, d_gain_second = rms_back(first, gain_second, dot_nt(d_query, query_second))
    grad_first = grad_second + back

    grad_first_low = grad_first.astype(BF16)
    d_output_first = dot_tn(low_first, grad_first_low)
    grad_att = dot_nt(grad_first_low, output_first).astype(BF16)
    d_query, d_keys, d_values, d_window = attend_back(
        query, keys, values, weights, attended, grad_att, window.shape
    )
    d_table = lax.dot_general(
        d_window.reshape(heads, window_width),
        onehot.astype(F32),
        (((1,), (1,)), ((), ())),
        precision=lax.Precision.HIGHEST,
    )
    d_keyval_first = jnp.stack([dot_tn(normed_whole, d_keys), dot_tn(normed_whole, d_values)])
    grad_normed = scatter(
        dot_nt(d_keys, keyval_first[0]) + dot_nt(d_values, keyval_first[1])
    ).astype(F32) + dot_nt(d_query, query_first)
    d_query_first = dot_tn(normed_first, d_query)
    back, d_gain_first = rms_back(inputs, gain_first, grad_normed)
    d_inputs = grad_first + back

    gains = [d_gain_first, d_gain_second, d_gain_third]
    squares = [d_query_first, d_output_first, d_query_second, d_output_second]
    pairs = [d_keyval_first, d_keyval_second]
    total = lambda a, axis=0: lax.psum(scatter(a, axis), "rep").astype(F32)
    gains = [total(gain[0]) for gain in gains]
    squares = [total(square) for square in squares]
    pairs = [total(pair, 1) for pair in pairs]
    d_table, d_inner, d_outer = total(d_table, 1), total(d_inner), total(d_outer)
    totals = (gains[0], squares[0], pairs[0], squares[1], d_table)
    totals += (gains[1], squares[2], pairs[1], squares[3], gains[2], d_inner, d_outer)
    return (result[None], d_inputs[None], d_memory.astype(F32)[None]) + totals


def solution(mesh):
    rows, line = P("rep", "shard", None), P("shard")
    matrix, pair, table = P("shard", None), P(None, "shard", None), P(None, "shard")
    weights = (line, matrix, pair, matrix, table, line, matrix, pair, matrix, line, matrix, matrix)
    return jax.shard_map(
        layer,
        mesh=mesh,
        in_specs=(rows, rows, P("rep", "shard"), P(), rows) + weights,
        out_specs=(rows, rows, rows) + weights,
        check_vma=False,
    )
```

```python
import functools
import types

import jax
import jax.numpy as jnp
from jax import lax
from jax.experimental import pallas as pl
from jax.experimental.pallas import tpu as pltpu
from jax.sharding import PartitionSpec as P

H = 12
HD = 64
LANES = 2 * HD
EPSILON = 1e-06
MASKED = -1e30
F32 = jnp.float32
BF16 = jnp.bfloat16
VMEM_LIMIT = 56 * 2**20
FUSED_LIMIT = 62 * 2**20
AHEAD = 2
LATE = (1, 3)
LATE_START = (-1, 1)
SLOTS = 4
LAG = 1
MESH = pl.DeviceIdType.MESH


def dot(a, b):
    return lax.dot_general(a, b, (((1,), (0,)), ((), ())), preferred_element_type=F32)


def dot_nt(a, b):
    return lax.dot_general(a, b, (((1,), (1,)), ((), ())), preferred_element_type=F32)


def dot_tn(a, b):
    return lax.dot_general(a, b, (((0,), (0,)), ((), ())), preferred_element_type=F32)


def rms_scale(values):
    return lax.rsqrt(jnp.mean(values * values, axis=-1, keepdims=True) + EPSILON)


def rms_back(values, gain, grad):
    scale = rms_scale(values)
    scaled = gain * grad
    mean = jnp.mean(scaled * values, axis=-1, keepdims=True)
    d_values = scale * scaled - values * (scale * scale * scale) * mean
    d_gain = jnp.sum(grad * values * scale, axis=0, keepdims=True)
    return d_values, d_gain


def gelu_parts(x):
    c = 0.7978845608028654
    t = jnp.tanh(c * (x + 0.044715 * (x * x * x)))
    value = 0.5 * x * (1.0 + t)
    slope = 0.5 * (1.0 + t) + 0.5 * x * (1.0 - t * t) * (c * (1.0 + 3.0 * 0.044715 * (x * x)))
    return value, slope


def own_lanes(first):
    lane = lax.broadcasted_iota(jnp.int32, (1, LANES), 1)
    mine = (lane < HD) if first else (lane >= HD)
    return jnp.where(mine, 1.0, 0.0)


def stack_heads(pair):
    one, two = own_lanes(True).astype(pair.dtype), own_lanes(False).astype(pair.dtype)
    return jnp.concatenate([pair * one, pair * two], axis=0)


def merge_heads(stacked):
    rows = stacked.shape[0] // 2
    return stacked[:rows] * own_lanes(True) + stacked[rows:] * own_lanes(False)


def skew(window, width):
    sub = lax.broadcasted_iota(jnp.int32, (8, width), 0)
    rows = jnp.broadcast_to(window, (8, width))
    for bit in (1, 2, 4):
        rows = jnp.where((sub & bit) != 0, pltpu.roll(rows, bit, 1), rows)
    return jnp.concatenate(
        [pltpu.roll(rows, (8 * g + width - 128) % width, 1) for g in range(16)], axis=0
    )


def unskew(total, width):
    sub = lax.broadcasted_iota(jnp.int32, (8, width), 0)
    rows = jnp.zeros((8, width), F32)
    for g in range(16):
        rows = rows + pltpu.roll(total[8 * g : 8 * g + 8], 128 - 8 * g, 1)
    for bit in (1, 2, 4):
        rows = jnp.where((sub & bit) != 0, pltpu.roll(rows, width - bit, 1), rows)
    return jnp.sum(rows, axis=0, keepdims=True)


def attend_kernel(biased, q_ref, k_ref, v_ref, *refs):
    if biased:
        row_ids, key_ids, window_ref, out_ref, p_ref = refs
    else:
        out_ref, p_ref = refs
    rows, length = q_ref.shape[0], k_ref.shape[0]
    blocks = rows // 128
    scores = dot_nt(stack_heads(q_ref[...]), k_ref[...])
    for head in range(2):
        if biased:
            width = window_ref.shape[2]
            table = skew(window_ref[0, head : head + 1, :], width)
        for b in range(blocks):
            at = head * rows + b * 128
            part = scores[at : at + 128]
            if biased:
                shift = (blocks - 1 - b) * 128
                allowed = key_ids[...] <= row_ids[b * 128 : b * 128 + 128, :]
                part = jnp.where(allowed, part + table[:, shift : shift + length], MASKED)
            top = jnp.max(part, axis=-1, keepdims=True)
            raised = jnp.exp(part - top)
            share = 1.0 / jnp.sum(raised, axis=-1, keepdims=True)
            p_ref[0, at : at + 128, :] = (raised * share).astype(BF16)
    out_ref[...] = merge_heads(dot(p_ref[0], v_ref[...]))


def attend_back_kernel(folded, q_ref, k_ref, v_ref, p_ref, out_ref, grad_ref, *refs):
    if folded:
        dq_ref, dk_ref, dv_ref, window_ref, ds_ref = refs
    else:
        dq_ref, dk_ref, dv_ref, ds_ref = refs
    rows, length = q_ref.shape[0], k_ref.shape[0]
    blocks = rows // 128
    grad = grad_ref[...]
    grads = stack_heads(grad)
    delta_wide = grad.astype(F32) * out_ref[...]
    d_weights = dot_nt(grads, v_ref[...])
    for head in range(2):
        if folded:
            width = window_ref.shape[2]
            total = jnp.zeros((128, width), F32)
        delta = jnp.sum(delta_wide * own_lanes(head == 0), axis=-1, keepdims=True)
        for b in range(blocks):
            at = head * rows + b * 128
            part = p_ref[0, at : at + 128, :].astype(F32) * (
                d_weights[at : at + 128] - delta[b * 128 : b * 128 + 128]
            )
            ds_ref[at : at + 128, :] = part.astype(BF16)
            if folded:
                shift = (blocks - 1 - b) * 128
                pieces = [part]
                if shift:
                    pieces = [jnp.zeros((128, shift), F32)] + pieces
                if width - shift - length:
                    pieces = pieces + [jnp.zeros((128, width - shift - length), F32)]
                total = total + jnp.concatenate(pieces, axis=1)
        if folded:
            window_ref[0, head : head + 1, :] = unskew(total, width)
    queries = stack_heads(q_ref[...])
    dq_ref[...] = merge_heads(dot(ds_ref[...], k_ref[...])).astype(BF16)
    dk_ref[...] = dot(queries.T, ds_ref[...]).T.astype(BF16)
    dv_ref[...] = dot(grads.T, p_ref[0]).T.astype(BF16)


def attend(query, keys, values, bias=None):
    rows, width = query.shape
    length = keys.shape[0]
    pairs = width // LANES
    column = lambda n: pl.BlockSpec((n, LANES), lambda i: (0, i))
    whole = lambda a: pl.BlockSpec(a.shape, lambda i: (0,) * a.ndim)
    operands, specs = [query, keys, values], [column(rows), column(length), column(length)]
    if bias is not None:
        row_ids, key_ids, window = bias
        operands += [row_ids, key_ids, window]
        specs += [
            whole(row_ids),
            whole(key_ids),
            pl.BlockSpec((1,) + window.shape[1:], lambda i: (i, 0, 0)),
        ]
    return pl.pallas_call(
        functools.partial(attend_kernel, bias is not None),
        grid=(pairs,),
        in_specs=specs,
        out_specs=[
            column(rows),
            pl.BlockSpec((1, 2 * rows, length), lambda i: (i, 0, 0)),
        ],
        out_shape=[
            jax.ShapeDtypeStruct((rows, width), F32),
            jax.ShapeDtypeStruct((pairs, 2 * rows, length), BF16),
        ],
        compiler_params=pltpu.CompilerParams(vmem_limit_bytes=VMEM_LIMIT),
        cost_estimate=pl.CostEstimate(
            flops=16 * rows * length * width,
            bytes_accessed=2 * pairs * 2 * rows * length,
            transcendentals=pairs * 2 * rows * length,
        ),
    )(*operands)


def attend_back(query, keys, values, weights, output, grad, window_shape=None):
    rows, width = query.shape
    length = keys.shape[0]
    pairs = width // LANES
    column = lambda n: pl.BlockSpec((n, LANES), lambda i: (0, i))
    out_specs = [column(rows), column(length), column(length)]
    out_shape = [
        jax.ShapeDtypeStruct((rows, width), BF16),
        jax.ShapeDtypeStruct((length, width), BF16),
        jax.ShapeDtypeStruct((length, width), BF16),
    ]
    if window_shape is not None:
        out_specs.append(pl.BlockSpec((1,) + window_shape[1:], lambda i: (i, 0, 0)))
        out_shape.append(jax.ShapeDtypeStruct(window_shape, F32))
    return pl.pallas_call(
        functools.partial(attend_back_kernel, window_shape is not None),
        grid=(pairs,),
        in_specs=[
            column(rows),
            column(length),
            column(length),
            pl.BlockSpec((1, 2 * rows, length), lambda i: (i, 0, 0)),
            column(rows),
            column(rows),
        ],
        out_specs=out_specs,
        out_shape=out_shape,
        scratch_shapes=[pltpu.VMEM((2 * rows, length), BF16)],
        compiler_params=pltpu.CompilerParams(vmem_limit_bytes=VMEM_LIMIT),
        cost_estimate=pl.CostEstimate(
            flops=32 * rows * length * width,
            bytes_accessed=2 * pairs * 2 * rows * length,
            transcendentals=0,
        ),
    )(query, keys, values, weights, output, grad)


def gather(values, axis=0):
    return lax.all_gather(values, "shard", axis=axis, tiled=True)


def scatter(values, axis=0):
    return lax.psum_scatter(values.astype(BF16), "shard", scatter_dimension=axis, tiled=True)


class Place:
    def __init__(self, reps, shards):
        self.nx, self.nh = shards // 2, reps // 4
        rep, shard = lax.axis_index("rep"), lax.axis_index("shard")
        self.rep, self.shard = rep, shard
        self.core, self.x = lax.rem(shard, 2), lax.div(shard, 2)
        self.y, z = lax.rem(rep, 2), lax.div(rep, 2)
        self.low, self.high = lax.rem(z, 2), lax.div(z, 2)

    def other_core(self):
        return (self.rep, self.x * 2 + 1 - self.core)

    def x_at(self, step):
        x = lax.rem(self.x + step, self.nx)
        return x, (self.rep, x * 2 + self.core)

    def other_y(self):
        return (self.rep + 1 - 2 * self.y, self.shard)

    def other_low(self):
        return (self.rep + 2 - 4 * self.low, self.shard)

    def high_at(self, step):
        high = lax.rem(self.high + step, self.nh)
        return high, (high * 4 + self.low * 2 + self.y, self.shard)

    def partners(self):
        found = [self.other_core(), self.other_y(), self.other_low()]
        found += [self.x_at(d)[1] for d in range(1, self.nx)]
        found += [self.high_at(d)[1] for d in range(1, self.nh)]
        return found


def enter(place):
    barrier = pltpu.get_barrier_semaphore()
    partners = place.partners()
    for device in partners:
        pl.semaphore_signal(barrier, inc=1, device_id=device, device_id_type=MESH)
    pl.semaphore_wait(barrier, len(partners))


def remote(src, dst, send, recv, device):
    return pltpu.make_async_remote_copy(
        src_ref=src, dst_ref=dst, send_sem=send, recv_sem=recv, device_id=device, device_id_type=MESH
    )


def added(*parts):
    total = parts[0].astype(F32)
    for part in parts[1:]:
        total = total + part.astype(F32)
    return total


class Reduction:
    def __init__(self, place, x_first, names, fin, parts, recv_x, recv_y, recv_low, recv_high, send, recv, own_sem):
        self.place, self.x_first, self.parts, self.fin = place, x_first, parts, fin
        self.names = names
        self.recv_x, self.recv_y, self.recv_low, self.recv_high = recv_x, recv_y, recv_low, recv_high
        self.send, self.recv, self.own_sem = send, recv, own_sem
        self.half = parts.shape[3] // 2
        self.rows = self.half // place.nh
        stages = [self.over_y, self.over_low, self.over_high]
        stages = [self.over_x] + stages if x_first else stages + [self.over_x]
        stages += [self.back_high, self.back_low, self.back_y]
        self.copies = stages
        self.adds = stages.index(self.back_high)

    @staticmethod
    def scratch(n, x_first, nx, nh, q, half):
        copies = 4 + nx + 2 * (nh - 1)
        wide = (n,) if x_first else (n, nx)
        x_part = (2, q) if x_first else (q // (2 * nh),)
        return [
            pltpu.VMEM((n, nx, 2, q, half), BF16),
            pltpu.VMEM((n, nx - 1) + x_part + (half,), BF16),
            pltpu.VMEM(wide + (q, half), BF16),
            pltpu.VMEM(wide + (q // 2, half), BF16),
            pltpu.VMEM((n, nh - 1) + wide[1:] + (q // (2 * nh), half), BF16),
            pltpu.SemaphoreType.DMA((n, copies)),
            pltpu.SemaphoreType.DMA((n, copies)),
            pltpu.SemaphoreType.DMA((n,)),
        ]

    def copy(self, u, which, src, dst, device):
        return remote(src, dst, self.send.at[u, which], self.recv.at[u, which], device)

    def low_rows(self, low):
        return pl.ds(pl.multiple_of(low * self.half, 16), self.half)

    def high_rows(self, high):
        at = self.place.low * self.half + high * self.rows
        return pl.ds(pl.multiple_of(at, 16), self.rows)

    def chips(self):
        return self.place.x if self.x_first else slice(None)

    def over_core(self, u, src):
        return [self.copy(u, 0, src, self.parts.at[u], self.place.other_core())]

    def over_x(self, u):
        p, out = self.place, []
        rest = () if self.x_first else (p.y, self.high_rows(p.high))
        for d in range(1, p.nx):
            x, device = p.x_at(d)
            src = self.parts.at[(u, x) + rest]
            out.append(self.copy(u, 2 + d, src, self.recv_x.at[u, d - 1], device))
        return out, (u, p.x) + rest, [self.recv_x.at[u, d] for d in range(p.nx - 1)]

    def over_y(self, u):
        p, chips = self.place, self.chips()
        src = self.parts.at[u, chips, 1 - p.y]
        copies = [self.copy(u, 1, src, self.recv_y.at[u], p.other_y())]
        return copies, (u, chips, p.y), [self.recv_y.at[u]]

    def over_low(self, u):
        p, chips = self.place, self.chips()
        src = self.parts.at[u, chips, p.y, self.low_rows(1 - p.low)]
        copies = [self.copy(u, 2 + p.nx, src, self.recv_low.at[u], p.other_low())]
        return copies, (u, chips, p.y, self.low_rows(p.low)), [self.recv_low.at[u]]

    def over_high(self, u):
        p, chips, out = self.place, self.chips(), []
        for d in range(1, p.nh):
            high, device = p.high_at(d)
            src = self.parts.at[u, chips, p.y, self.high_rows(high)]
            out.append(self.copy(u, 3 + p.nx + d, src, self.recv_high.at[u, d - 1], device))
        came = [self.recv_high.at[u, d] for d in range(p.nh - 1)]
        return out, (u, chips, p.y, self.high_rows(p.high)), came

    def piece(self, u):
        p = self.place
        rows = self.high_rows(p.high)
        return self.parts.at[u, p.x, p.y, rows], self.fin.at[self.names[u], p.y, rows]

    def keep(self, u):
        return pltpu.make_async_copy(*self.piece(u), self.own_sem.at[u])

    def back_high(self, u):
        p = self.place
        return [
            self.copy(u, 2 + p.nx + p.nh + d, *self.piece(u), p.high_at(d)[1])
            for d in range(1, p.nh)
        ]

    def back_low(self, u):
        p = self.place
        rows = self.fin.at[self.names[u], p.y, self.low_rows(p.low)]
        return [self.copy(u, 3 + p.nx, rows, rows, p.other_low())]

    def back_y(self, u):
        half = self.fin.at[self.names[u], self.place.y]
        return [self.copy(u, 2, half, half, self.place.other_y())]

    def begin(self, u, src):
        self.over_core(u, src)[0].start()

    def collect(self, u, src, own):
        self.over_core(u, src)[0].wait_recv()
        self.parts[u] = added(self.parts[u], own[...]).astype(BF16)

    def start(self, u, stage):
        if stage < len(self.copies):
            copies = self.copies[stage](u)
            for copy in copies[0] if stage < self.adds else copies:
                copy.start()

    def step(self, u, stage):
        if stage < self.adds:
            copies, stays, came = self.copies[stage](u)
            for copy in copies:
                copy.wait_recv()
            total = added(self.parts[stays], *[part[...] for part in came])
            self.parts[stays] = total.astype(BF16)
            if stage + 1 == self.adds:
                self.keep(u).start()
        else:
            for copy in self.copies[stage](u):
                copy.wait_recv()
            if stage == self.adds:
                self.keep(u).wait()
        self.start(u, stage + 1)

    def sent(self, u):
        for stage in range(len(self.copies)):
            copies = self.copies[stage](u)
            for copy in copies[0] if stage < self.adds else copies:
                copy.wait_send()


class SmallSum:
    def __init__(self, place, held, landed, send, recv):
        self.place, self.held, self.landed = place, held, landed
        self.send, self.recv = send, recv

    @staticmethod
    def scratch(nx, nh, shape):
        copies = 3 + nx - 1 + nh - 1
        return [
            pltpu.VMEM((6,) + shape, F32),
            pltpu.VMEM((copies,) + shape, F32),
            pltpu.SemaphoreType.DMA((copies,)),
            pltpu.SemaphoreType.DMA((copies,)),
        ]

    def copies(self, stage):
        p = self.place
        first, devices = [
            (0, [p.other_core()]),
            (3, [p.x_at(d)[1] for d in range(1, p.nx)]),
            (1, [p.other_y()]),
            (2, [p.other_low()]),
            (2 + p.nx, [p.high_at(d)[1] for d in range(1, p.nh)]),
        ][stage]
        return [
            remote(self.held.at[stage], self.landed.at[first + i], self.send.at[first + i], self.recv.at[first + i], device)
            for i, device in enumerate(devices)
        ], list(range(first, first + len(devices)))

    def begin(self, value):
        self.held[0] = value
        self.launch()

    def launch(self):
        for copy in self.copies(0)[0]:
            copy.start()

    def step(self, stage, stages=5):
        copies, slots = self.copies(stage)
        for copy in copies:
            copy.wait_recv()
        total = self.held[stage]
        for slot in slots:
            total = total + self.landed[slot]
        self.held[stage + 1] = total
        if stage + 1 < stages:
            for copy in self.copies(stage + 1)[0]:
                copy.start()
        return total

    def sent(self, stages=5):
        for stage in range(stages):
            for copy in self.copies(stage)[0]:
                copy.wait_send()


class Gather:
    def __init__(self, place, whole, own, hidden_rows, send, recv, own_sem):
        self.place, self.whole, self.own = place, whole, own
        self.send, self.recv, self.own_sem = send, recv, own_sem
        self.width = whole.shape[1]
        self.q = self.width // (2 * place.nx)
        self.square = len(own) - hidden_rows // self.q
        self.hidden_rows = hidden_rows

    @staticmethod
    def scratch(units, nx):
        copies = 1 + 4 * (nx - 1)
        return [
            pltpu.SemaphoreType.DMA((units, copies)),
            pltpu.SemaphoreType.DMA((units, copies)),
            pltpu.SemaphoreType.DMA((units,)),
        ]

    def rows(self, u, shard, half=None):
        if isinstance(u, int) and u >= self.square:
            at = self.square * self.width + shard * self.hidden_rows + (u - self.square) * self.q
        else:
            at = u * self.width + shard * self.q
        if half is None:
            return pl.ds(pl.multiple_of(at, 16), self.q)
        return pl.ds(pl.multiple_of(at + half * (self.q // 2), 16), self.q // 2)

    def part(self, u, shard, half=None):
        return self.whole.at[self.rows(u, shard, half)]

    def copy(self, u, which, src, dst, device):
        return remote(src, dst, self.send.at[u, which], self.recv.at[u, which], device)

    def to_core(self, u):
        shard = self.place.shard
        return self.copy(u, 0, self.own[u], self.part(u, shard), self.place.other_core())

    def keep(self, u):
        return pltpu.make_async_copy(
            self.own[u], self.part(u, self.place.shard), self.own_sem.at[u]
        )

    def over_x(self, u, d):
        p = self.place
        half = self.own[u].at[pl.ds(pl.multiple_of(p.y * (self.q // 2), 16), self.q // 2)]
        return self.copy(u, 4 * d - 3, half, self.part(u, p.shard, p.y), p.x_at(d)[1])

    def came(self, d):
        p = self.place
        return lax.rem(p.x + p.nx - d, p.nx) * 2 + p.core

    def on_y(self, u, d):
        p = self.place
        here = self.part(u, self.came(d), p.y)
        return self.copy(u, 4 * d - 2, here, here, p.other_y())

    def on_core(self, u, d):
        p = self.place
        here = self.part(u, self.came(d), p.y)
        return self.copy(u, 4 * d - 1, here, here, p.other_core())

    def last_core(self, u, d):
        p = self.place
        here = self.part(u, self.came(d), 1 - p.y)
        return self.copy(u, 4 * d, here, here, p.other_core())

    def issue(self, u):
        for d in range(1, self.place.nx):
            self.over_x(u, d).start()
        self.to_core(u).start()
        self.keep(u).start()

    def relay_x(self, u):
        for d in range(1, self.place.nx):
            self.arrive_x(u, d)
            self.on_y(u, d).start()
            self.on_core(u, d).start()

    def arrive_x(self, u, d):
        p = self.place
        here = self.part(u, self.came(d), p.y)
        self.copy(u, 4 * d - 3, here, here, p.x_at(d)[1]).wait_recv()

    def relay_y(self, u):
        for d in range(1, self.place.nx):
            self.on_y(u, d).wait_recv()
            self.last_core(u, d).start()

    def ready(self, u):
        p = self.place
        here = self.part(u, p.shard)
        pltpu.make_async_copy(here, here, self.own_sem.at[u]).wait()
        self.copy(u, 0, here, here, p.other_core()).wait_recv()
        for d in range(1, p.nx):
            self.on_core(u, d).wait_recv()
            self.last_core(u, d).wait_recv()

    def sent(self, u):
        p = self.place
        here = self.part(u, p.shard)
        self.copy(u, 0, here, here, p.other_core()).wait_send()
        for d in range(1, p.nx):
            here = self.part(u, self.came(d), p.y)
            self.copy(u, 4 * d - 3, here, here, p.x_at(d)[1]).wait_send()
            self.on_y(u, d).wait_send()
            self.on_core(u, d).wait_send()
            self.last_core(u, d).wait_send()


class Spread:
    def __init__(self, place, own, whole, send, recv, own_sem):
        self.place, self.own, self.whole = place, own, whole
        self.send, self.recv, self.own_sem = send, recv, own_sem
        self.count = own.shape[0]

    @staticmethod
    def scratch(nx):
        copies = 1 + 2 * (nx - 1)
        return [
            pltpu.SemaphoreType.DMA((copies,)),
            pltpu.SemaphoreType.DMA((copies,)),
            pltpu.SemaphoreType.DMA(()),
        ]

    def part(self, shard):
        return self.whole.at[pl.ds(pl.multiple_of(shard * self.count, 16), self.count)]

    def copy(self, which, src, dst, device):
        return remote(src, dst, self.send.at[which], self.recv.at[which], device)

    def to_core(self):
        return self.copy(0, self.own, self.part(self.place.shard), self.place.other_core())

    def over_x(self, d):
        p = self.place
        return self.copy(2 * d - 1, self.own, self.part(p.shard), p.x_at(d)[1])

    def on_core(self, d):
        p = self.place
        here = self.part(lax.rem(p.x + p.nx - d, p.nx) * 2 + p.core)
        return self.copy(2 * d, here, here, p.other_core())

    def keep(self):
        return pltpu.make_async_copy(self.own, self.part(self.place.shard), self.own_sem)

    def issue(self):
        for d in range(1, self.place.nx):
            self.over_x(d).start()
        self.to_core().start()
        self.keep().start()

    def relay_x(self):
        for d in range(1, self.place.nx):
            self.over_x(d).wait_recv()
            self.on_core(d).start()

    def ready(self):
        self.keep().wait()
        self.to_core().wait_recv()
        for d in range(1, self.place.nx):
            self.on_core(d).wait_recv()

    def sent(self):
        self.to_core().wait_send()
        for d in range(1, self.place.nx):
            self.over_x(d).wait_send()
            self.on_core(d).wait_send()


def attend_pair(query, keys, values_ref, p_ref, bias=None):
    rows, length = query.shape[0], keys.shape[0]
    blocks = rows // 128
    scores = dot_nt(stack_heads(query), keys)
    for head in range(2):
        if bias is not None:
            row_ids, key_ids, window = bias
            table = skew(window[head : head + 1], window.shape[1])
        for b in range(blocks):
            at = head * rows + b * 128
            part = scores[at : at + 128]
            if bias is not None:
                shift = (blocks - 1 - b) * 128
                allowed = key_ids <= row_ids[b * 128 : b * 128 + 128]
                part = jnp.where(allowed, part + table[:, shift : shift + length], MASKED)
            top = jnp.max(part, axis=-1, keepdims=True)
            raised = jnp.exp(part - top)
            share = 1.0 / jnp.sum(raised, axis=-1, keepdims=True)
            p_ref[at : at + 128, :] = (raised * share).astype(BF16)
    return merge_heads(dot(p_ref[...], values_ref[...]))


def bucket_onehot(buckets_ref, place, rows, length):
    start = length - rows - place.shard * rows
    window = buckets_ref[:, pl.ds(pl.multiple_of(start, LANES), length + rows)]
    which = lax.broadcasted_iota(jnp.int32, (LANES, length + rows), 0)
    return jnp.where(window == which, 1.0, 0.0)


def forward_kernel(reps, shards, names, *refs):
    r = types.SimpleNamespace(**dict(zip(names, refs)))
    place = Place(reps, shards)
    rows, width = r.tok_in.shape
    length = r.tok.shape[0]
    pairs = width // LANES
    q = width // shards
    part = r.feed_in.shape[1] // width
    own = [r.self_query, r.self_keyval.at[0], r.self_keyval.at[1], r.self_output]
    own += [r.cross_query, r.cross_keyval.at[0], r.cross_keyval.at[1], r.cross_output]
    own += [r.feed_in.at[:, pl.ds(j * width, width)] for j in range(part)]
    own += [r.feed_out.at[pl.ds(j * q, q)] for j in range(part)]
    units = len(own)
    small = SmallSum(place, r.small_held, r.small_landed, r.small_send, r.small_recv)
    gather = Gather(place, r.whole, own, r.feed_out.shape[0], r.w_send, r.w_recv, r.w_own)
    tokens = Spread(place, r.tok_in, r.tok, r.t_send, r.t_recv, r.t_own)
    memories = Spread(place, r.enc_in, r.enc, r.e_send, r.e_recv, r.e_own)

    def weight(u):
        return r.whole[pl.ds(pl.multiple_of(u * width, width), width), :]

    def emit_weights(u, count):
        block = pl.ds(u * width, count * width)
        return pltpu.make_async_copy(r.whole.at[block], r.w_out.at[block], r.out_sem.at[u])

    def emit_kv(i):
        return pltpu.make_async_copy(r.kv.at[i], r.kv_out.at[i], r.out_sem.at[units + i])

    emit_tok = pltpu.make_async_copy(r.tok_t, r.tok_out, r.out_sem.at[units + 4])
    emit_enc = pltpu.make_async_copy(r.enc_t, r.enc_out, r.out_sem.at[units + 5])

    def emit_p(which, i):
        slot = lax.rem(i, 2)
        return pltpu.make_async_copy(r.probs.at[slot], r.p_out.at[which, i], r.p_sem.at[slot])

    def gain(i):
        return r.small_held[2, i : i + 1, :width]

    shard = place.shard
    wide = r.small_held.shape[2]
    sub = lax.broadcasted_iota(jnp.int32, (8, wide), 0)
    padded = lambda a: jnp.concatenate([a, jnp.zeros((a.shape[0], wide - a.shape[1]), F32)], axis=1)
    shifted = lambda a, by: pltpu.roll(padded(a), shard * by, 1)
    ids = r.ids[...].astype(F32)
    gains = [gain_ref[...].astype(F32).reshape(1, q) for gain_ref in (r.norm_self, r.norm_cross, r.norm_feed)]
    mine = jnp.concatenate(gains + [jnp.zeros((5, q), F32)], axis=0)
    mine = jnp.where(sub == 3, 0.0, shifted(mine, q))
    mine = mine + jnp.where(sub == 3, shifted(jnp.broadcast_to(ids, (8, rows)), rows), 0.0)
    table = r.bucket_bias[...].astype(F32).T
    heads, cut = table.shape
    table = jnp.concatenate([table, jnp.zeros((16 - heads, cut), F32)], axis=0)
    r.small_held[0] = jnp.concatenate([mine, shifted(table, cut)], axis=0)
    r.row_ids[...] = jnp.broadcast_to(ids, (8, rows)).T[:, 0:1]
    enter(place)
    small.launch()
    line = [(gather, (u,)) for u in (1, 2, 0)] + [(tokens, ()), (memories, ())]
    line += [(gather, (u,)) for u in [3, 5, 6, 4, 7] + list(range(8, units))]

    def issue(at):
        if at < len(line):
            line[at][0].issue(*line[at][1])

    def relay(owner, *u):
        owner.relay_x(*u)
        issue(line.index((owner, u)) + AHEAD)

    for at in range(AHEAD):
        issue(at)
    small.step(0, 2)
    gathered = small.step(1, 2)
    r.small_out[...] = gathered
    table = gathered[8:24, :LANES].astype(BF16)
    biases = dot(table, bucket_onehot(r.buckets, place, rows, length).astype(BF16))
    for i in range(pairs):
        r.window[i] = biases[2 * i : 2 * i + 2]
    for u in (1, 2, 0):
        relay(gather, u)
    for u in (1, 2, 0):
        gather.relay_y(u)
    relay(tokens)
    tokens.ready()
    tokens.sent()

    def norm_rows(i, carry):
        at = pl.ds(pl.multiple_of(i * rows, 16), rows)
        values = r.tok[at, :].astype(F32)
        normed = (values * rms_scale(values) * gain(0)).astype(BF16)
        r.tok[at, :] = normed
        r.tok_t[:, pl.ds(pl.multiple_of(i * rows, LANES), rows)] = normed.T
        return carry

    lax.fori_loop(0, length // rows, norm_rows, 0)
    emit_tok.start()

    def project_pair(source, target, base):
        def step(i, carry):
            at = pl.ds(pl.multiple_of(i * rows, 16), rows)
            block = source[at, :]
            for which in range(2):
                out = dot(block, weight(base + which)).astype(BF16)
                for j in range(pairs):
                    r.kv[target + which, j, at, :] = out[:, j * LANES : (j + 1) * LANES]
            return carry

        lax.fori_loop(0, source.shape[0] // rows, step, 0)
        emit_kv(target).start()
        emit_kv(target + 1).start()

    def project_query(normed, u, which):
        out = dot(normed, weight(u)).astype(BF16)
        for j in range(pairs):
            r.q_out[which, j] = out[:, j * LANES : (j + 1) * LANES]

    def attention(which, bias, relays):
        def pair(i, carry):
            @pl.when(i >= 2)
            def _():
                emit_p(which, i).wait()

            slot = lax.rem(i, 2)
            more = None
            if bias:
                more = (r.row_ids[...], r.small_held[2, 3:4, :length], r.window[i])
            r.low_out[which, i] = attend_pair(
                r.q_out[which, i],
                r.kv[2 * which, i],
                r.kv.at[2 * which + 1, i],
                r.probs.at[slot],
                more,
            )
            emit_p(which, i).start()
            for step, relay, u in relays:
                @pl.when(i == step)
                def _():
                    relay(*u)

            return carry

        lax.fori_loop(0, pairs, pair, 0)
        emit_p(which, 0).wait()
        emit_p(which, 1).wait()
        low = [r.low_out[which, j].astype(BF16) for j in range(pairs)]
        low = jnp.concatenate(low, axis=1)
        r.low_t[which] = low.T
        return low

    gather.ready(1)
    gather.ready(2)
    project_pair(r.tok, 0, 1)
    gather.ready(0)
    emit_weights(0, 3).start()
    mine = pl.ds(pl.multiple_of(place.shard * rows, 16), rows)
    project_query(r.tok[mine, :], 0, 0)
    over_y = gather.relay_y

    def over_x(u):
        relay(gather, u)

    low = attention(
        0,
        True,
        [
            (0, relay, (memories,)),
            (1, over_x, (3,)),
            (2, over_x, (5,)),
            (3, over_x, (6,)),
            (3, over_y, (3,)),
            (4, over_x, (4,)),
            (4, over_y, (5,)),
            (5, over_y, (6,)),
        ],
    )
    gather.ready(3)
    r.first_out[...] = r.tok_in[...].astype(F32) + dot(low, weight(3))
    over_x(7)
    over_y(4)
    memories.ready()

    def turn_rows(i, carry):
        at = pl.ds(pl.multiple_of(i * rows, LANES), rows)
        r.enc_t[:, at] = r.enc[at, :].T
        return carry

    lax.fori_loop(0, length // rows, turn_rows, 0)
    emit_enc.start()
    gather.ready(5)
    gather.ready(6)
    project_pair(r.enc, 2, 5)
    gather.ready(4)
    first = r.first_out[...]
    normed = (first * rms_scale(first) * gain(1)).astype(BF16)
    r.normed2_t[...] = normed.T
    project_query(normed, 4, 1)
    over_x(8)
    over_y(7)
    low = attention(
        1,
        False,
        [
            (1, over_x, (9,)),
            (1, over_y, (8,)),
            (2, over_x, (10,)),
            (3, over_y, (9,)),
            (4, over_x, (11,)),
            (5, over_y, (10,)),
        ],
    )
    gather.ready(7)
    emit_weights(3, 5).start()
    r.second_out[...] = r.first_out[...] + dot(low, weight(7))
    over_x(12)
    over_y(11)
    second = r.second_out[...]
    normed = (second * rms_scale(second) * gain(2)).astype(BF16)
    r.normed[...] = normed
    r.normed3_t[...] = normed.T
    for j in range(part):
        gather.ready(8 + j)
        value, slope = gelu_parts(dot(r.normed[...], weight(8 + j)))
        value = value.astype(BF16)
        r.hidden[j] = value
        r.hidden_t[j * width : (j + 1) * width, :] = value.T
        r.slope_out[j] = slope
        if j + 1 < part:
            over_x(13 + j)
            over_y(12 + j)
    over_y(units - 1)
    for j in range(part):
        gather.ready(8 + part + j)
    emit_weights(8, units - 8).start()
    total = second
    for j in range(part):
        total = total + dot(r.hidden[j], weight(8 + part + j))
    r.result[...] = total.astype(BF16)
    for u in range(units):
        gather.sent(u)
    memories.sent()
    small.sent(2)
    for u, count in ((0, 3), (3, 5), (8, units - 8)):
        emit_weights(u, count).wait()
    for i in range(4):
        emit_kv(i).wait()
    emit_tok.wait()
    emit_enc.wait()


def forward(tokens, encoded, ids, buckets, gains, bucket_bias, shards_of, reps, shards):
    rows, width = tokens.shape
    length, memory = rows * shards, encoded.shape[0] * shards
    nx = shards // 2
    feed_in, feed_out = shards_of[-2:]
    hidden = feed_in.shape[1]
    units = 8 + 2 * (hidden // width)
    pairs = width // LANES
    small = (24, max(length, width))
    kept = lambda *shape, dtype=BF16: (pl.BlockSpec(memory_space=pl.ANY), jax.ShapeDtypeStruct(shape, dtype))
    near = lambda *shape, dtype=F32: (pl.BlockSpec(memory_space=pltpu.VMEM), jax.ShapeDtypeStruct(shape, dtype))
    outs = dict(
        result=near(rows, width, dtype=BF16),
        first_out=near(rows, width),
        second_out=near(rows, width),
        low_out=near(2, pairs, rows, LANES),
        q_out=near(2, pairs, rows, LANES, dtype=BF16),
        small_out=near(*small),
        low_t=near(2, width, rows, dtype=BF16),
        normed2_t=near(width, rows, dtype=BF16),
        normed3_t=near(width, rows, dtype=BF16),
        hidden_t=near(hidden, rows, dtype=BF16),
        slope_out=near(hidden // width, rows, width),
        w_out=kept(units * width, width),
        kv_out=kept(4, pairs, length, LANES),
        tok_out=kept(width, length),
        enc_out=kept(width, memory),
        p_out=kept(2, pairs, 2 * rows, length),
    )
    scratch = dict(
        whole=pltpu.VMEM((units * width, width), BF16),
        tok=pltpu.VMEM((length, width), BF16),
        enc=pltpu.VMEM((memory, width), BF16),
        kv=pltpu.VMEM((4, pairs, length, LANES), BF16),
        window=pltpu.VMEM((pairs, 2, length + rows), F32),
        row_ids=pltpu.VMEM((rows, 1), F32),
        probs=pltpu.VMEM((2, 2 * rows, length), BF16),
        normed=pltpu.VMEM((rows, width), BF16),
        hidden=pltpu.VMEM((hidden // width, rows, width), BF16),
        tok_t=pltpu.VMEM((width, length), BF16),
        enc_t=pltpu.VMEM((width, memory), BF16),
        p_sem=pltpu.SemaphoreType.DMA((2,)),
        out_sem=pltpu.SemaphoreType.DMA((units + 6,)),
    )
    scratch.update(zip(("small_held", "small_landed", "small_send", "small_recv"), SmallSum.scratch(nx, reps // 4, small)))
    scratch.update(zip(("w_send", "w_recv", "w_own"), Gather.scratch(units, nx)))
    scratch.update(zip(("t_send", "t_recv", "t_own"), Spread.scratch(nx)))
    scratch.update(zip(("e_send", "e_recv", "e_own"), Spread.scratch(nx)))
    shard_names = ["self_query", "self_keyval", "self_output", "cross_query", "cross_keyval", "cross_output", "feed_in", "feed_out"]
    near_names = ["tok_in", "enc_in", "ids", "buckets", "norm_self", "norm_cross", "norm_feed", "bucket_bias"]
    names = near_names + shard_names + list(outs) + list(scratch)
    made = pl.pallas_call(
        functools.partial(forward_kernel, reps, shards, tuple(names)),
        in_specs=[pl.BlockSpec(memory_space=pltpu.VMEM)] * 8 + [pl.BlockSpec(memory_space=pl.ANY)] * 8,
        out_specs=[spec for spec, _ in outs.values()],
        out_shape=[shape for _, shape in outs.values()],
        scratch_shapes=list(scratch.values()),
        compiler_params=pltpu.CompilerParams(
            collective_id=2, has_side_effects=True, vmem_limit_bytes=FUSED_LIMIT
        ),
    )(tokens, encoded, ids, buckets, *gains, bucket_bias, *shards_of)
    return types.SimpleNamespace(**dict(zip(outs, made)))


class RowSum:
    def __init__(self, place, parts, recv_a, recv_b, send, recv):
        self.place, self.parts, self.recv_a, self.recv_b = place, parts, recv_a, recv_b
        self.send, self.recv = send, recv

    @staticmethod
    def scratch(nx, width, rows):
        return [
            pltpu.VMEM((2, nx, width, rows), BF16),
            pltpu.VMEM((nx, width, rows), BF16),
            pltpu.VMEM((nx - 1, width, rows), BF16),
            pltpu.SemaphoreType.DMA((nx,)),
            pltpu.SemaphoreType.DMA((nx,)),
        ]

    def copy(self, which, src, dst, device):
        return remote(src, dst, self.send.at[which], self.recv.at[which], device)

    def to_core(self):
        p = self.place
        return self.copy(0, self.parts.at[1 - p.core], self.recv_a, p.other_core())

    def over_x(self, d):
        x, device = self.place.x_at(d)
        return self.copy(d, self.recv_a.at[x], self.recv_b.at[d - 1], device)

    def begin(self, total):
        rows = self.parts.shape[3]
        for s in range(2 * self.place.nx):
            self.parts[s % 2, s // 2] = total[:, s * rows : (s + 1) * rows].astype(BF16)
        self.to_core().start()

    def pass_x(self):
        self.to_core().wait_recv()
        self.recv_a[...] = added(self.recv_a[...], self.parts[self.place.core]).astype(BF16)
        for d in range(1, self.place.nx):
            self.over_x(d).start()

    def finish(self):
        p = self.place
        for d in range(1, p.nx):
            self.over_x(d).wait_recv()
        return added(self.recv_a[p.x], *[self.recv_b[d] for d in range(p.nx - 1)])

    def sent(self):
        for d in range(1, self.place.nx):
            self.over_x(d).wait_send()


def attend_back_pair(query, keys, values, p_ref, output, grad, ds_ref, width=None):
    rows, length = query.shape[0], keys.shape[0]
    blocks = rows // 128
    grads, queries = stack_heads(grad), stack_heads(query)
    delta_wide = grad.astype(F32) * output
    d_weights = dot_nt(grads, values)
    windows = []
    for head in range(2):
        delta = jnp.sum(delta_wide * own_lanes(head == 0), axis=-1, keepdims=True)
        total = None
        for b in range(blocks):
            at = head * rows + b * 128
            part = p_ref[at : at + 128, :].astype(F32) * (
                d_weights[at : at + 128] - delta[b * 128 : b * 128 + 128]
            )
            ds_ref[at : at + 128, :] = part.astype(BF16)
            if width is not None:
                shift = (blocks - 1 - b) * 128
                pieces = [jnp.zeros((128, shift), F32)] if shift else []
                pieces.append(part)
                if width - shift - length:
                    pieces.append(jnp.zeros((128, width - shift - length), F32))
                placed = jnp.concatenate(pieces, axis=1)
                total = placed if total is None else total + placed
        if width is not None:
            windows.append(unskew(total, width))
    d_query = merge_heads(dot(ds_ref[...], keys)).astype(BF16)
    d_keys = dot(queries.T, ds_ref[...]).astype(BF16)
    d_values = dot(grads.T, p_ref[...]).astype(BF16)
    return d_query, d_keys, d_values, windows


REDUCTION = ("_parts", "_x", "_y", "_low", "_high", "_send", "_recv", "_own")


def late_units(units):
    return [n for n in LATE if n < units]


def backward_kernel(reps, shards, names, *refs):
    r = types.SimpleNamespace(**dict(zip(names, refs)))
    place = Place(reps, shards)
    rows, width = r.cotangent.shape
    length = r.enc_t.shape[1]
    pairs = width // LANES
    q = width // shards
    part = r.hidden_t.shape[0] // width
    units = 8 + 2 * part
    late = late_units(units)
    order = [n for n in range(units) if n not in late]
    reductions = [
        Reduction(place, x_first, names, r.fin, *(getattr(r, name + end) for end in REDUCTION))
        for x_first, names, name in ((True, order, "a"), (False, late, "b"))
    ]
    stages = len(reductions[0].copies)

    def owner(n):
        return (reductions[1], late.index(n)) if n in late else (reductions[0], order.index(n))

    small = SmallSum(place, r.small_held, r.small_landed, r.small_send, r.small_recv)
    sum_memory = RowSum(place, r.m_parts, r.m_a, r.m_b, r.m_send, r.m_recv)
    sum_tokens = RowSum(place, r.m_parts, r.t_a, r.t_b, r.t_send, r.t_recv)

    def gain(i):
        return r.gains[i : i + 1, :width]

    def load_weight(u, slot):
        block = pl.ds(u * width, width)
        return pltpu.make_async_copy(r.w_in.at[block], r.w.at[slot], r.w_sem.at[slot])

    def load_slope(j):
        slot = j % 2
        return pltpu.make_async_copy(r.slope.at[j], r.slopes.at[slot], r.s_sem.at[slot])

    def load_kv(i, slot):
        return pltpu.make_async_copy(r.kv_in.at[i], r.kv.at[slot], r.kv_sem.at[slot])

    def load_p(which, i):
        slot = lax.rem(i, 2)
        return pltpu.make_async_copy(r.p_in.at[which, i], r.probs.at[slot], r.p_sem.at[slot])

    def load_t(source, which):
        return pltpu.make_async_copy(source, r.rows_t, r.t_sem.at[which])

    def away(n):
        return r.made.at[n % SLOTS, 1 - place.core]

    def fill(n, value):
        slot = n % SLOTS
        rest = value.shape[0] // shards
        half = width // 2
        for s in range(shards):
            for h in range(2):
                r.made[slot, s % 2, s // 2, h] = value[
                    s * rest : (s + 1) * rest, h * half : (h + 1) * half
                ].astype(BF16)
        red, u = owner(n)
        red.begin(u, away(n))

    def left(n):
        red, u = owner(n)
        red.over_core(u, away(n))[0].wait_send()

    def free(n):
        if n >= SLOTS:
            left(n - SLOTS)

    def take(n):
        red, u = owner(n)
        red.collect(u, away(n), r.made.at[n % SLOTS, place.core])
        if n in late:
            red.start(u, 0)
        elif order.index(n) < AHEAD:
            red.start(u, 0)

    done_stages = {n: 0 for n in range(units)}

    def move(n, upto):
        red, u = owner(n)
        while done_stages[n] < min(upto, stages):
            red.step(u, done_stages[n])
            done_stages[n] += 1

    def advance(t):
        for back in range(stages):
            at = t - back
            if 0 <= at < len(order):
                move(order[at], back + 1)
            if back == 0 and 0 <= t + AHEAD < len(order):
                red, u = owner(order[t + AHEAD])
                red.start(u, 0)
        for i, n in enumerate(late):
            move(n, t - LATE_START[i])

    enter(place)
    load_slope(0).start()
    for slot, u in enumerate((8, 8 + part)):
        load_weight(u, slot).start()
    for slot in range(2):
        load_kv(2 + slot, slot).start()
        load_p(1, slot).start()
    load_t(r.enc_t, 0).start()
    r.acc[...] = jnp.zeros((rows, width), F32)

    for j in range(part):
        slot = 2 * (j % 2)
        load_weight(8, slot).wait()
        load_weight(8 + part, slot + 1).wait()
        load_slope(j).wait()
        if j + 1 < part:
            load_slope(j + 1).start()
            load_weight(8 + j + 1, 2 - slot).start()
            load_weight(8 + part + j + 1, 3 - slot).start()
        grad_hidden = dot_nt(r.cotangent[...], r.w[slot + 1])
        grad = (grad_hidden * r.slopes[j % 2]).astype(BF16)
        free(j)
        fill(j, dot(r.normed3_t[...], grad))
        r.acc[...] += dot_nt(grad, r.w[slot])
        if j >= 1:
            take(j - 1)
    for slot, u in ((0, 7), (1, 5), (2, 6), (3, 4)):
        load_weight(u, slot).start()
    take(part - 1)
    for m in range(part):
        n = part + m
        free(n)
        value = jnp.concatenate(
            [
                dot(r.hidden_t[s * width + m * q : s * width + (m + 1) * q, :], r.cotangent[...])
                for s in range(shards)
            ],
            axis=0,
        )
        fill(n, value)
        if m >= 1:
            take(n - 1)
    back, d_gain3 = rms_back(r.second[...], gain(2), r.acc[...])
    r.grad[...] = r.cotangent[...].astype(F32) + back
    take(2 * part - 1)
    advance(0)

    def attention(which, fold, steps):
        def pair(i, carry):
            slot = lax.rem(i, 2)
            load_p(which, i).wait()
            d_query, d_keys, d_values, windows = attend_back_pair(
                r.queries[which, i],
                r.kv[0, i],
                r.kv[1, i],
                r.probs.at[slot],
                r.low[which, i],
                r.grad_att[i],
                r.ds,
                length + rows if fold else None,
            )
            r.d_query[i] = d_query
            at = pl.ds(pl.multiple_of(i * LANES, LANES), LANES)
            r.dk_t[at, :] = d_keys
            r.dv_t[at, :] = d_values
            if fold:
                r.d_window[i] = jnp.concatenate(windows, axis=0)

            @pl.when(i + 2 < pairs)
            def _():
                load_p(which, i + 2).start()

            for step, n in steps:
                @pl.when(i == step)
                def _():
                    advance(n)

            return carry

        lax.fori_loop(0, pairs, pair, 0)

    def spread_grad(value):
        for i in range(pairs):
            r.grad_att[i] = value[:, i * LANES : (i + 1) * LANES].astype(BF16)

    def joined_query():
        return jnp.concatenate([r.d_query[i] for i in range(pairs)], axis=1)

    n = 2 * part
    grad_low = r.grad[...].astype(BF16)
    free(n)
    fill(n, dot(r.low_t[1], grad_low))
    load_weight(7, 0).wait()
    spread_grad(dot_nt(grad_low, r.w[0]))
    load_weight(3, 0).start()
    take(n)
    for slot in range(2):
        load_kv(2 + slot, slot).wait()
    attention(1, False, [(1, 1), (5, 2)])
    for slot in range(2):
        load_kv(slot, slot).start()
        load_p(0, slot).start()
    load_weight(5, 1).wait()
    load_weight(6, 2).wait()
    sum_memory.begin(dot(r.w[1], r.dk_t[...]) + dot(r.w[2], r.dv_t[...]))
    load_weight(1, 1).start()
    load_weight(2, 2).start()
    load_t(r.enc_t, 0).wait()
    free(n + 1)
    fill(n + 1, dot_nt(r.rows_t[...], r.dk_t[...]))
    sum_memory.pass_x()
    free(n + 2)
    fill(n + 2, dot_nt(r.rows_t[...], r.dv_t[...]))
    take(n + 1)
    advance(3)
    load_t(r.tok_t, 1).start()
    d_query = joined_query()
    load_weight(4, 3).wait()
    back, d_gain2 = rms_back(r.first[...], gain(1), dot_nt(d_query, r.w[3]))
    load_weight(0, 3).start()
    free(n + 3)
    fill(n + 3, dot(r.normed2_t[...], d_query))
    take(n + 2)
    r.grad[...] = r.grad[...] + back
    advance(4)

    grad_low = r.grad[...].astype(BF16)
    take(n + 3)
    free(n + 4)
    fill(n + 4, dot(r.low_t[0], grad_low))
    load_weight(3, 0).wait()
    spread_grad(dot_nt(grad_low, r.w[0]))
    take(n + 4)
    for slot in range(2):
        load_kv(slot, slot).wait()
    attention(0, True, [(2, 5), (5, 6)])
    load_weight(1, 1).wait()
    load_weight(2, 2).wait()
    sum_memory.to_core().wait_send()
    sum_tokens.begin(dot(r.w[1], r.dk_t[...]) + dot(r.w[2], r.dv_t[...]))
    load_t(r.tok_t, 1).wait()
    free(n + 5)
    fill(n + 5, dot_nt(r.rows_t[...], r.dk_t[...]))
    sum_tokens.pass_x()
    free(n + 6)
    fill(n + 6, dot_nt(r.rows_t[...], r.dv_t[...]))
    take(n + 5)
    r.d_memory[...] = sum_memory.finish().T
    advance(7)
    d_query = joined_query()
    free(n + 7)
    mine = pl.ds(pl.multiple_of(place.shard * rows, LANES), rows)
    fill(n + 7, dot(r.rows_t[:, mine], d_query))
    take(n + 6)
    load_weight(0, 3).wait()
    r.acc[...] = dot_nt(d_query, r.w[3])
    windows = jnp.concatenate([r.d_window[i] for i in range(pairs)], axis=0)
    d_table = lax.dot_general(
        windows,
        bucket_onehot(r.buckets, place, rows, length),
        (((1,), (1,)), ((), ())),
        precision=lax.Precision.HIGHEST,
        preferred_element_type=F32,
    )
    take(n + 7)
    advance(8)
    values = r.tokens[...].astype(F32)
    back, d_gain1 = rms_back(values, gain(0), r.acc[...] + sum_tokens.finish().T)
    r.d_tokens[...] = r.grad[...] + back
    r.small_held[0] = jnp.zeros(r.small_held.shape[1:], F32)
    for i, d_gain in enumerate((d_gain1, d_gain2, d_gain3)):
        r.small_held[0, i : i + 1, :width] = d_gain
    r.small_held[0, 8 : 8 + 2 * pairs, :LANES] = d_table
    small.launch()
    for t in range(9, len(order) + stages):
        advance(t)
        if t < 14:
            small.step(t - 9)
    for n in range(units):
        move(n, stages)
    r.small_out[...] = r.small_held[5]
    for n in range(units):
        if n >= units - SLOTS:
            left(n)
        red, u = owner(n)
        red.sent(u)
    small.sent()
    sum_tokens.to_core().wait_send()
    sum_memory.sent()
    sum_tokens.sent()


def backward(tokens, cotangent, buckets, held, reps, shards):
    rows, width = tokens.shape
    length = held.enc_out.shape[1]
    nx, nh = shards // 2, reps // 4
    pairs = width // LANES
    q, half = width // shards, width // 2
    units = held.w_out.shape[0] // width
    small = (24, width)
    kept = pl.BlockSpec(memory_space=pl.ANY)
    near = pl.BlockSpec(memory_space=pltpu.VMEM)
    ins = dict(
        tokens=(near, tokens),
        cotangent=(near, cotangent),
        buckets=(near, buckets),
        gains=(near, held.small_out),
        first=(near, held.first_out),
        second=(near, held.second_out),
        low=(near, held.low_out),
        low_t=(near, held.low_t),
        queries=(near, held.q_out),
        normed2_t=(near, held.normed2_t),
        normed3_t=(near, held.normed3_t),
        hidden_t=(near, held.hidden_t),
        slope=(kept, held.slope_out),
        tok_t=(kept, held.tok_out),
        enc_t=(kept, held.enc_out),
        w_in=(kept, held.w_out),
        kv_in=(kept, held.kv_out),
        p_in=(kept, held.p_out),
    )
    outs = dict(
        d_tokens=(near, jax.ShapeDtypeStruct((rows, width), F32)),
        d_memory=(near, jax.ShapeDtypeStruct((rows, width), F32)),
        small_out=(near, jax.ShapeDtypeStruct(small, F32)),
        fin=(kept, jax.ShapeDtypeStruct((units, 2, q, half), BF16)),
    )
    scratch = dict(
        w=pltpu.VMEM((4, width, width), BF16),
        kv=pltpu.VMEM((2, pairs, length, LANES), BF16),
        probs=pltpu.VMEM((2, 2 * rows, length), BF16),
        ds=pltpu.VMEM((2 * rows, length), BF16),
        rows_t=pltpu.VMEM((width, length), BF16),
        dk_t=pltpu.VMEM((width, length), BF16),
        dv_t=pltpu.VMEM((width, length), BF16),
        d_query=pltpu.VMEM((pairs, rows, LANES), BF16),
        grad_att=pltpu.VMEM((pairs, rows, LANES), BF16),
        d_window=pltpu.VMEM((pairs, 2, length + rows), F32),
        acc=pltpu.VMEM((rows, width), F32),
        grad=pltpu.VMEM((rows, width), F32),
        made=pltpu.VMEM((SLOTS, 2, nx, 2, q, half), BF16),
        slopes=pltpu.VMEM((2, rows, width), F32),
        s_sem=pltpu.SemaphoreType.DMA((2,)),
        w_sem=pltpu.SemaphoreType.DMA((4,)),
        kv_sem=pltpu.SemaphoreType.DMA((2,)),
        p_sem=pltpu.SemaphoreType.DMA((2,)),
        t_sem=pltpu.SemaphoreType.DMA((2,)),
    )
    counts = {"a": units - len(late_units(units)), "b": len(late_units(units))}
    for name, count in counts.items():
        made_for = Reduction.scratch(count, name == "a", nx, nh, q, half)
        scratch.update(zip((name + end for end in REDUCTION), made_for))
    scratch.update(
        zip(("small_held", "small_landed", "small_send", "small_recv"), SmallSum.scratch(nx, nh, small))
    )
    for name in "mt":
        keys = (name + end for end in ("_parts", "_a", "_b", "_send", "_recv"))
        scratch.update(zip(keys, RowSum.scratch(nx, width, rows)))
    del scratch["t_parts"]
    names = tuple(list(ins) + list(outs) + list(scratch))
    made = pl.pallas_call(
        functools.partial(backward_kernel, reps, shards, names),
        in_specs=[spec for spec, _ in ins.values()],
        out_specs=[spec for spec, _ in outs.values()],
        out_shape=[shape for _, shape in outs.values()],
        scratch_shapes=list(scratch.values()),
        compiler_params=pltpu.CompilerParams(
            collective_id=3, has_side_effects=True, vmem_limit_bytes=FUSED_LIMIT
        ),
    )(*[value for _, value in ins.values()])
    return types.SimpleNamespace(**dict(zip(outs, made)))


def finish_kernel(squares, shards, names, *refs):
    r = types.SimpleNamespace(**dict(zip(names, refs)))
    step = pl.program_id(0)
    shard = lax.axis_index("shard")
    whole = lambda ref: jnp.concatenate([ref[0, 0], ref[0, 1]], axis=1).astype(F32)
    r.feed_in[...] = whole(r.fin_in)
    r.feed_out[...] = whole(r.fin_out)
    for source, group in zip((r.fin_cross, r.fin_self), squares):
        value = whole(source)
        for name, first, count in group:
            out = getattr(r, name)

            @pl.when((step >= first) & (step < first + count))
            def _():
                out[...] = value.reshape(out.shape)

    r.d_tokens[...] = r.tokens_in[...]
    r.d_memory[...] = r.memory_in[...]
    r.result[...] = r.result_in[...]

    @pl.when(step == 0)
    def _():
        small = r.small[...]
        width = small.shape[1]
        mine = lambda by: pltpu.roll(small, lax.rem(width - shard * by, width), 1)
        gains = mine(width // shards)
        for i, out in enumerate((r.norm_self, r.norm_cross, r.norm_feed)):
            out[...] = gains[i : i + 1, : width // shards].reshape(out.shape)
        cut, heads = r.bucket_bias.shape
        r.bucket_bias[...] = mine(cut)[8:24, :LANES].T[:cut, :heads]


def finish(made, result, table_shape, shards):
    units, _, q, half = made.fin.shape
    rows, width = made.d_tokens.shape
    steps = units // 4
    still = lambda *shape: pl.BlockSpec(shape, lambda n: (0,) * len(shape))
    line = pl.BlockSpec((rows // steps, width), lambda n: (n, 0))
    unit = lambda group: pl.BlockSpec((1, 2, q, half), lambda n: (group * steps + n, 0, 0, 0))
    pair = lambda first: pl.BlockSpec((1, q, width), lambda n: (jnp.where(n <= first, 0, 1), 0, 0))
    squares = (
        (("cross_output", 0, 1), ("cross_keyval", 1, 2), ("cross_query", 3, 1)),
        (("self_output", 0, 1), ("self_keyval", 1, 2), ("self_query", 3, 1)),
    )
    square = ((q, width), still(q, width))
    outs = dict(
        feed_in=((q, steps * width), pl.BlockSpec((q, width), lambda n: (0, n))),
        feed_out=((steps * q, width), pl.BlockSpec((q, width), lambda n: (n, 0))),
        cross_output=square,
        cross_keyval=((2, q, width), pair(1)),
        cross_query=square,
        self_output=square,
        self_keyval=((2, q, width), pair(1)),
        self_query=square,
        d_tokens=((rows, width), line),
        d_memory=((rows, width), line),
        result=((rows, width), line),
        norm_self=((q,), still(q)),
        norm_cross=((q,), still(q)),
        norm_feed=((q,), still(q)),
        bucket_bias=(table_shape, still(*table_shape)),
    )
    names = ("fin_in", "fin_out", "fin_cross", "fin_self", "tokens_in", "memory_in", "result_in", "small")
    done = pl.pallas_call(
        functools.partial(finish_kernel, squares, shards, names + tuple(outs)),
        grid=(steps,),
        in_specs=[unit(0), unit(1), unit(2), unit(3), line, line, line, still(*made.small_out.shape)],
        out_specs=[spec for _, spec in outs.values()],
        out_shape=[
            jax.ShapeDtypeStruct(shape, BF16 if name == "result" else F32)
            for name, (shape, _) in outs.items()
        ],
        compiler_params=pltpu.CompilerParams(vmem_limit_bytes=VMEM_LIMIT),
    )(*[made.fin] * 4, made.d_tokens, made.d_memory, result, made.small_out)
    return types.SimpleNamespace(**dict(zip(outs, done)))


def tiles_evenly(reps, shards, width):
    if reps % 4 or shards % 2 or width % shards:
        return False
    return (width // shards) % (8 * reps) == 0 and width % (4 * HD) == 0


def layer(
    tokens,
    encoded,
    block_ids,
    buckets,
    cotangent,
    norm_self,
    self_query,
    self_keyval,
    self_output,
    bucket_bias,
    norm_cross,
    cross_query,
    cross_keyval,
    cross_output,
    norm_feed,
    feed_in,
    feed_out,
):
    groups, positions, model_width = tokens.shape
    reps, shards = lax.axis_size("rep"), lax.axis_size("shard")
    length = (buckets.shape[0] + 1) // 2
    memory_local = encoded.shape[1]
    row_anchor = lax.axis_index("shard") * positions
    heads, bucket_count = bucket_bias.shape[0], bucket_bias.shape[1] * shards
    window_width = length + positions
    fused = tiles_evenly(reps, shards, model_width) and encoded.shape == tokens.shape
    fused = fused and feed_out.shape[0] == model_width
    fused = fused and feed_in.shape[1] == 4 * model_width and positions % LANES == 0
    if fused:
        offsets = jnp.pad(buckets, (1, 0))[None, :]
        gains = (norm_self, norm_cross, norm_feed)
        matrices = (self_query, self_keyval, self_output, cross_query, cross_keyval, cross_output)
        matrices += (feed_in, feed_out)
        held = forward(
            tokens[0], encoded[0], block_ids, offsets, gains, bucket_bias.T, matrices, reps, shards
        )
        made = backward(tokens[0], cotangent[0], offsets, held, reps, shards)
        out = finish(made, held.result, bucket_bias.T.shape, shards)
        return (
            out.result[None],
            out.d_tokens[None],
            out.d_memory[None],
            out.norm_self,
            out.self_query,
            out.self_keyval,
            out.self_output,
            out.bucket_bias.T,
            out.norm_cross,
            out.cross_query,
            out.cross_keyval,
            out.cross_output,
            out.norm_feed,
            out.feed_in,
            out.feed_out,
        )

    inputs = tokens[0].astype(F32)
    encoded_whole = gather(encoded[0])
    ids_whole = gather(block_ids[0])
    gains = gather(jnp.stack([norm_self, norm_cross, norm_feed]), 1).astype(F32)
    gain_first, gain_second, gain_third = gains[0:1], gains[1:2], gains[2:3]
    query_first, keyval_first, output_first, table = (
        gather(self_query),
        gather(self_keyval, 1),
        gather(self_output),
        gather(bucket_bias, 1),
    )
    query_second, keyval_second, output_second = (
        gather(cross_query),
        gather(cross_keyval, 1),
        gather(cross_output),
    )
    inner, outer = gather(feed_in), gather(feed_out)

    window_buckets = lax.dynamic_slice_in_dim(
        jnp.pad(buckets, (1, 0)), length - row_anchor - positions, window_width
    )
    onehot = window_buckets[None, :] == jnp.arange(bucket_count, dtype=jnp.int32)[:, None]
    window = dot(table, onehot.astype(BF16)).reshape(heads // 2, 2, window_width)

    normed_first = (inputs * rms_scale(inputs) * gain_first).astype(BF16)
    normed_whole = gather(normed_first)
    query = dot(normed_first, query_first).astype(BF16)
    keys = dot(normed_whole, keyval_first[0]).astype(BF16)
    values = dot(normed_whole, keyval_first[1]).astype(BF16)
    attended, weights = attend(
        query, keys, values, (block_ids[0][:, None], ids_whole[None, :], window)
    )
    low_first = attended.astype(BF16)
    first = inputs + dot(low_first, output_first)

    memory_keys = dot(encoded_whole, keyval_second[0]).astype(BF16)
    memory_values = dot(encoded_whole, keyval_second[1]).astype(BF16)
    normed_second = (first * rms_scale(first) * gain_second).astype(BF16)
    query_cross = dot(normed_second, query_second).astype(BF16)
    attended_cross, weights_cross = attend(query_cross, memory_keys, memory_values)
    low_second = attended_cross.astype(BF16)
    second = first + dot(low_second, output_second)

    normed_third = (second * rms_scale(second) * gain_third).astype(BF16)
    preact = dot(normed_third, inner)
    value, slope = gelu_parts(preact)
    hidden = value.astype(BF16)
    result = (second + dot(hidden, outer)).astype(BF16)

    grad_result = cotangent[0]
    d_outer = dot_tn(hidden, grad_result)
    grad_preact = (dot_nt(grad_result, outer) * slope).astype(BF16)
    d_inner = dot_tn(normed_third, grad_preact)
    back, d_gain_third = rms_back(second, gain_third, dot_nt(grad_preact, inner))
    grad_second = grad_result.astype(F32) + back

    grad_second_low = grad_second.astype(BF16)
    d_output_second = dot_tn(low_second, grad_second_low)
    grad_att = dot_nt(grad_second_low, output_second).astype(BF16)
    d_query, d_keys, d_values = attend_back(
        query_cross, memory_keys, memory_values, weights_cross, attended_cross, grad_att
    )
    d_keyval_second = jnp.stack(
        [dot_tn(encoded_whole, d_keys), dot_tn(encoded_whole, d_values)]
    )
    d_memory = scatter(dot_nt(d_keys, keyval_second[0]) + dot_nt(d_values, keyval_second[1]))
    d_query_second = dot_tn(normed_second, d_query)
    back, d_gain_second = rms_back(first, gain_second, dot_nt(d_query, query_second))
    grad_first = grad_second + back

    grad_first_low = grad_first.astype(BF16)
    d_output_first = dot_tn(low_first, grad_first_low)
    grad_att = dot_nt(grad_first_low, output_first).astype(BF16)
    d_query, d_keys, d_values, d_window = attend_back(
        query, keys, values, weights, attended, grad_att, window.shape
    )
    d_table = lax.dot_general(
        d_window.reshape(heads, window_width),
        onehot.astype(F32),
        (((1,), (1,)), ((), ())),
        precision=lax.Precision.HIGHEST,
    )
    d_keyval_first = jnp.stack([dot_tn(normed_whole, d_keys), dot_tn(normed_whole, d_values)])
    grad_normed = scatter(
        dot_nt(d_keys, keyval_first[0]) + dot_nt(d_values, keyval_first[1])
    ).astype(F32) + dot_nt(d_query, query_first)
    d_query_first = dot_tn(normed_first, d_query)
    back, d_gain_first = rms_back(inputs, gain_first, grad_normed)
    d_inputs = grad_first + back

    gains = [d_gain_first, d_gain_second, d_gain_third]
    squares = [d_query_first, d_output_first, d_query_second, d_output_second]
    pairs = [d_keyval_first, d_keyval_second]
    total = lambda a, axis=0: lax.psum(scatter(a, axis), "rep").astype(F32)
    gains = [total(gain[0]) for gain in gains]
    squares = [total(square) for square in squares]
    pairs = [total(pair, 1) for pair in pairs]
    d_table, d_inner, d_outer = total(d_table, 1), total(d_inner), total(d_outer)
    totals = (gains[0], squares[0], pairs[0], squares[1], d_table)
    totals += (gains[1], squares[2], pairs[1], squares[3], gains[2], d_inner, d_outer)
    return (result[None], d_inputs[None], d_memory.astype(F32)[None]) + totals


def solution(mesh):
    rows, line = P("rep", "shard", None), P("shard")
    matrix, pair, table = P("shard", None), P(None, "shard", None), P(None, "shard")
    weights = (line, matrix, pair, matrix, table, line, matrix, pair, matrix, line, matrix, matrix)
    return jax.shard_map(
        layer,
        mesh=mesh,
        in_specs=(rows, rows, P("rep", "shard"), P(), rows) + weights,
        out_specs=(rows, rows, rows) + weights,
        check_vma=False,
    )
```

```python
import functools
import types

import jax
import jax.numpy as jnp
from jax import lax
from jax.experimental import pallas as pl
from jax.experimental.pallas import tpu as pltpu
from jax.sharding import PartitionSpec as P

H = 12
HD = 64
LANES = 2 * HD
EPSILON = 1e-06
MASKED = -1e30
F32 = jnp.float32
BF16 = jnp.bfloat16
VMEM_LIMIT = 56 * 2**20
FUSED_LIMIT = 62 * 2**20
AHEAD = 2
AHEAD_BUSY = 2
LAST_SUM = 12
TICKS = {0: 1, 2: 2, 6: 3, 7: 4, 8: 5, 11: 6, 14: 7, 15: 8, 16: 9}
LINE = 3
SELF_PUMPS = ((1, 6), (3, 7), (5, 8))
CROSS_PUMPS = ((1, 12), (3, 13), (5, 14))
QUARTERS = (0, 1, 2, 3)
LATE = (1, 3)
LATE_START = (-1, 1)
SLOTS = 4
LAG = 1
MESH = pl.DeviceIdType.MESH


def dot(a, b):
    return lax.dot_general(a, b, (((1,), (0,)), ((), ())), preferred_element_type=F32)


def dot_nt(a, b):
    return lax.dot_general(a, b, (((1,), (1,)), ((), ())), preferred_element_type=F32)


def dot_tn(a, b):
    return lax.dot_general(a, b, (((0,), (0,)), ((), ())), preferred_element_type=F32)


def rms_scale(values):
    return lax.rsqrt(jnp.mean(values * values, axis=-1, keepdims=True) + EPSILON)


def rms_back(values, gain, grad):
    scale = rms_scale(values)
    scaled = gain * grad
    mean = jnp.mean(scaled * values, axis=-1, keepdims=True)
    d_values = scale * scaled - values * (scale * scale * scale) * mean
    d_gain = jnp.sum(grad * values * scale, axis=0, keepdims=True)
    return d_values, d_gain


def gelu_parts(x):
    c = 0.7978845608028654
    t = jnp.tanh(c * (x + 0.044715 * (x * x * x)))
    value = 0.5 * x * (1.0 + t)
    slope = 0.5 * (1.0 + t) + 0.5 * x * (1.0 - t * t) * (c * (1.0 + 3.0 * 0.044715 * (x * x)))
    return value, slope


def own_lanes(first):
    lane = lax.broadcasted_iota(jnp.int32, (1, LANES), 1)
    mine = (lane < HD) if first else (lane >= HD)
    return jnp.where(mine, 1.0, 0.0)


def stack_heads(pair):
    one, two = own_lanes(True).astype(pair.dtype), own_lanes(False).astype(pair.dtype)
    return jnp.concatenate([pair * one, pair * two], axis=0)


def merge_heads(stacked):
    rows = stacked.shape[0] // 2
    return stacked[:rows] * own_lanes(True) + stacked[rows:] * own_lanes(False)


def skew(window, width):
    sub = lax.broadcasted_iota(jnp.int32, (8, width), 0)
    rows = jnp.broadcast_to(window, (8, width))
    for bit in (1, 2, 4):
        rows = jnp.where((sub & bit) != 0, pltpu.roll(rows, bit, 1), rows)
    return jnp.concatenate(
        [pltpu.roll(rows, (8 * g + width - 128) % width, 1) for g in range(16)], axis=0
    )


def unskew(total, width):
    sub = lax.broadcasted_iota(jnp.int32, (8, width), 0)
    rows = jnp.zeros((8, width), F32)
    for g in range(16):
        rows = rows + pltpu.roll(total[8 * g : 8 * g + 8], 128 - 8 * g, 1)
    for bit in (1, 2, 4):
        rows = jnp.where((sub & bit) != 0, pltpu.roll(rows, width - bit, 1), rows)
    return jnp.sum(rows, axis=0, keepdims=True)


def attend_kernel(biased, q_ref, k_ref, v_ref, *refs):
    if biased:
        row_ids, key_ids, window_ref, out_ref, p_ref = refs
    else:
        out_ref, p_ref = refs
    rows, length = q_ref.shape[0], k_ref.shape[0]
    blocks = rows // 128
    scores = dot_nt(stack_heads(q_ref[...]), k_ref[...])
    for head in range(2):
        if biased:
            width = window_ref.shape[2]
            table = skew(window_ref[0, head : head + 1, :], width)
        for b in range(blocks):
            at = head * rows + b * 128
            part = scores[at : at + 128]
            if biased:
                shift = (blocks - 1 - b) * 128
                allowed = key_ids[...] <= row_ids[b * 128 : b * 128 + 128, :]
                part = jnp.where(allowed, part + table[:, shift : shift + length], MASKED)
            top = jnp.max(part, axis=-1, keepdims=True)
            raised = jnp.exp(part - top)
            share = 1.0 / jnp.sum(raised, axis=-1, keepdims=True)
            p_ref[0, at : at + 128, :] = (raised * share).astype(BF16)
    out_ref[...] = merge_heads(dot(p_ref[0], v_ref[...]))


def attend_back_kernel(folded, q_ref, k_ref, v_ref, p_ref, out_ref, grad_ref, *refs):
    if folded:
        dq_ref, dk_ref, dv_ref, window_ref, ds_ref = refs
    else:
        dq_ref, dk_ref, dv_ref, ds_ref = refs
    rows, length = q_ref.shape[0], k_ref.shape[0]
    blocks = rows // 128
    grad = grad_ref[...]
    grads = stack_heads(grad)
    delta_wide = grad.astype(F32) * out_ref[...]
    d_weights = dot_nt(grads, v_ref[...])
    for head in range(2):
        if folded:
            width = window_ref.shape[2]
            total = jnp.zeros((128, width), F32)
        delta = jnp.sum(delta_wide * own_lanes(head == 0), axis=-1, keepdims=True)
        for b in range(blocks):
            at = head * rows + b * 128
            part = p_ref[0, at : at + 128, :].astype(F32) * (
                d_weights[at : at + 128] - delta[b * 128 : b * 128 + 128]
            )
            ds_ref[at : at + 128, :] = part.astype(BF16)
            if folded:
                shift = (blocks - 1 - b) * 128
                pieces = [part]
                if shift:
                    pieces = [jnp.zeros((128, shift), F32)] + pieces
                if width - shift - length:
                    pieces = pieces + [jnp.zeros((128, width - shift - length), F32)]
                total = total + jnp.concatenate(pieces, axis=1)
        if folded:
            window_ref[0, head : head + 1, :] = unskew(total, width)
    queries = stack_heads(q_ref[...])
    dq_ref[...] = merge_heads(dot(ds_ref[...], k_ref[...])).astype(BF16)
    dk_ref[...] = dot(queries.T, ds_ref[...]).T.astype(BF16)
    dv_ref[...] = dot(grads.T, p_ref[0]).T.astype(BF16)


def attend(query, keys, values, bias=None):
    rows, width = query.shape
    length = keys.shape[0]
    pairs = width // LANES
    column = lambda n: pl.BlockSpec((n, LANES), lambda i: (0, i))
    whole = lambda a: pl.BlockSpec(a.shape, lambda i: (0,) * a.ndim)
    operands, specs = [query, keys, values], [column(rows), column(length), column(length)]
    if bias is not None:
        row_ids, key_ids, window = bias
        operands += [row_ids, key_ids, window]
        specs += [
            whole(row_ids),
            whole(key_ids),
            pl.BlockSpec((1,) + window.shape[1:], lambda i: (i, 0, 0)),
        ]
    return pl.pallas_call(
        functools.partial(attend_kernel, bias is not None),
        grid=(pairs,),
        in_specs=specs,
        out_specs=[
            column(rows),
            pl.BlockSpec((1, 2 * rows, length), lambda i: (i, 0, 0)),
        ],
        out_shape=[
            jax.ShapeDtypeStruct((rows, width), F32),
            jax.ShapeDtypeStruct((pairs, 2 * rows, length), BF16),
        ],
        compiler_params=pltpu.CompilerParams(vmem_limit_bytes=VMEM_LIMIT),
        cost_estimate=pl.CostEstimate(
            flops=16 * rows * length * width,
            bytes_accessed=2 * pairs * 2 * rows * length,
            transcendentals=pairs * 2 * rows * length,
        ),
    )(*operands)


def attend_back(query, keys, values, weights, output, grad, window_shape=None):
    rows, width = query.shape
    length = keys.shape[0]
    pairs = width // LANES
    column = lambda n: pl.BlockSpec((n, LANES), lambda i: (0, i))
    out_specs = [column(rows), column(length), column(length)]
    out_shape = [
        jax.ShapeDtypeStruct((rows, width), BF16),
        jax.ShapeDtypeStruct((length, width), BF16),
        jax.ShapeDtypeStruct((length, width), BF16),
    ]
    if window_shape is not None:
        out_specs.append(pl.BlockSpec((1,) + window_shape[1:], lambda i: (i, 0, 0)))
        out_shape.append(jax.ShapeDtypeStruct(window_shape, F32))
    return pl.pallas_call(
        functools.partial(attend_back_kernel, window_shape is not None),
        grid=(pairs,),
        in_specs=[
            column(rows),
            column(length),
            column(length),
            pl.BlockSpec((1, 2 * rows, length), lambda i: (i, 0, 0)),
            column(rows),
            column(rows),
        ],
        out_specs=out_specs,
        out_shape=out_shape,
        scratch_shapes=[pltpu.VMEM((2 * rows, length), BF16)],
        compiler_params=pltpu.CompilerParams(vmem_limit_bytes=VMEM_LIMIT),
        cost_estimate=pl.CostEstimate(
            flops=32 * rows * length * width,
            bytes_accessed=2 * pairs * 2 * rows * length,
            transcendentals=0,
        ),
    )(query, keys, values, weights, output, grad)


def gather(values, axis=0):
    return lax.all_gather(values, "shard", axis=axis, tiled=True)


def scatter(values, axis=0):
    return lax.psum_scatter(values.astype(BF16), "shard", scatter_dimension=axis, tiled=True)


class Place:
    def __init__(self, reps, shards):
        self.nx, self.nh = shards // 2, reps // 4
        rep, shard = lax.axis_index("rep"), lax.axis_index("shard")
        self.rep, self.shard = rep, shard
        self.core, self.x = lax.rem(shard, 2), lax.div(shard, 2)
        self.y, z = lax.rem(rep, 2), lax.div(rep, 2)
        self.low, self.high = lax.rem(z, 2), lax.div(z, 2)

    def other_core(self):
        return (self.rep, self.x * 2 + 1 - self.core)

    def x_at(self, step):
        x = lax.rem(self.x + step, self.nx)
        return x, (self.rep, x * 2 + self.core)

    def other_y(self):
        return (self.rep + 1 - 2 * self.y, self.shard)

    def other_low(self):
        return (self.rep + 2 - 4 * self.low, self.shard)

    def high_at(self, step):
        high = lax.rem(self.high + step, self.nh)
        return high, (high * 4 + self.low * 2 + self.y, self.shard)

    def partners(self):
        found = [self.other_core(), self.other_y(), self.other_low()]
        found += [self.x_at(d)[1] for d in range(1, self.nx)]
        found += [self.high_at(d)[1] for d in range(1, self.nh)]
        return found


def enter(place):
    barrier = pltpu.get_barrier_semaphore()
    partners = place.partners()
    for device in partners:
        pl.semaphore_signal(barrier, inc=1, device_id=device, device_id_type=MESH)
    pl.semaphore_wait(barrier, len(partners))


def remote(src, dst, send, recv, device):
    return pltpu.make_async_remote_copy(
        src_ref=src, dst_ref=dst, send_sem=send, recv_sem=recv, device_id=device, device_id_type=MESH
    )


def added(*parts):
    if len(parts) == 2:
        return parts[0] + parts[1]
    total = parts[0].astype(F32)
    for part in parts[1:]:
        total = total + part.astype(F32)
    return total


class Reduction:
    def __init__(self, place, x_first, names, fin, parts, recv_x, recv_y, recv_low, recv_high, send, recv, own_sem):
        self.place, self.x_first, self.parts, self.fin = place, x_first, parts, fin
        self.names = names
        self.recv_x, self.recv_y, self.recv_low, self.recv_high = recv_x, recv_y, recv_low, recv_high
        self.send, self.recv, self.own_sem = send, recv, own_sem
        self.half = parts.shape[3] // 2
        self.rows = self.half // place.nh
        stages = [self.over_y, self.over_low, self.over_high]
        stages = [self.over_x] + stages if x_first else stages + [self.over_x]
        stages += [self.back_high, self.back_low, self.back_y]
        self.copies = stages
        self.adds = stages.index(self.back_high)

    @staticmethod
    def scratch(n, x_first, nx, nh, q, half):
        copies = 4 + nx + 2 * (nh - 1)
        wide = (n,) if x_first else (n, nx)
        x_part = (2, q) if x_first else (q // (2 * nh),)
        return [
            pltpu.VMEM((n, nx, 2, q, half), BF16),
            pltpu.VMEM((n, nx - 1) + x_part + (half,), BF16),
            pltpu.VMEM(wide + (q, half), BF16),
            pltpu.VMEM(wide + (q // 2, half), BF16),
            pltpu.VMEM((n, nh - 1) + wide[1:] + (q // (2 * nh), half), BF16),
            pltpu.SemaphoreType.DMA((n, copies)),
            pltpu.SemaphoreType.DMA((n, copies)),
            pltpu.SemaphoreType.DMA((n,)),
        ]

    def copy(self, u, which, src, dst, device):
        return remote(src, dst, self.send.at[u, which], self.recv.at[u, which], device)

    def low_rows(self, low):
        return pl.ds(pl.multiple_of(low * self.half, 16), self.half)

    def high_rows(self, high):
        at = self.place.low * self.half + high * self.rows
        return pl.ds(pl.multiple_of(at, 16), self.rows)

    def chips(self):
        return self.place.x if self.x_first else slice(None)

    def over_core(self, u, src):
        return [self.copy(u, 0, src, self.parts.at[u], self.place.other_core())]

    def over_x(self, u):
        p, out = self.place, []
        rest = () if self.x_first else (p.y, self.high_rows(p.high))
        for d in range(1, p.nx):
            x, device = p.x_at(d)
            src = self.parts.at[(u, x) + rest]
            out.append(self.copy(u, 2 + d, src, self.recv_x.at[u, d - 1], device))
        return out, (u, p.x) + rest, [self.recv_x.at[u, d] for d in range(p.nx - 1)]

    def over_y(self, u):
        p, chips = self.place, self.chips()
        src = self.parts.at[u, chips, 1 - p.y]
        copies = [self.copy(u, 1, src, self.recv_y.at[u], p.other_y())]
        return copies, (u, chips, p.y), [self.recv_y.at[u]]

    def over_low(self, u):
        p, chips = self.place, self.chips()
        src = self.parts.at[u, chips, p.y, self.low_rows(1 - p.low)]
        copies = [self.copy(u, 2 + p.nx, src, self.recv_low.at[u], p.other_low())]
        return copies, (u, chips, p.y, self.low_rows(p.low)), [self.recv_low.at[u]]

    def over_high(self, u):
        p, chips, out = self.place, self.chips(), []
        for d in range(1, p.nh):
            high, device = p.high_at(d)
            src = self.parts.at[u, chips, p.y, self.high_rows(high)]
            out.append(self.copy(u, 3 + p.nx + d, src, self.recv_high.at[u, d - 1], device))
        came = [self.recv_high.at[u, d] for d in range(p.nh - 1)]
        return out, (u, chips, p.y, self.high_rows(p.high)), came

    def piece(self, u):
        p = self.place
        rows = self.high_rows(p.high)
        return self.parts.at[u, p.x, p.y, rows], self.fin.at[self.names[u], p.y, rows]

    def keep(self, u):
        return pltpu.make_async_copy(*self.piece(u), self.own_sem.at[u])

    def back_high(self, u):
        p = self.place
        return [
            self.copy(u, 2 + p.nx + p.nh + d, *self.piece(u), p.high_at(d)[1])
            for d in range(1, p.nh)
        ]

    def back_low(self, u):
        p = self.place
        rows = self.fin.at[self.names[u], p.y, self.low_rows(p.low)]
        return [self.copy(u, 3 + p.nx, rows, rows, p.other_low())]

    def back_y(self, u):
        half = self.fin.at[self.names[u], self.place.y]
        return [self.copy(u, 2, half, half, self.place.other_y())]

    def begin(self, u, src):
        self.over_core(u, src)[0].start()

    def collect(self, u, src, own):
        self.over_core(u, src)[0].wait_recv()
        self.parts[u] = added(self.parts[u], own[...]).astype(BF16)

    def start(self, u, stage):
        if stage < len(self.copies):
            copies = self.copies[stage](u)
            for copy in copies[0] if stage < self.adds else copies:
                copy.start()

    def step(self, u, stage):
        if stage < self.adds:
            copies, stays, came = self.copies[stage](u)
            for copy in copies:
                copy.wait_recv()
            total = added(self.parts[stays], *[part[...] for part in came])
            self.parts[stays] = total.astype(BF16)
            if stage + 1 == self.adds:
                self.keep(u).start()
        else:
            for copy in self.copies[stage](u):
                copy.wait_recv()
            if stage == self.adds:
                self.keep(u).wait()
        self.start(u, stage + 1)

    def sent(self, u):
        for stage in range(len(self.copies)):
            copies = self.copies[stage](u)
            for copy in copies[0] if stage < self.adds else copies:
                copy.wait_send()


class SmallSum:
    def __init__(self, place, held, landed, send, recv):
        self.place, self.held, self.landed = place, held, landed
        self.send, self.recv = send, recv

    @staticmethod
    def scratch(nx, nh, shape):
        copies = 3 + nx - 1 + nh - 1
        return [
            pltpu.VMEM((6,) + shape, F32),
            pltpu.VMEM((copies,) + shape, F32),
            pltpu.SemaphoreType.DMA((copies,)),
            pltpu.SemaphoreType.DMA((copies,)),
        ]

    def copies(self, stage):
        p = self.place
        first, devices = [
            (0, [p.other_core()]),
            (3, [p.x_at(d)[1] for d in range(1, p.nx)]),
            (1, [p.other_y()]),
            (2, [p.other_low()]),
            (2 + p.nx, [p.high_at(d)[1] for d in range(1, p.nh)]),
        ][stage]
        return [
            remote(self.held.at[stage], self.landed.at[first + i], self.send.at[first + i], self.recv.at[first + i], device)
            for i, device in enumerate(devices)
        ], list(range(first, first + len(devices)))

    def begin(self, value):
        self.held[0] = value
        self.launch()

    def launch(self):
        for copy in self.copies(0)[0]:
            copy.start()

    def step(self, stage, stages=5):
        copies, slots = self.copies(stage)
        for copy in copies:
            copy.wait_recv()
        total = self.held[stage]
        for slot in slots:
            total = total + self.landed[slot]
        self.held[stage + 1] = total
        if stage + 1 < stages:
            for copy in self.copies(stage + 1)[0]:
                copy.start()
        return total

    def sent(self, stages=5):
        for stage in range(stages):
            for copy in self.copies(stage)[0]:
                copy.wait_send()


class Gather:
    def __init__(self, place, whole, own, hidden_rows, send, recv, own_sem):
        self.place, self.whole, self.own = place, whole, own
        self.send, self.recv, self.own_sem = send, recv, own_sem
        self.width = whole.shape[1]
        self.q = self.width // (2 * place.nx)
        self.square = len(own) - hidden_rows // self.q
        self.hidden_rows = hidden_rows

    @staticmethod
    def scratch(units, nx):
        copies = 1 + 8 * (nx - 1)
        return [
            pltpu.SemaphoreType.DMA((units, copies)),
            pltpu.SemaphoreType.DMA((units, copies)),
            pltpu.SemaphoreType.DMA((units,)),
        ]

    def cut(self, u, far_first, far_second=False):
        p = self.place
        first, second = (p.y, p.low) if u % 2 == 0 else (p.low, p.y)
        first = 1 - first if far_first else first
        second = 1 - second if far_second else second
        if u not in QUARTERS:
            return first * (self.q // 2)
        return (first * 2 + second) * (self.q // 4)

    def size(self, u):
        return self.q // 4 if u in QUARTERS else self.q // 2

    def first(self, u):
        return self.place.other_y() if u % 2 == 0 else self.place.other_low()

    def second(self, u):
        return self.place.other_low() if u % 2 == 0 else self.place.other_y()

    def part(self, u, shard, at=None):
        if u >= self.square:
            start = self.square * self.width + shard * self.hidden_rows
            start = start + (u - self.square) * self.q
        else:
            start = u * self.width + shard * self.q
        if at is None:
            return self.whole.at[pl.ds(pl.multiple_of(start, 16), self.q)]
        return self.whole.at[pl.ds(pl.multiple_of(start + at, 16), self.size(u))]

    def came(self, d):
        p = self.place
        return lax.rem(p.x + p.nx - d, p.nx) * 2 + p.core

    def copy(self, u, which, src, dst, device):
        return remote(src, dst, self.send.at[u, which], self.recv.at[u, which], device)

    def to_core(self, u):
        shard = self.place.shard
        return self.copy(u, 0, self.own[u], self.part(u, shard), self.place.other_core())

    def keep(self, u):
        return pltpu.make_async_copy(
            self.own[u], self.part(u, self.place.shard), self.own_sem.at[u]
        )

    def over_x(self, u, d):
        p = self.place
        at = self.cut(u, False)
        src = self.own[u].at[pl.ds(pl.multiple_of(at, 16), self.size(u))]
        return self.copy(u, 8 * d - 7, src, self.part(u, p.shard, at), p.x_at(d)[1])

    def on(self, u, d, which, far_first, far_second, device):
        here = self.part(u, self.came(d), self.cut(u, far_first, far_second))
        return self.copy(u, 8 * d - 7 + which, here, here, device)

    def onward(self, u, d, which):
        core, first, second = self.place.other_core(), self.first(u), self.second(u)
        far_first, far_second, device = (
            (False, False, first),
            (False, False, second),
            (False, False, core),
            (False, True, first),
            (False, True, core),
            (True, False, core),
            (True, True, core),
        )[which]
        return self.on(u, d, which + 1, far_first, far_second, device)

    def issue(self, u):
        for d in range(1, self.place.nx):
            self.over_x(u, d).start()
        self.to_core(u).start()
        self.keep(u).start()

    def relay_x(self, u):
        for d in range(1, self.place.nx):
            self.over_x(u, d).wait_recv()
            for which in (0, 1, 2) if u in QUARTERS else (0, 2):
                self.onward(u, d, which).start()

    def relay_second(self, u):
        for d in range(1, self.place.nx if u in QUARTERS else 1):
            self.onward(u, d, 1).wait_recv()
            self.onward(u, d, 3).start()
            self.onward(u, d, 4).start()

    def relay_first(self, u):
        for d in range(1, self.place.nx):
            self.onward(u, d, 0).wait_recv()
            self.onward(u, d, 5).start()
            if u in QUARTERS:
                self.onward(u, d, 3).wait_recv()
                self.onward(u, d, 6).start()

    def ready(self, u):
        self.keep(u).wait()
        self.to_core(u).wait_recv()
        for d in range(1, self.place.nx):
            for which in (2, 4, 5, 6) if u in QUARTERS else (2, 5):
                self.onward(u, d, which).wait_recv()

    def sent(self, u):
        self.to_core(u).wait_send()
        for d in range(1, self.place.nx):
            self.over_x(u, d).wait_send()
            for which in range(7) if u in QUARTERS else (0, 2, 5):
                self.onward(u, d, which).wait_send()


class Spread:
    def __init__(self, place, own, whole, send, recv, own_sem):
        self.place, self.own, self.whole = place, own, whole
        self.send, self.recv, self.own_sem = send, recv, own_sem
        self.count = own.shape[0]

    @staticmethod
    def scratch(nx):
        copies = 1 + 2 * (nx - 1)
        return [
            pltpu.SemaphoreType.DMA((copies,)),
            pltpu.SemaphoreType.DMA((copies,)),
            pltpu.SemaphoreType.DMA(()),
        ]

    def part(self, shard):
        return self.whole.at[pl.ds(pl.multiple_of(shard * self.count, 16), self.count)]

    def copy(self, which, src, dst, device):
        return remote(src, dst, self.send.at[which], self.recv.at[which], device)

    def to_core(self):
        return self.copy(0, self.own, self.part(self.place.shard), self.place.other_core())

    def over_x(self, d):
        p = self.place
        return self.copy(2 * d - 1, self.own, self.part(p.shard), p.x_at(d)[1])

    def on_core(self, d):
        p = self.place
        here = self.part(lax.rem(p.x + p.nx - d, p.nx) * 2 + p.core)
        return self.copy(2 * d, here, here, p.other_core())

    def keep(self):
        return pltpu.make_async_copy(self.own, self.part(self.place.shard), self.own_sem)

    def issue(self):
        for d in range(1, self.place.nx):
            self.over_x(d).start()
        self.to_core().start()
        self.keep().start()

    def relay_x(self):
        for d in range(1, self.place.nx):
            self.over_x(d).wait_recv()
            self.on_core(d).start()

    def ready(self):
        self.keep().wait()
        self.to_core().wait_recv()
        for d in range(1, self.place.nx):
            self.on_core(d).wait_recv()

    def sent(self):
        self.to_core().wait_send()
        for d in range(1, self.place.nx):
            self.over_x(d).wait_send()
            self.on_core(d).wait_send()


def attend_pair(query, keys, values_ref, p_ref, bias=None):
    rows, length = query.shape[0], keys.shape[0]
    blocks = rows // 128
    scores = dot_nt(stack_heads(query), keys)
    for head in range(2):
        if bias is not None:
            row_ids, key_ids, window = bias
            table = skew(window[head : head + 1], window.shape[1])
        for b in range(blocks):
            at = head * rows + b * 128
            part = scores[at : at + 128]
            if bias is not None:
                shift = (blocks - 1 - b) * 128
                allowed = key_ids <= row_ids[b * 128 : b * 128 + 128]
                part = jnp.where(allowed, part + table[:, shift : shift + length], MASKED)
            top = jnp.max(part, axis=-1, keepdims=True)
            raised = jnp.exp(part - top)
            share = 1.0 / jnp.sum(raised, axis=-1, keepdims=True)
            p_ref[at : at + 128, :] = (raised * share).astype(BF16)
    return merge_heads(dot(p_ref[...], values_ref[...]))


def bucket_onehot(buckets_ref, place, rows, length):
    start = length - rows - place.shard * rows
    window = buckets_ref[:, pl.ds(pl.multiple_of(start, LANES), length + rows)]
    which = lax.broadcasted_iota(jnp.int32, (LANES, length + rows), 0)
    return jnp.where(window == which, 1.0, 0.0)


def forward_kernel(reps, shards, names, *refs):
    r = types.SimpleNamespace(**dict(zip(names, refs)))
    place = Place(reps, shards)
    rows, width = r.tok_in.shape
    length = r.tok.shape[0]
    pairs = width // LANES
    q = width // shards
    part = r.feed_in.shape[1] // width
    own = [r.self_query, r.self_keyval.at[0], r.self_keyval.at[1], r.self_output]
    own += [r.cross_query, r.cross_keyval.at[0], r.cross_keyval.at[1], r.cross_output]
    own += [r.feed_in.at[:, pl.ds(j * width, width)] for j in range(part)]
    own += [r.feed_out.at[pl.ds(j * q, q)] for j in range(part)]
    units = len(own)
    small = SmallSum(place, r.small_held, r.small_landed, r.small_send, r.small_recv)
    gather = Gather(place, r.whole, own, r.feed_out.shape[0], r.w_send, r.w_recv, r.w_own)
    tokens = Spread(place, r.tok_in, r.tok, r.t_send, r.t_recv, r.t_own)
    memories = Spread(place, r.enc_in, r.enc, r.e_send, r.e_recv, r.e_own)

    def weight(u):
        return r.whole[pl.ds(pl.multiple_of(u * width, width), width), :]

    def emit_weights(u, count):
        block = pl.ds(u * width, count * width)
        return pltpu.make_async_copy(r.whole.at[block], r.w_out.at[block], r.out_sem.at[u])

    def emit_kv(i):
        return pltpu.make_async_copy(r.kv.at[i], r.kv_out.at[i], r.out_sem.at[units + i])

    leaving = []

    def emit(src, dst):
        copy = pltpu.make_async_copy(src, dst, r.emit_sem.at[len(leaving)])
        copy.start()
        leaving.append(copy)

    emit_tok = pltpu.make_async_copy(r.tok_t, r.tok_out, r.out_sem.at[units + 4])
    emit_enc = pltpu.make_async_copy(r.enc_t, r.enc_out, r.out_sem.at[units + 5])

    def emit_p(which, i):
        slot = lax.rem(i, 2)
        return pltpu.make_async_copy(r.probs.at[slot], r.p_out.at[which, i], r.p_sem.at[slot])

    def gain(i):
        return r.small_held[2, i : i + 1, :width]

    shard = place.shard
    wide = r.small_held.shape[2]
    sub = lax.broadcasted_iota(jnp.int32, (8, wide), 0)
    padded = lambda a: jnp.concatenate([a, jnp.zeros((a.shape[0], wide - a.shape[1]), F32)], axis=1)
    shifted = lambda a, by: pltpu.roll(padded(a), shard * by, 1)
    ids = r.ids[...].astype(F32)
    gains = [gain_ref[...].astype(F32).reshape(1, q) for gain_ref in (r.norm_self, r.norm_cross, r.norm_feed)]
    mine = jnp.concatenate(gains + [jnp.zeros((5, q), F32)], axis=0)
    mine = jnp.where(sub == 3, 0.0, shifted(mine, q))
    mine = mine + jnp.where(sub == 3, shifted(jnp.broadcast_to(ids, (8, rows)), rows), 0.0)
    table = r.bucket_bias[...].astype(F32).T
    heads, cut = table.shape
    table = jnp.concatenate([table, jnp.zeros((16 - heads, cut), F32)], axis=0)
    r.small_held[0] = jnp.concatenate([mine, shifted(table, cut)], axis=0)
    r.row_ids[...] = jnp.broadcast_to(ids, (8, rows)).T[:, 0:1]
    enter(place)
    small.launch()
    line = [(gather, (u,)) for u in (1, 2, 0, 3)] + [(tokens, ())]
    line += [(gather, (u,)) for u in (5, 6)] + [(memories, ())]
    line += [(gather, (u,)) for u in [4, 7] + list(range(8, units))]
    pumped = [0]
    steps = ("relay_x", "relay_second", "relay_first")

    def issue(at):
        if at < len(line):
            line[at][0].issue(*line[at][1])

    def pump(at):
        for late, name in enumerate(steps):
            if 0 <= at - late < len(line):
                owner, u = line[at - late]
                if hasattr(owner, name):
                    getattr(owner, name)(*u)
            if late == 0:
                issue(at + LINE)

    def pump_to(end):
        while pumped[0] < end:
            pump(pumped[0])
            pumped[0] += 1

    def have(*wanted):
        last = max(line.index((gather, (u,))) for u in wanted)
        pump_to(last + len(steps))
        for u in wanted:
            gather.ready(u)

    for at in range(LINE):
        issue(at)
    small.step(0, 2)
    gathered = small.step(1, 2)
    r.small_out[...] = gathered
    table = gathered[8:24, :LANES].astype(BF16)
    biases = dot(table, bucket_onehot(r.buckets, place, rows, length).astype(BF16))
    for i in range(pairs):
        r.window[i] = biases[2 * i : 2 * i + 2]
    pump_to(5)
    tokens.ready()
    tokens.sent()

    def norm_rows(i, carry):
        at = pl.ds(pl.multiple_of(i * rows, 16), rows)
        values = r.tok[at, :].astype(F32)
        normed = (values * rms_scale(values) * gain(0)).astype(BF16)
        r.tok[at, :] = normed
        r.tok_t[:, pl.ds(pl.multiple_of(i * rows, LANES), rows)] = normed.T
        return carry

    lax.fori_loop(0, length // rows, norm_rows, 0)
    emit_tok.start()

    def project_pair(source, target, base):
        def step(i, carry):
            at = pl.ds(pl.multiple_of(i * rows, 16), rows)
            block = source[at, :]
            for which in range(2):
                out = dot(block, weight(base + which)).astype(BF16)
                for j in range(pairs):
                    r.kv[target + which, j, at, :] = out[:, j * LANES : (j + 1) * LANES]
            return carry

        lax.fori_loop(0, source.shape[0] // rows, step, 0)
        emit_kv(target).start()
        emit_kv(target + 1).start()

    def project_query(normed, u, which):
        out = dot(normed, weight(u)).astype(BF16)
        for j in range(pairs):
            r.queries[which, j] = out[:, j * LANES : (j + 1) * LANES]

    def attention(which, bias, relays):
        def pair(i, carry):
            @pl.when(i >= 2)
            def _():
                emit_p(which, i).wait()

            slot = lax.rem(i, 2)
            more = None
            if bias:
                more = (r.row_ids[...], r.small_held[2, 3:4, :length], r.window[i])
            r.low[which, i] = attend_pair(
                r.queries[which, i],
                r.kv[2 * which, i],
                r.kv.at[2 * which + 1, i],
                r.probs.at[slot],
                more,
            )
            emit_p(which, i).start()
            for step, end in relays:
                @pl.when(i == step)
                def _():
                    pump_to(end)

            return carry

        lax.fori_loop(0, pairs, pair, 0)
        emit_p(which, 0).wait()
        emit_p(which, 1).wait()
        low = [r.low[which, j].astype(BF16) for j in range(pairs)]
        low = jnp.concatenate(low, axis=1)
        r.low_t[which] = low.T
        emit(r.low.at[which], r.low_out.at[which])
        emit(r.low_t.at[which], r.low_t_out.at[which])
        emit(r.queries.at[which], r.q_out.at[which])
        return low

    have(1, 2)
    project_pair(r.tok, 0, 1)
    have(0)
    emit_weights(0, 3).start()
    mine = pl.ds(pl.multiple_of(place.shard * rows, 16), rows)
    project_query(r.tok[mine, :], 0, 0)
    low = attention(0, True, SELF_PUMPS)
    have(3)
    r.first[...] = r.tok_in[...].astype(F32) + dot(low, weight(3))
    emit(r.first, r.first_out)
    pump_to(8)
    memories.ready()

    def turn_rows(i, carry):
        at = pl.ds(pl.multiple_of(i * rows, LANES), rows)
        r.enc_t[:, at] = r.enc[at, :].T
        return carry

    lax.fori_loop(0, length // rows, turn_rows, 0)
    emit_enc.start()
    have(5, 6)
    project_pair(r.enc, 2, 5)
    have(4)
    first = r.first[...]
    normed = (first * rms_scale(first) * gain(1)).astype(BF16)
    r.normed2_t[...] = normed.T
    emit(r.normed2_t, r.normed2_out)
    project_query(normed, 4, 1)
    low = attention(1, False, CROSS_PUMPS)
    have(7)
    emit_weights(3, 5).start()
    r.second[...] = r.first[...] + dot(low, weight(7))
    emit(r.second, r.second_out)
    second = r.second[...]
    normed = (second * rms_scale(second) * gain(2)).astype(BF16)
    r.normed[...] = normed
    r.normed3_t[...] = normed.T
    emit(r.normed3_t, r.normed3_out)
    for j in range(part):
        have(8 + j)
        value, slope = gelu_parts(dot(r.normed[...], weight(8 + j)))
        value = value.astype(BF16)
        r.hidden[j] = value
        r.hidden_t[j * width : (j + 1) * width, :] = value.T
        r.slope[j] = slope
        block = pl.ds(j * width, width)
        emit(r.hidden_t.at[block], r.hidden_out.at[block])
        emit(r.slope.at[j], r.slope_out.at[j])
    have(*range(8 + part, units))
    emit_weights(8, units - 8).start()
    total = second
    for j in range(part):
        total = total + dot(r.hidden[j], weight(8 + part + j))
    r.result[...] = total.astype(BF16)
    for u in range(units):
        gather.sent(u)
    memories.sent()
    small.sent(2)
    for u, count in ((0, 3), (3, 5), (8, units - 8)):
        emit_weights(u, count).wait()
    for i in range(4):
        emit_kv(i).wait()
    emit_tok.wait()
    emit_enc.wait()
    for copy in leaving:
        copy.wait()


def forward(tokens, encoded, ids, buckets, gains, bucket_bias, shards_of, reps, shards):
    rows, width = tokens.shape
    length, memory = rows * shards, encoded.shape[0] * shards
    nx = shards // 2
    feed_in, feed_out = shards_of[-2:]
    hidden = feed_in.shape[1]
    units = 8 + 2 * (hidden // width)
    pairs = width // LANES
    small = (24, max(length, width))
    kept = lambda *shape, dtype=BF16: (pl.BlockSpec(memory_space=pl.ANY), jax.ShapeDtypeStruct(shape, dtype))
    near = lambda *shape, dtype=F32: (pl.BlockSpec(memory_space=pltpu.VMEM), jax.ShapeDtypeStruct(shape, dtype))
    outs = dict(
        result=near(rows, width, dtype=BF16),
        small_out=near(*small),
        first_out=kept(rows, width, dtype=F32),
        second_out=kept(rows, width, dtype=F32),
        low_out=kept(2, pairs, rows, LANES, dtype=F32),
        low_t_out=kept(2, width, rows),
        q_out=kept(2, pairs, rows, LANES),
        normed2_out=kept(width, rows),
        normed3_out=kept(width, rows),
        hidden_out=kept(hidden, rows),
        slope_out=kept(hidden // width, rows, width, dtype=F32),
        w_out=kept(units * width, width),
        kv_out=kept(4, pairs, length, LANES),
        tok_out=kept(width, length),
        enc_out=kept(width, memory),
        p_out=kept(2, pairs, 2 * rows, length),
    )
    scratch = dict(
        whole=pltpu.VMEM((units * width, width), BF16),
        tok=pltpu.VMEM((length, width), BF16),
        enc=pltpu.VMEM((memory, width), BF16),
        kv=pltpu.VMEM((4, pairs, length, LANES), BF16),
        window=pltpu.VMEM((pairs, 2, length + rows), F32),
        row_ids=pltpu.VMEM((rows, 1), F32),
        probs=pltpu.VMEM((2, 2 * rows, length), BF16),
        first=pltpu.VMEM((rows, width), F32),
        second=pltpu.VMEM((rows, width), F32),
        low=pltpu.VMEM((2, pairs, rows, LANES), F32),
        low_t=pltpu.VMEM((2, width, rows), BF16),
        queries=pltpu.VMEM((2, pairs, rows, LANES), BF16),
        normed2_t=pltpu.VMEM((width, rows), BF16),
        normed3_t=pltpu.VMEM((width, rows), BF16),
        hidden_t=pltpu.VMEM((hidden, rows), BF16),
        slope=pltpu.VMEM((hidden // width, rows, width), F32),
        emit_sem=pltpu.SemaphoreType.DMA((10 + 2 * (hidden // width),)),
        normed=pltpu.VMEM((rows, width), BF16),
        hidden=pltpu.VMEM((hidden // width, rows, width), BF16),
        tok_t=pltpu.VMEM((width, length), BF16),
        enc_t=pltpu.VMEM((width, memory), BF16),
        p_sem=pltpu.SemaphoreType.DMA((2,)),
        out_sem=pltpu.SemaphoreType.DMA((units + 6,)),
    )
    scratch.update(zip(("small_held", "small_landed", "small_send", "small_recv"), SmallSum.scratch(nx, reps // 4, small)))
    scratch.update(zip(("w_send", "w_recv", "w_own"), Gather.scratch(units, nx)))
    scratch.update(zip(("t_send", "t_recv", "t_own"), Spread.scratch(nx)))
    scratch.update(zip(("e_send", "e_recv", "e_own"), Spread.scratch(nx)))
    shard_names = ["self_query", "self_keyval", "self_output", "cross_query", "cross_keyval", "cross_output", "feed_in", "feed_out"]
    near_names = ["tok_in", "enc_in", "ids", "buckets", "norm_self", "norm_cross", "norm_feed", "bucket_bias"]
    names = near_names + shard_names + list(outs) + list(scratch)
    made = pl.pallas_call(
        functools.partial(forward_kernel, reps, shards, tuple(names)),
        in_specs=[pl.BlockSpec(memory_space=pltpu.VMEM)] * 8 + [pl.BlockSpec(memory_space=pl.ANY)] * 8,
        out_specs=[spec for spec, _ in outs.values()],
        out_shape=[shape for _, shape in outs.values()],
        scratch_shapes=list(scratch.values()),
        compiler_params=pltpu.CompilerParams(
            collective_id=2, has_side_effects=True, vmem_limit_bytes=FUSED_LIMIT
        ),
    )(tokens, encoded, ids, buckets, *gains, bucket_bias, *shards_of)
    return types.SimpleNamespace(**dict(zip(outs, made)))


class RowSum:
    def __init__(self, place, parts, recv_a, recv_b, send, recv):
        self.place, self.parts, self.recv_a, self.recv_b = place, parts, recv_a, recv_b
        self.send, self.recv = send, recv

    @staticmethod
    def scratch(nx, width, rows):
        return [
            pltpu.VMEM((2, nx, width, rows), BF16),
            pltpu.VMEM((nx, width, rows), BF16),
            pltpu.VMEM((nx - 1, width, rows), BF16),
            pltpu.SemaphoreType.DMA((nx,)),
            pltpu.SemaphoreType.DMA((nx,)),
        ]

    def copy(self, which, src, dst, device):
        return remote(src, dst, self.send.at[which], self.recv.at[which], device)

    def to_core(self):
        p = self.place
        return self.copy(0, self.parts.at[1 - p.core], self.recv_a, p.other_core())

    def over_x(self, d):
        x, device = self.place.x_at(d)
        return self.copy(d, self.recv_a.at[x], self.recv_b.at[d - 1], device)

    def begin(self, total):
        rows = self.parts.shape[3]
        for s in range(2 * self.place.nx):
            self.parts[s % 2, s // 2] = total[:, s * rows : (s + 1) * rows].astype(BF16)
        self.to_core().start()

    def pass_x(self):
        self.to_core().wait_recv()
        self.recv_a[...] = added(self.recv_a[...], self.parts[self.place.core]).astype(BF16)
        for d in range(1, self.place.nx):
            self.over_x(d).start()

    def finish(self):
        p = self.place
        for d in range(1, p.nx):
            self.over_x(d).wait_recv()
        return added(self.recv_a[p.x], *[self.recv_b[d] for d in range(p.nx - 1)]).astype(F32)

    def sent(self):
        for d in range(1, self.place.nx):
            self.over_x(d).wait_send()


def attend_back_pair(query, keys, values, p_ref, output, grad, ds_ref, width=None):
    rows, length = query.shape[0], keys.shape[0]
    blocks = rows // 128
    grads, queries = stack_heads(grad), stack_heads(query)
    delta_wide = grad.astype(F32) * output
    d_weights = dot_nt(grads, values)
    windows = []
    for head in range(2):
        delta = jnp.sum(delta_wide * own_lanes(head == 0), axis=-1, keepdims=True)
        total = None
        for b in range(blocks):
            at = head * rows + b * 128
            part = p_ref[at : at + 128, :].astype(F32) * (
                d_weights[at : at + 128] - delta[b * 128 : b * 128 + 128]
            )
            ds_ref[at : at + 128, :] = part.astype(BF16)
            if width is not None:
                shift = (blocks - 1 - b) * 128
                pieces = [jnp.zeros((128, shift), F32)] if shift else []
                pieces.append(part)
                if width - shift - length:
                    pieces.append(jnp.zeros((128, width - shift - length), F32))
                placed = jnp.concatenate(pieces, axis=1)
                total = placed if total is None else total + placed
        if width is not None:
            windows.append(unskew(total, width))
    d_query = merge_heads(dot(ds_ref[...], keys)).astype(BF16)
    d_keys = dot(queries.T, ds_ref[...]).astype(BF16)
    d_values = dot(grads.T, p_ref[...]).astype(BF16)
    return d_query, d_keys, d_values, windows


BROUGHT = ("normed3_t", "hidden_t", "second", "low_t", "queries", "low", "first", "normed2_t")
REDUCTION = ("_parts", "_x", "_y", "_low", "_high", "_send", "_recv", "_own")


def late_units(units):
    return [n for n in LATE if n < units]


def backward_kernel(reps, shards, names, *refs):
    r = types.SimpleNamespace(**dict(zip(names, refs)))
    place = Place(reps, shards)
    rows, width = r.cotangent.shape
    length = r.enc_t.shape[1]
    pairs = width // LANES
    q = width // shards
    part = r.hidden_t.shape[0] // width
    units = 8 + 2 * part
    late = late_units(units)
    order = [n for n in range(units) if n not in late]
    reductions = [
        Reduction(place, x_first, names, r.fin, *(getattr(r, name + end) for end in REDUCTION))
        for x_first, names, name in ((True, order, "a"), (False, late, "b"))
    ]
    stages = len(reductions[0].copies)

    def owner(n):
        return (reductions[1], late.index(n)) if n in late else (reductions[0], order.index(n))

    small = SmallSum(place, r.small_held, r.small_landed, r.small_send, r.small_recv)
    sum_memory = RowSum(place, r.m_parts, r.m_a, r.m_b, r.m_send, r.m_recv)
    sum_tokens = RowSum(place, r.m_parts, r.t_a, r.t_b, r.t_send, r.t_recv)

    def gain(i):
        return r.gains[i : i + 1, :width]

    def load_weight(u, slot):
        block = pl.ds(u * width, width)
        return pltpu.make_async_copy(r.w_in.at[block], r.w.at[slot], r.w_sem.at[slot])

    ticks = [0]

    def slot_done(slot):
        while ticks[0] < TICKS.get(slot, 0):
            advance(ticks[0])
            ticks[0] += 1

    def load_slope(j):
        slot = j % 2
        return pltpu.make_async_copy(r.slope.at[j], r.slopes.at[slot], r.s_sem.at[slot])

    def load_kv(i, slot):
        return pltpu.make_async_copy(r.kv_in.at[i], r.kv.at[slot], r.kv_sem.at[slot])

    def load_p(which, i):
        slot = lax.rem(i, 2)
        return pltpu.make_async_copy(r.p_in.at[which, i], r.probs.at[slot], r.p_sem.at[slot])

    def load_t(source, which):
        return pltpu.make_async_copy(source, r.rows_t, r.t_sem.at[which])

    def away(n):
        return r.made.at[n % SLOTS, 1 - place.core]

    def fill(n, value):
        slot = n % SLOTS
        rest = value.shape[0] // shards
        half = width // 2
        for s in range(shards):
            for h in range(2):
                r.made[slot, s % 2, s // 2, h] = value[
                    s * rest : (s + 1) * rest, h * half : (h + 1) * half
                ].astype(BF16)
        red, u = owner(n)
        red.begin(u, away(n))

    def left(n):
        red, u = owner(n)
        red.over_core(u, away(n))[0].wait_send()

    def free(n):
        if n >= SLOTS:
            left(n - SLOTS)

    done_stages = {n: 0 for n in range(units)}
    started = [0]

    def set_out(end):
        while started[0] < min(end, len(order)):
            red, u = owner(order[started[0]])
            red.start(u, 0)
            started[0] += 1

    def take(n):
        red, u = owner(n)
        red.collect(u, away(n), r.made.at[n % SLOTS, place.core])
        if n in late:
            red.start(u, 0)
        elif order.index(n) < AHEAD_BUSY:
            set_out(order.index(n) + 1)

    def move(n, upto):
        red, u = owner(n)
        while done_stages[n] < min(upto, stages):
            red.step(u, done_stages[n])
            done_stages[n] += 1

    def advance(t):
        for back in range(stages):
            at = t - back
            if 0 <= at < len(order):
                move(order[at], back + 1)
            if back == 0:
                set_out(t + 1 + (AHEAD_BUSY if t + 1 < max(TICKS.values()) else AHEAD))
        for i, n in enumerate(late):
            move(n, t - LATE_START[i])

    def bring(name):
        source, sem = getattr(r, name + "_in"), r.bring_sem.at[BROUGHT.index(name)]
        return pltpu.make_async_copy(source, getattr(r, name), sem)

    load_slope(0).start()
    for slot, u in enumerate((8, 8 + part)):
        load_weight(u, slot).start()
    for name in BROUGHT[:3]:
        bring(name).start()
    enter(place)
    for name in BROUGHT[3:]:
        bring(name).start()
    for slot in range(2):
        load_kv(2 + slot, slot).start()
        load_p(1, slot).start()
    load_t(r.enc_t, 0).start()
    r.acc[...] = jnp.zeros((rows, width), F32)

    for j in range(part):
        slot = 2 * (j % 2)
        load_weight(8, slot).wait()
        load_weight(8 + part, slot + 1).wait()
        load_slope(j).wait()
        if j + 1 < part:
            load_slope(j + 1).start()
            load_weight(8 + j + 1, 2 - slot).start()
            load_weight(8 + part + j + 1, 3 - slot).start()
        if j == 0:
            bring("normed3_t").wait()
        grad_hidden = dot_nt(r.cotangent[...], r.w[slot + 1])
        grad = (grad_hidden * r.slopes[j % 2]).astype(BF16)
        free(j)
        fill(j, dot(r.normed3_t[...], grad))
        r.acc[...] += dot_nt(grad, r.w[slot])
        if j >= 1:
            take(j - 1)
    for slot, u in ((0, 7), (1, 5), (2, 6), (3, 4)):
        load_weight(u, slot).start()
    take(part - 1)
    bring("hidden_t").wait()
    for m in range(part):
        n = part + m
        free(n)
        value = jnp.concatenate(
            [
                dot(r.hidden_t[s * width + m * q : s * width + (m + 1) * q, :], r.cotangent[...])
                for s in range(shards)
            ],
            axis=0,
        )
        fill(n, value)
        if m >= 1:
            take(n - 1)
    bring("second").wait()
    back, d_gain3 = rms_back(r.second[...], gain(2), r.acc[...])
    r.grad[...] = r.cotangent[...].astype(F32) + back
    take(2 * part - 1)
    slot_done(0)

    def attention(which, fold, first_slot):
        def pair(i, carry):
            slot = lax.rem(i, 2)
            load_p(which, i).wait()
            d_query, d_keys, d_values, windows = attend_back_pair(
                r.queries[which, i],
                r.kv[0, i],
                r.kv[1, i],
                r.probs.at[slot],
                r.low[which, i],
                r.grad_att[i],
                r.ds,
                length + rows if fold else None,
            )
            r.d_query[i] = d_query
            at = pl.ds(pl.multiple_of(i * LANES, LANES), LANES)
            r.dk_t[at, :] = d_keys
            r.dv_t[at, :] = d_values
            if fold:
                r.d_window[i] = jnp.concatenate(windows, axis=0)

            @pl.when(i + 2 < pairs)
            def _():
                load_p(which, i + 2).start()

            for step in range(pairs):
                if first_slot + step in TICKS:
                    @pl.when(i == step)
                    def _():
                        slot_done(first_slot + step)

            return carry

        lax.fori_loop(0, pairs, pair, 0)

    def spread_grad(value):
        for i in range(pairs):
            r.grad_att[i] = value[:, i * LANES : (i + 1) * LANES].astype(BF16)

    def joined_query():
        return jnp.concatenate([r.d_query[i] for i in range(pairs)], axis=1)

    for name in BROUGHT[3:]:
        bring(name).wait()
    n = 2 * part
    grad_low = r.grad[...].astype(BF16)
    free(n)
    fill(n, dot(r.low_t[1], grad_low))
    load_weight(7, 0).wait()
    spread_grad(dot_nt(grad_low, r.w[0]))
    load_weight(3, 0).start()
    take(n)
    for slot in range(2):
        load_kv(2 + slot, slot).wait()
    attention(1, False, 1)
    for slot in range(2):
        load_kv(slot, slot).start()
        load_p(0, slot).start()
    load_weight(5, 1).wait()
    load_weight(6, 2).wait()
    sum_memory.begin(dot(r.w[1], r.dk_t[...]) + dot(r.w[2], r.dv_t[...]))
    load_weight(1, 1).start()
    load_weight(2, 2).start()
    load_t(r.enc_t, 0).wait()
    free(n + 1)
    fill(n + 1, dot_nt(r.rows_t[...], r.dk_t[...]))
    sum_memory.pass_x()
    free(n + 2)
    fill(n + 2, dot_nt(r.rows_t[...], r.dv_t[...]))
    take(n + 1)
    slot_done(7)
    load_t(r.tok_t, 1).start()
    d_query = joined_query()
    load_weight(4, 3).wait()
    back, d_gain2 = rms_back(r.first[...], gain(1), dot_nt(d_query, r.w[3]))
    load_weight(0, 3).start()
    free(n + 3)
    fill(n + 3, dot(r.normed2_t[...], d_query))
    take(n + 2)
    r.grad[...] = r.grad[...] + back
    slot_done(8)

    grad_low = r.grad[...].astype(BF16)
    take(n + 3)
    free(n + 4)
    fill(n + 4, dot(r.low_t[0], grad_low))
    load_weight(3, 0).wait()
    spread_grad(dot_nt(grad_low, r.w[0]))
    take(n + 4)
    for slot in range(2):
        load_kv(slot, slot).wait()
    attention(0, True, 9)
    load_weight(1, 1).wait()
    load_weight(2, 2).wait()
    sum_memory.to_core().wait_send()
    sum_tokens.begin(dot(r.w[1], r.dk_t[...]) + dot(r.w[2], r.dv_t[...]))
    load_t(r.tok_t, 1).wait()
    free(n + 5)
    fill(n + 5, dot_nt(r.rows_t[...], r.dk_t[...]))
    sum_tokens.pass_x()
    free(n + 6)
    fill(n + 6, dot_nt(r.rows_t[...], r.dv_t[...]))
    take(n + 5)
    r.d_memory[...] = sum_memory.finish().T
    slot_done(15)
    d_query = joined_query()
    free(n + 7)
    mine = pl.ds(pl.multiple_of(place.shard * rows, LANES), rows)
    fill(n + 7, dot(r.rows_t[:, mine], d_query))
    take(n + 6)
    load_weight(0, 3).wait()
    r.acc[...] = dot_nt(d_query, r.w[3])
    windows = jnp.concatenate([r.d_window[i] for i in range(pairs)], axis=0)
    d_table = lax.dot_general(
        windows,
        bucket_onehot(r.buckets, place, rows, length),
        (((1,), (1,)), ((), ())),
        precision=lax.Precision.HIGHEST,
        preferred_element_type=F32,
    )
    take(n + 7)
    slot_done(16)
    for t in range(ticks[0], len(order) + stages):
        advance(t)
        if t == LAST_SUM:
            values = r.tokens[...].astype(F32)
            total = r.acc[...] + sum_tokens.finish().T
            back, d_gain1 = rms_back(values, gain(0), total)
            r.d_tokens[...] = r.grad[...] + back
            r.small_held[0] = jnp.zeros(r.small_held.shape[1:], F32)
            for i, d_gain in enumerate((d_gain1, d_gain2, d_gain3)):
                r.small_held[0, i : i + 1, :width] = d_gain
            r.small_held[0, 8 : 8 + 2 * pairs, :LANES] = d_table
            small.launch()
        elif LAST_SUM < t < LAST_SUM + 6:
            small.step(t - LAST_SUM - 1)
    for n in range(units):
        move(n, stages)
    r.small_out[...] = r.small_held[5]
    for n in range(units):
        if n >= units - SLOTS:
            left(n)
        red, u = owner(n)
        red.sent(u)
    small.sent()
    sum_tokens.to_core().wait_send()
    sum_memory.sent()
    sum_tokens.sent()


def backward(tokens, cotangent, buckets, held, reps, shards):
    rows, width = tokens.shape
    length = held.enc_out.shape[1]
    nx, nh = shards // 2, reps // 4
    pairs = width // LANES
    q, half = width // shards, width // 2
    units = held.w_out.shape[0] // width
    small = (24, width)
    kept = pl.BlockSpec(memory_space=pl.ANY)
    near = pl.BlockSpec(memory_space=pltpu.VMEM)
    arrays = (held.normed3_out, held.hidden_out, held.second_out, held.low_t_out)
    arrays += (held.q_out, held.low_out, held.first_out, held.normed2_out)
    brought = dict(zip(BROUGHT, arrays))
    ins = dict(
        tokens=(near, tokens),
        cotangent=(near, cotangent),
        buckets=(near, buckets),
        gains=(near, held.small_out),
        **{name + "_in": (kept, array) for name, array in brought.items()},
        slope=(kept, held.slope_out),
        tok_t=(kept, held.tok_out),
        enc_t=(kept, held.enc_out),
        w_in=(kept, held.w_out),
        kv_in=(kept, held.kv_out),
        p_in=(kept, held.p_out),
    )
    outs = dict(
        d_tokens=(near, jax.ShapeDtypeStruct((rows, width), F32)),
        d_memory=(near, jax.ShapeDtypeStruct((rows, width), F32)),
        small_out=(near, jax.ShapeDtypeStruct(small, F32)),
        fin=(kept, jax.ShapeDtypeStruct((units, 2, q, half), BF16)),
    )
    scratch = {name: pltpu.VMEM(array.shape, array.dtype) for name, array in brought.items()}
    scratch.update(
        bring_sem=pltpu.SemaphoreType.DMA((len(brought),)),
        w=pltpu.VMEM((4, width, width), BF16),
        kv=pltpu.VMEM((2, pairs, length, LANES), BF16),
        probs=pltpu.VMEM((2, 2 * rows, length), BF16),
        ds=pltpu.VMEM((2 * rows, length), BF16),
        rows_t=pltpu.VMEM((width, length), BF16),
        dk_t=pltpu.VMEM((width, length), BF16),
        dv_t=pltpu.VMEM((width, length), BF16),
        d_query=pltpu.VMEM((pairs, rows, LANES), BF16),
        grad_att=pltpu.VMEM((pairs, rows, LANES), BF16),
        d_window=pltpu.VMEM((pairs, 2, length + rows), F32),
        acc=pltpu.VMEM((rows, width), F32),
        grad=pltpu.VMEM((rows, width), F32),
        made=pltpu.VMEM((SLOTS, 2, nx, 2, q, half), BF16),
        slopes=pltpu.VMEM((2, rows, width), F32),
        s_sem=pltpu.SemaphoreType.DMA((2,)),
        w_sem=pltpu.SemaphoreType.DMA((4,)),
        kv_sem=pltpu.SemaphoreType.DMA((2,)),
        p_sem=pltpu.SemaphoreType.DMA((2,)),
        t_sem=pltpu.SemaphoreType.DMA((2,)),
    )
    counts = {"a": units - len(late_units(units)), "b": len(late_units(units))}
    for name, count in counts.items():
        made_for = Reduction.scratch(count, name == "a", nx, nh, q, half)
        scratch.update(zip((name + end for end in REDUCTION), made_for))
    scratch.update(
        zip(("small_held", "small_landed", "small_send", "small_recv"), SmallSum.scratch(nx, nh, small))
    )
    for name in "mt":
        keys = (name + end for end in ("_parts", "_a", "_b", "_send", "_recv"))
        scratch.update(zip(keys, RowSum.scratch(nx, width, rows)))
    del scratch["t_parts"]
    names = tuple(list(ins) + list(outs) + list(scratch))
    made = pl.pallas_call(
        functools.partial(backward_kernel, reps, shards, names),
        in_specs=[spec for spec, _ in ins.values()],
        out_specs=[spec for spec, _ in outs.values()],
        out_shape=[shape for _, shape in outs.values()],
        scratch_shapes=list(scratch.values()),
        compiler_params=pltpu.CompilerParams(
            collective_id=3, has_side_effects=True, vmem_limit_bytes=FUSED_LIMIT
        ),
    )(*[value for _, value in ins.values()])
    return types.SimpleNamespace(**dict(zip(outs, made)))


def finish_kernel(squares, shards, names, *refs):
    r = types.SimpleNamespace(**dict(zip(names, refs)))
    step = pl.program_id(0)
    shard = lax.axis_index("shard")
    whole = lambda ref: jnp.concatenate([ref[0, 0], ref[0, 1]], axis=1).astype(F32)
    r.feed_in[...] = whole(r.fin_in)
    r.feed_out[...] = whole(r.fin_out)
    for source, group in zip((r.fin_cross, r.fin_self), squares):
        value = whole(source)
        for name, first, count in group:
            out = getattr(r, name)

            @pl.when((step >= first) & (step < first + count))
            def _():
                out[...] = value.reshape(out.shape)

    r.d_tokens[...] = r.tokens_in[...]
    r.d_memory[...] = r.memory_in[...]
    r.result[...] = r.result_in[...]

    @pl.when(step == 0)
    def _():
        small = r.small[...]
        width = small.shape[1]
        mine = lambda by: pltpu.roll(small, lax.rem(width - shard * by, width), 1)
        gains = mine(width // shards)
        for i, out in enumerate((r.norm_self, r.norm_cross, r.norm_feed)):
            out[...] = gains[i : i + 1, : width // shards].reshape(out.shape)
        cut, heads = r.bucket_bias.shape
        r.bucket_bias[...] = mine(cut)[8:24, :LANES].T[:cut, :heads]


def finish(made, result, table_shape, shards):
    units, _, q, half = made.fin.shape
    rows, width = made.d_tokens.shape
    steps = units // 4
    still = lambda *shape: pl.BlockSpec(shape, lambda n: (0,) * len(shape))
    line = pl.BlockSpec((rows // steps, width), lambda n: (n, 0))
    unit = lambda group: pl.BlockSpec((1, 2, q, half), lambda n: (group * steps + n, 0, 0, 0))
    pair = lambda first: pl.BlockSpec((1, q, width), lambda n: (jnp.where(n <= first, 0, 1), 0, 0))
    squares = (
        (("cross_output", 0, 1), ("cross_keyval", 1, 2), ("cross_query", 3, 1)),
        (("self_output", 0, 1), ("self_keyval", 1, 2), ("self_query", 3, 1)),
    )
    square = ((q, width), still(q, width))
    outs = dict(
        feed_in=((q, steps * width), pl.BlockSpec((q, width), lambda n: (0, n))),
        feed_out=((steps * q, width), pl.BlockSpec((q, width), lambda n: (n, 0))),
        cross_output=square,
        cross_keyval=((2, q, width), pair(1)),
        cross_query=square,
        self_output=square,
        self_keyval=((2, q, width), pair(1)),
        self_query=square,
        d_tokens=((rows, width), line),
        d_memory=((rows, width), line),
        result=((rows, width), line),
        norm_self=((q,), still(q)),
        norm_cross=((q,), still(q)),
        norm_feed=((q,), still(q)),
        bucket_bias=(table_shape, still(*table_shape)),
    )
    names = ("fin_in", "fin_out", "fin_cross", "fin_self", "tokens_in", "memory_in", "result_in", "small")
    done = pl.pallas_call(
        functools.partial(finish_kernel, squares, shards, names + tuple(outs)),
        grid=(steps,),
        in_specs=[unit(0), unit(1), unit(2), unit(3), line, line, line, still(*made.small_out.shape)],
        out_specs=[spec for _, spec in outs.values()],
        out_shape=[
            jax.ShapeDtypeStruct(shape, BF16 if name == "result" else F32)
            for name, (shape, _) in outs.items()
        ],
        compiler_params=pltpu.CompilerParams(vmem_limit_bytes=VMEM_LIMIT),
    )(*[made.fin] * 4, made.d_tokens, made.d_memory, result, made.small_out)
    return types.SimpleNamespace(**dict(zip(outs, done)))


def tiles_evenly(reps, shards, width):
    if reps % 4 or shards % 2 or width % shards:
        return False
    return (width // shards) % (8 * reps) == 0 and width % (4 * HD) == 0


def layer(
    tokens,
    encoded,
    block_ids,
    buckets,
    cotangent,
    norm_self,
    self_query,
    self_keyval,
    self_output,
    bucket_bias,
    norm_cross,
    cross_query,
    cross_keyval,
    cross_output,
    norm_feed,
    feed_in,
    feed_out,
):
    groups, positions, model_width = tokens.shape
    reps, shards = lax.axis_size("rep"), lax.axis_size("shard")
    length = (buckets.shape[0] + 1) // 2
    memory_local = encoded.shape[1]
    row_anchor = lax.axis_index("shard") * positions
    heads, bucket_count = bucket_bias.shape[0], bucket_bias.shape[1] * shards
    window_width = length + positions
    fused = tiles_evenly(reps, shards, model_width) and encoded.shape == tokens.shape
    fused = fused and feed_out.shape[0] == model_width
    fused = fused and feed_in.shape[1] == 4 * model_width and positions % LANES == 0
    if fused:
        offsets = jnp.pad(buckets, (1, 0))[None, :]
        gains = (norm_self, norm_cross, norm_feed)
        matrices = (self_query, self_keyval, self_output, cross_query, cross_keyval, cross_output)
        matrices += (feed_in, feed_out)
        held = forward(
            tokens[0], encoded[0], block_ids, offsets, gains, bucket_bias.T, matrices, reps, shards
        )
        made = backward(tokens[0], cotangent[0], offsets, held, reps, shards)
        out = finish(made, held.result, bucket_bias.T.shape, shards)
        return (
            out.result[None],
            out.d_tokens[None],
            out.d_memory[None],
            out.norm_self,
            out.self_query,
            out.self_keyval,
            out.self_output,
            out.bucket_bias.T,
            out.norm_cross,
            out.cross_query,
            out.cross_keyval,
            out.cross_output,
            out.norm_feed,
            out.feed_in,
            out.feed_out,
        )

    inputs = tokens[0].astype(F32)
    encoded_whole = gather(encoded[0])
    ids_whole = gather(block_ids[0])
    gains = gather(jnp.stack([norm_self, norm_cross, norm_feed]), 1).astype(F32)
    gain_first, gain_second, gain_third = gains[0:1], gains[1:2], gains[2:3]
    query_first, keyval_first, output_first, table = (
        gather(self_query),
        gather(self_keyval, 1),
        gather(self_output),
        gather(bucket_bias, 1),
    )
    query_second, keyval_second, output_second = (
        gather(cross_query),
        gather(cross_keyval, 1),
        gather(cross_output),
    )
    inner, outer = gather(feed_in), gather(feed_out)

    window_buckets = lax.dynamic_slice_in_dim(
        jnp.pad(buckets, (1, 0)), length - row_anchor - positions, window_width
    )
    onehot = window_buckets[None, :] == jnp.arange(bucket_count, dtype=jnp.int32)[:, None]
    window = dot(table, onehot.astype(BF16)).reshape(heads // 2, 2, window_width)

    normed_first = (inputs * rms_scale(inputs) * gain_first).astype(BF16)
    normed_whole = gather(normed_first)
    query = dot(normed_first, query_first).astype(BF16)
    keys = dot(normed_whole, keyval_first[0]).astype(BF16)
    values = dot(normed_whole, keyval_first[1]).astype(BF16)
    attended, weights = attend(
        query, keys, values, (block_ids[0][:, None], ids_whole[None, :], window)
    )
    low_first = attended.astype(BF16)
    first = inputs + dot(low_first, output_first)

    memory_keys = dot(encoded_whole, keyval_second[0]).astype(BF16)
    memory_values = dot(encoded_whole, keyval_second[1]).astype(BF16)
    normed_second = (first * rms_scale(first) * gain_second).astype(BF16)
    query_cross = dot(normed_second, query_second).astype(BF16)
    attended_cross, weights_cross = attend(query_cross, memory_keys, memory_values)
    low_second = attended_cross.astype(BF16)
    second = first + dot(low_second, output_second)

    normed_third = (second * rms_scale(second) * gain_third).astype(BF16)
    preact = dot(normed_third, inner)
    value, slope = gelu_parts(preact)
    hidden = value.astype(BF16)
    result = (second + dot(hidden, outer)).astype(BF16)

    grad_result = cotangent[0]
    d_outer = dot_tn(hidden, grad_result)
    grad_preact = (dot_nt(grad_result, outer) * slope).astype(BF16)
    d_inner = dot_tn(normed_third, grad_preact)
    back, d_gain_third = rms_back(second, gain_third, dot_nt(grad_preact, inner))
    grad_second = grad_result.astype(F32) + back

    grad_second_low = grad_second.astype(BF16)
    d_output_second = dot_tn(low_second, grad_second_low)
    grad_att = dot_nt(grad_second_low, output_second).astype(BF16)
    d_query, d_keys, d_values = attend_back(
        query_cross, memory_keys, memory_values, weights_cross, attended_cross, grad_att
    )
    d_keyval_second = jnp.stack(
        [dot_tn(encoded_whole, d_keys), dot_tn(encoded_whole, d_values)]
    )
    d_memory = scatter(dot_nt(d_keys, keyval_second[0]) + dot_nt(d_values, keyval_second[1]))
    d_query_second = dot_tn(normed_second, d_query)
    back, d_gain_second = rms_back(first, gain_second, dot_nt(d_query, query_second))
    grad_first = grad_second + back

    grad_first_low = grad_first.astype(BF16)
    d_output_first = dot_tn(low_first, grad_first_low)
    grad_att = dot_nt(grad_first_low, output_first).astype(BF16)
    d_query, d_keys, d_values, d_window = attend_back(
        query, keys, values, weights, attended, grad_att, window.shape
    )
    d_table = lax.dot_general(
        d_window.reshape(heads, window_width),
        onehot.astype(F32),
        (((1,), (1,)), ((), ())),
        precision=lax.Precision.HIGHEST,
    )
    d_keyval_first = jnp.stack([dot_tn(normed_whole, d_keys), dot_tn(normed_whole, d_values)])
    grad_normed = scatter(
        dot_nt(d_keys, keyval_first[0]) + dot_nt(d_values, keyval_first[1])
    ).astype(F32) + dot_nt(d_query, query_first)
    d_query_first = dot_tn(normed_first, d_query)
    back, d_gain_first = rms_back(inputs, gain_first, grad_normed)
    d_inputs = grad_first + back

    gains = [d_gain_first, d_gain_second, d_gain_third]
    squares = [d_query_first, d_output_first, d_query_second, d_output_second]
    pairs = [d_keyval_first, d_keyval_second]
    total = lambda a, axis=0: lax.psum(scatter(a, axis), "rep").astype(F32)
    gains = [total(gain[0]) for gain in gains]
    squares = [total(square) for square in squares]
    pairs = [total(pair, 1) for pair in pairs]
    d_table, d_inner, d_outer = total(d_table, 1), total(d_inner), total(d_outer)
    totals = (gains[0], squares[0], pairs[0], squares[1], d_table)
    totals += (gains[1], squares[2], pairs[1], squares[3], gains[2], d_inner, d_outer)
    return (result[None], d_inputs[None], d_memory.astype(F32)[None]) + totals


def solution(mesh):
    rows, line = P("rep", "shard", None), P("shard")
    matrix, pair, table = P("shard", None), P(None, "shard", None), P(None, "shard")
    weights = (line, matrix, pair, matrix, table, line, matrix, pair, matrix, line, matrix, matrix)
    return jax.shard_map(
        layer,
        mesh=mesh,
        in_specs=(rows, rows, P("rep", "shard"), P(), rows) + weights,
        out_specs=(rows, rows, rows) + weights,
        check_vma=False,
    )
```

```python
import functools
import types

import jax
import jax.numpy as jnp
from jax import lax
from jax.experimental import pallas as pl
from jax.experimental.pallas import tpu as pltpu
from jax.sharding import PartitionSpec as P

H = 12
HD = 64
LANES = 2 * HD
EPSILON = 1e-06
MASKED = -1e30
F32 = jnp.float32
BF16 = jnp.bfloat16
VMEM_LIMIT = 56 * 2**20
FUSED_LIMIT = 62 * 2**20
AHEAD = 2
CLOSE = 2
LAST_SUM = 12
TICKS = {0: 1, 2: 2, 5: 3, 7: 4, 8: 5, 10: 6, 12: 7, 14: 8, 15: 9, 16: 10}
LINE = 3
SELF_PUMPS = ((1, 6), (3, 7), (5, 8))
CROSS_PUMPS = ((1, 12), (3, 13), (5, 14))
QUARTERS = (0, 1, 2, 3)
LATE = (1, 3)
LATE_START = (-1, 1)
SLOTS = 4
LAG = 1
MESH = pl.DeviceIdType.MESH


def dot(a, b):
    return lax.dot_general(a, b, (((1,), (0,)), ((), ())), preferred_element_type=F32)


def dot_nt(a, b):
    return lax.dot_general(a, b, (((1,), (1,)), ((), ())), preferred_element_type=F32)


def dot_tn(a, b):
    return lax.dot_general(a, b, (((0,), (0,)), ((), ())), preferred_element_type=F32)


def rms_scale(values):
    return lax.rsqrt(jnp.mean(values * values, axis=-1, keepdims=True) + EPSILON)


def rms_back(values, gain, grad):
    scale = rms_scale(values)
    scaled = gain * grad
    mean = jnp.mean(scaled * values, axis=-1, keepdims=True)
    d_values = scale * scaled - values * (scale * scale * scale) * mean
    d_gain = jnp.sum(grad * values * scale, axis=0, keepdims=True)
    return d_values, d_gain


def gelu_parts(x):
    c = 0.7978845608028654
    t = jnp.tanh(c * (x + 0.044715 * (x * x * x)))
    value = 0.5 * x * (1.0 + t)
    slope = 0.5 * (1.0 + t) + 0.5 * x * (1.0 - t * t) * (c * (1.0 + 3.0 * 0.044715 * (x * x)))
    return value, slope


def own_lanes(first):
    lane = lax.broadcasted_iota(jnp.int32, (1, LANES), 1)
    mine = (lane < HD) if first else (lane >= HD)
    return jnp.where(mine, 1.0, 0.0)


def stack_heads(pair):
    one, two = own_lanes(True).astype(pair.dtype), own_lanes(False).astype(pair.dtype)
    return jnp.concatenate([pair * one, pair * two], axis=0)


def merge_heads(stacked):
    rows = stacked.shape[0] // 2
    return stacked[:rows] * own_lanes(True) + stacked[rows:] * own_lanes(False)


def skew(window, width):
    sub = lax.broadcasted_iota(jnp.int32, (8, width), 0)
    rows = jnp.broadcast_to(window, (8, width))
    for bit in (1, 2, 4):
        rows = jnp.where((sub & bit) != 0, pltpu.roll(rows, bit, 1), rows)
    return jnp.concatenate(
        [pltpu.roll(rows, (8 * g + width - 128) % width, 1) for g in range(16)], axis=0
    )


def unskew(total, width):
    sub = lax.broadcasted_iota(jnp.int32, (8, width), 0)
    rows = jnp.zeros((8, width), F32)
    for g in range(16):
        rows = rows + pltpu.roll(total[8 * g : 8 * g + 8], 128 - 8 * g, 1)
    for bit in (1, 2, 4):
        rows = jnp.where((sub & bit) != 0, pltpu.roll(rows, width - bit, 1), rows)
    return jnp.sum(rows, axis=0, keepdims=True)


def attend_kernel(biased, q_ref, k_ref, v_ref, *refs):
    if biased:
        row_ids, key_ids, window_ref, out_ref, p_ref = refs
    else:
        out_ref, p_ref = refs
    rows, length = q_ref.shape[0], k_ref.shape[0]
    blocks = rows // 128
    scores = dot_nt(stack_heads(q_ref[...]), k_ref[...])
    for head in range(2):
        if biased:
            width = window_ref.shape[2]
            table = skew(window_ref[0, head : head + 1, :], width)
        for b in range(blocks):
            at = head * rows + b * 128
            part = scores[at : at + 128]
            if biased:
                shift = (blocks - 1 - b) * 128
                allowed = key_ids[...] <= row_ids[b * 128 : b * 128 + 128, :]
                part = jnp.where(allowed, part + table[:, shift : shift + length], MASKED)
            top = jnp.max(part, axis=-1, keepdims=True)
            raised = jnp.exp(part - top)
            share = 1.0 / jnp.sum(raised, axis=-1, keepdims=True)
            p_ref[0, at : at + 128, :] = (raised * share).astype(BF16)
    out_ref[...] = merge_heads(dot(p_ref[0], v_ref[...]))


def attend_back_kernel(folded, q_ref, k_ref, v_ref, p_ref, out_ref, grad_ref, *refs):
    if folded:
        dq_ref, dk_ref, dv_ref, window_ref, ds_ref = refs
    else:
        dq_ref, dk_ref, dv_ref, ds_ref = refs
    rows, length = q_ref.shape[0], k_ref.shape[0]
    blocks = rows // 128
    grad = grad_ref[...]
    grads = stack_heads(grad)
    delta_wide = grad.astype(F32) * out_ref[...]
    d_weights = dot_nt(grads, v_ref[...])
    for head in range(2):
        if folded:
            width = window_ref.shape[2]
            total = jnp.zeros((128, width), F32)
        delta = jnp.sum(delta_wide * own_lanes(head == 0), axis=-1, keepdims=True)
        for b in range(blocks):
            at = head * rows + b * 128
            part = p_ref[0, at : at + 128, :].astype(F32) * (
                d_weights[at : at + 128] - delta[b * 128 : b * 128 + 128]
            )
            ds_ref[at : at + 128, :] = part.astype(BF16)
            if folded:
                shift = (blocks - 1 - b) * 128
                pieces = [part]
                if shift:
                    pieces = [jnp.zeros((128, shift), F32)] + pieces
                if width - shift - length:
                    pieces = pieces + [jnp.zeros((128, width - shift - length), F32)]
                total = total + jnp.concatenate(pieces, axis=1)
        if folded:
            window_ref[0, head : head + 1, :] = unskew(total, width)
    queries = stack_heads(q_ref[...])
    dq_ref[...] = merge_heads(dot(ds_ref[...], k_ref[...])).astype(BF16)
    dk_ref[...] = dot(queries.T, ds_ref[...]).T.astype(BF16)
    dv_ref[...] = dot(grads.T, p_ref[0]).T.astype(BF16)


def attend(query, keys, values, bias=None):
    rows, width = query.shape
    length = keys.shape[0]
    pairs = width // LANES
    column = lambda n: pl.BlockSpec((n, LANES), lambda i: (0, i))
    whole = lambda a: pl.BlockSpec(a.shape, lambda i: (0,) * a.ndim)
    operands, specs = [query, keys, values], [column(rows), column(length), column(length)]
    if bias is not None:
        row_ids, key_ids, window = bias
        operands += [row_ids, key_ids, window]
        specs += [
            whole(row_ids),
            whole(key_ids),
            pl.BlockSpec((1,) + window.shape[1:], lambda i: (i, 0, 0)),
        ]
    return pl.pallas_call(
        functools.partial(attend_kernel, bias is not None),
        grid=(pairs,),
        in_specs=specs,
        out_specs=[
            column(rows),
            pl.BlockSpec((1, 2 * rows, length), lambda i: (i, 0, 0)),
        ],
        out_shape=[
            jax.ShapeDtypeStruct((rows, width), F32),
            jax.ShapeDtypeStruct((pairs, 2 * rows, length), BF16),
        ],
        compiler_params=pltpu.CompilerParams(vmem_limit_bytes=VMEM_LIMIT),
        cost_estimate=pl.CostEstimate(
            flops=16 * rows * length * width,
            bytes_accessed=2 * pairs * 2 * rows * length,
            transcendentals=pairs * 2 * rows * length,
        ),
    )(*operands)


def attend_back(query, keys, values, weights, output, grad, window_shape=None):
    rows, width = query.shape
    length = keys.shape[0]
    pairs = width // LANES
    column = lambda n: pl.BlockSpec((n, LANES), lambda i: (0, i))
    out_specs = [column(rows), column(length), column(length)]
    out_shape = [
        jax.ShapeDtypeStruct((rows, width), BF16),
        jax.ShapeDtypeStruct((length, width), BF16),
        jax.ShapeDtypeStruct((length, width), BF16),
    ]
    if window_shape is not None:
        out_specs.append(pl.BlockSpec((1,) + window_shape[1:], lambda i: (i, 0, 0)))
        out_shape.append(jax.ShapeDtypeStruct(window_shape, F32))
    return pl.pallas_call(
        functools.partial(attend_back_kernel, window_shape is not None),
        grid=(pairs,),
        in_specs=[
            column(rows),
            column(length),
            column(length),
            pl.BlockSpec((1, 2 * rows, length), lambda i: (i, 0, 0)),
            column(rows),
            column(rows),
        ],
        out_specs=out_specs,
        out_shape=out_shape,
        scratch_shapes=[pltpu.VMEM((2 * rows, length), BF16)],
        compiler_params=pltpu.CompilerParams(vmem_limit_bytes=VMEM_LIMIT),
        cost_estimate=pl.CostEstimate(
            flops=32 * rows * length * width,
            bytes_accessed=2 * pairs * 2 * rows * length,
            transcendentals=0,
        ),
    )(query, keys, values, weights, output, grad)


def gather(values, axis=0):
    return lax.all_gather(values, "shard", axis=axis, tiled=True)


def scatter(values, axis=0):
    return lax.psum_scatter(values.astype(BF16), "shard", scatter_dimension=axis, tiled=True)


class Place:
    def __init__(self, reps, shards):
        self.nx, self.nh = shards // 2, reps // 4
        rep, shard = lax.axis_index("rep"), lax.axis_index("shard")
        self.rep, self.shard = rep, shard
        self.core, self.x = lax.rem(shard, 2), lax.div(shard, 2)
        self.y, z = lax.rem(rep, 2), lax.div(rep, 2)
        self.low, self.high = lax.rem(z, 2), lax.div(z, 2)

    def other_core(self):
        return (self.rep, self.x * 2 + 1 - self.core)

    def x_at(self, step):
        x = lax.rem(self.x + step, self.nx)
        return x, (self.rep, x * 2 + self.core)

    def other_y(self):
        return (self.rep + 1 - 2 * self.y, self.shard)

    def other_low(self):
        return (self.rep + 2 - 4 * self.low, self.shard)

    def high_at(self, step):
        high = lax.rem(self.high + step, self.nh)
        return high, (high * 4 + self.low * 2 + self.y, self.shard)

    def partners(self):
        found = [self.other_core(), self.other_y(), self.other_low()]
        found += [self.x_at(d)[1] for d in range(1, self.nx)]
        found += [self.high_at(d)[1] for d in range(1, self.nh)]
        return found


def enter(place):
    barrier = pltpu.get_barrier_semaphore()
    partners = place.partners()
    for device in partners:
        pl.semaphore_signal(barrier, inc=1, device_id=device, device_id_type=MESH)
    pl.semaphore_wait(barrier, len(partners))


def remote(src, dst, send, recv, device):
    return pltpu.make_async_remote_copy(
        src_ref=src, dst_ref=dst, send_sem=send, recv_sem=recv, device_id=device, device_id_type=MESH
    )


def added(*parts):
    if len(parts) == 2:
        return parts[0] + parts[1]
    total = parts[0].astype(F32)
    for part in parts[1:]:
        total = total + part.astype(F32)
    return total


class Reduction:
    def __init__(self, place, x_first, names, fin, parts, recv_x, recv_y, recv_low, recv_high, send, recv, own_sem):
        self.place, self.x_first, self.parts, self.fin = place, x_first, parts, fin
        self.names = names
        self.recv_x, self.recv_y, self.recv_low, self.recv_high = recv_x, recv_y, recv_low, recv_high
        self.send, self.recv, self.own_sem = send, recv, own_sem
        self.half = parts.shape[3] // 2
        self.rows = self.half // place.nh
        stages = [self.over_y, self.over_low, self.over_high]
        stages = [self.over_x] + stages if x_first else stages + [self.over_x]
        stages += [self.back_high, self.back_low, self.back_y]
        self.copies = stages
        self.adds = stages.index(self.back_high)

    @staticmethod
    def scratch(n, x_first, nx, nh, q, half):
        copies = 4 + nx + 2 * (nh - 1)
        wide = (n,) if x_first else (n, nx)
        x_part = (2, q) if x_first else (q // (2 * nh),)
        return [
            pltpu.VMEM((n, nx, 2, q, half), BF16),
            pltpu.VMEM((n, nx - 1) + x_part + (half,), BF16),
            pltpu.VMEM(wide + (q, half), BF16),
            pltpu.VMEM(wide + (q // 2, half), BF16),
            pltpu.VMEM((n, nh - 1) + wide[1:] + (q // (2 * nh), half), BF16),
            pltpu.SemaphoreType.DMA((n, copies)),
            pltpu.SemaphoreType.DMA((n, copies)),
            pltpu.SemaphoreType.DMA((n,)),
        ]

    def copy(self, u, which, src, dst, device):
        return remote(src, dst, self.send.at[u, which], self.recv.at[u, which], device)

    def low_rows(self, low):
        return pl.ds(pl.multiple_of(low * self.half, 16), self.half)

    def high_rows(self, high):
        at = self.place.low * self.half + high * self.rows
        return pl.ds(pl.multiple_of(at, 16), self.rows)

    def chips(self):
        return self.place.x if self.x_first else slice(None)

    def over_core(self, u, src):
        return [self.copy(u, 0, src, self.parts.at[u], self.place.other_core())]

    def over_x(self, u):
        p, out = self.place, []
        rest = () if self.x_first else (p.y, self.high_rows(p.high))
        for d in range(1, p.nx):
            x, device = p.x_at(d)
            src = self.parts.at[(u, x) + rest]
            out.append(self.copy(u, 2 + d, src, self.recv_x.at[u, d - 1], device))
        return out, (u, p.x) + rest, [self.recv_x.at[u, d] for d in range(p.nx - 1)]

    def over_y(self, u):
        p, chips = self.place, self.chips()
        src = self.parts.at[u, chips, 1 - p.y]
        copies = [self.copy(u, 1, src, self.recv_y.at[u], p.other_y())]
        return copies, (u, chips, p.y), [self.recv_y.at[u]]

    def over_low(self, u):
        p, chips = self.place, self.chips()
        src = self.parts.at[u, chips, p.y, self.low_rows(1 - p.low)]
        copies = [self.copy(u, 2 + p.nx, src, self.recv_low.at[u], p.other_low())]
        return copies, (u, chips, p.y, self.low_rows(p.low)), [self.recv_low.at[u]]

    def over_high(self, u):
        p, chips, out = self.place, self.chips(), []
        for d in range(1, p.nh):
            high, device = p.high_at(d)
            src = self.parts.at[u, chips, p.y, self.high_rows(high)]
            out.append(self.copy(u, 3 + p.nx + d, src, self.recv_high.at[u, d - 1], device))
        came = [self.recv_high.at[u, d] for d in range(p.nh - 1)]
        return out, (u, chips, p.y, self.high_rows(p.high)), came

    def piece(self, u):
        p = self.place
        rows = self.high_rows(p.high)
        return self.parts.at[u, p.x, p.y, rows], self.fin.at[self.names[u], p.y, rows]

    def keep(self, u):
        return pltpu.make_async_copy(*self.piece(u), self.own_sem.at[u])

    def back_high(self, u):
        p = self.place
        return [
            self.copy(u, 2 + p.nx + p.nh + d, *self.piece(u), p.high_at(d)[1])
            for d in range(1, p.nh)
        ]

    def back_low(self, u):
        p = self.place
        rows = self.fin.at[self.names[u], p.y, self.low_rows(p.low)]
        return [self.copy(u, 3 + p.nx, rows, rows, p.other_low())]

    def back_y(self, u):
        half = self.fin.at[self.names[u], self.place.y]
        return [self.copy(u, 2, half, half, self.place.other_y())]

    def begin(self, u, src):
        self.over_core(u, src)[0].start()

    def collect(self, u, src, own):
        self.over_core(u, src)[0].wait_recv()
        self.parts[u] = added(self.parts[u], own[...]).astype(BF16)

    def start(self, u, stage):
        if stage < len(self.copies):
            copies = self.copies[stage](u)
            for copy in copies[0] if stage < self.adds else copies:
                copy.start()

    def step(self, u, stage):
        if stage < self.adds:
            copies, stays, came = self.copies[stage](u)
            for copy in copies:
                copy.wait_recv()
            total = added(self.parts[stays], *[part[...] for part in came])
            self.parts[stays] = total.astype(BF16)
            if stage + 1 == self.adds:
                self.keep(u).start()
        else:
            for copy in self.copies[stage](u):
                copy.wait_recv()
            if stage == self.adds:
                self.keep(u).wait()
        self.start(u, stage + 1)

    def sent(self, u):
        for stage in range(len(self.copies)):
            copies = self.copies[stage](u)
            for copy in copies[0] if stage < self.adds else copies:
                copy.wait_send()


class SmallSum:
    def __init__(self, place, held, landed, send, recv):
        self.place, self.held, self.landed = place, held, landed
        self.send, self.recv = send, recv

    @staticmethod
    def scratch(nx, nh, shape):
        copies = 3 + nx - 1 + nh - 1
        return [
            pltpu.VMEM((6,) + shape, F32),
            pltpu.VMEM((copies,) + shape, F32),
            pltpu.SemaphoreType.DMA((copies,)),
            pltpu.SemaphoreType.DMA((copies,)),
        ]

    def copies(self, stage):
        p = self.place
        first, devices = [
            (0, [p.other_core()]),
            (3, [p.x_at(d)[1] for d in range(1, p.nx)]),
            (1, [p.other_y()]),
            (2, [p.other_low()]),
            (2 + p.nx, [p.high_at(d)[1] for d in range(1, p.nh)]),
        ][stage]
        return [
            remote(self.held.at[stage], self.landed.at[first + i], self.send.at[first + i], self.recv.at[first + i], device)
            for i, device in enumerate(devices)
        ], list(range(first, first + len(devices)))

    def begin(self, value):
        self.held[0] = value
        self.launch()

    def launch(self):
        for copy in self.copies(0)[0]:
            copy.start()

    def step(self, stage, stages=5):
        copies, slots = self.copies(stage)
        for copy in copies:
            copy.wait_recv()
        total = self.held[stage]
        for slot in slots:
            total = total + self.landed[slot]
        self.held[stage + 1] = total
        if stage + 1 < stages:
            for copy in self.copies(stage + 1)[0]:
                copy.start()
        return total

    def sent(self, stages=5):
        for stage in range(stages):
            for copy in self.copies(stage)[0]:
                copy.wait_send()


class Gather:
    def __init__(self, place, whole, own, hidden_rows, send, recv, own_sem):
        self.place, self.whole, self.own = place, whole, own
        self.send, self.recv, self.own_sem = send, recv, own_sem
        self.width = whole.shape[1]
        self.q = self.width // (2 * place.nx)
        self.square = len(own) - hidden_rows // self.q
        self.hidden_rows = hidden_rows

    @staticmethod
    def scratch(units, nx):
        copies = 1 + 8 * (nx - 1)
        return [
            pltpu.SemaphoreType.DMA((units, copies)),
            pltpu.SemaphoreType.DMA((units, copies)),
            pltpu.SemaphoreType.DMA((units,)),
        ]

    def cut(self, u, far_first, far_second=False):
        p = self.place
        first, second = (p.y, p.low) if u % 2 == 0 else (p.low, p.y)
        first = 1 - first if far_first else first
        second = 1 - second if far_second else second
        if u not in QUARTERS:
            return first * (self.q // 2)
        return (first * 2 + second) * (self.q // 4)

    def size(self, u):
        return self.q // 4 if u in QUARTERS else self.q // 2

    def first(self, u):
        return self.place.other_y() if u % 2 == 0 else self.place.other_low()

    def second(self, u):
        return self.place.other_low() if u % 2 == 0 else self.place.other_y()

    def part(self, u, shard, at=None):
        if u >= self.square:
            start = self.square * self.width + shard * self.hidden_rows
            start = start + (u - self.square) * self.q
        else:
            start = u * self.width + shard * self.q
        if at is None:
            return self.whole.at[pl.ds(pl.multiple_of(start, 16), self.q)]
        return self.whole.at[pl.ds(pl.multiple_of(start + at, 16), self.size(u))]

    def came(self, d):
        p = self.place
        return lax.rem(p.x + p.nx - d, p.nx) * 2 + p.core

    def copy(self, u, which, src, dst, device):
        return remote(src, dst, self.send.at[u, which], self.recv.at[u, which], device)

    def to_core(self, u):
        shard = self.place.shard
        return self.copy(u, 0, self.own[u], self.part(u, shard), self.place.other_core())

    def keep(self, u):
        return pltpu.make_async_copy(
            self.own[u], self.part(u, self.place.shard), self.own_sem.at[u]
        )

    def over_x(self, u, d):
        p = self.place
        at = self.cut(u, False)
        src = self.own[u].at[pl.ds(pl.multiple_of(at, 16), self.size(u))]
        return self.copy(u, 8 * d - 7, src, self.part(u, p.shard, at), p.x_at(d)[1])

    def on(self, u, d, which, far_first, far_second, device):
        here = self.part(u, self.came(d), self.cut(u, far_first, far_second))
        return self.copy(u, 8 * d - 7 + which, here, here, device)

    def onward(self, u, d, which):
        core, first, second = self.place.other_core(), self.first(u), self.second(u)
        far_first, far_second, device = (
            (False, False, first),
            (False, False, second),
            (False, False, core),
            (False, True, first),
            (False, True, core),
            (True, False, core),
            (True, True, core),
        )[which]
        return self.on(u, d, which + 1, far_first, far_second, device)

    def issue(self, u):
        for d in range(1, self.place.nx):
            self.over_x(u, d).start()
        self.to_core(u).start()
        self.keep(u).start()

    def relay_x(self, u):
        for d in range(1, self.place.nx):
            self.over_x(u, d).wait_recv()
            for which in (0, 1, 2) if u in QUARTERS else (0, 2):
                self.onward(u, d, which).start()

    def relay_second(self, u):
        for d in range(1, self.place.nx if u in QUARTERS else 1):
            self.onward(u, d, 1).wait_recv()
            self.onward(u, d, 3).start()
            self.onward(u, d, 4).start()

    def relay_first(self, u):
        for d in range(1, self.place.nx):
            self.onward(u, d, 0).wait_recv()
            self.onward(u, d, 5).start()
            if u in QUARTERS:
                self.onward(u, d, 3).wait_recv()
                self.onward(u, d, 6).start()

    def ready(self, u):
        self.keep(u).wait()
        self.to_core(u).wait_recv()
        for d in range(1, self.place.nx):
            for which in (2, 4, 5, 6) if u in QUARTERS else (2, 5):
                self.onward(u, d, which).wait_recv()

    def sent(self, u):
        self.to_core(u).wait_send()
        for d in range(1, self.place.nx):
            self.over_x(u, d).wait_send()
            for which in range(7) if u in QUARTERS else (0, 2, 5):
                self.onward(u, d, which).wait_send()


class Spread:
    def __init__(self, place, own, whole, send, recv, own_sem):
        self.place, self.own, self.whole = place, own, whole
        self.send, self.recv, self.own_sem = send, recv, own_sem
        self.count = own.shape[0]

    @staticmethod
    def scratch(nx):
        copies = 1 + 2 * (nx - 1)
        return [
            pltpu.SemaphoreType.DMA((copies,)),
            pltpu.SemaphoreType.DMA((copies,)),
            pltpu.SemaphoreType.DMA(()),
        ]

    def part(self, shard):
        return self.whole.at[pl.ds(pl.multiple_of(shard * self.count, 16), self.count)]

    def copy(self, which, src, dst, device):
        return remote(src, dst, self.send.at[which], self.recv.at[which], device)

    def to_core(self):
        return self.copy(0, self.own, self.part(self.place.shard), self.place.other_core())

    def over_x(self, d):
        p = self.place
        return self.copy(2 * d - 1, self.own, self.part(p.shard), p.x_at(d)[1])

    def on_core(self, d):
        p = self.place
        here = self.part(lax.rem(p.x + p.nx - d, p.nx) * 2 + p.core)
        return self.copy(2 * d, here, here, p.other_core())

    def keep(self):
        return pltpu.make_async_copy(self.own, self.part(self.place.shard), self.own_sem)

    def issue(self):
        for d in range(1, self.place.nx):
            self.over_x(d).start()
        self.to_core().start()
        self.keep().start()

    def relay_x(self):
        for d in range(1, self.place.nx):
            self.over_x(d).wait_recv()
            self.on_core(d).start()

    def ready(self):
        self.keep().wait()
        self.to_core().wait_recv()
        for d in range(1, self.place.nx):
            self.on_core(d).wait_recv()

    def sent(self):
        self.to_core().wait_send()
        for d in range(1, self.place.nx):
            self.over_x(d).wait_send()
            self.on_core(d).wait_send()


def attend_pair(query, keys, values_ref, p_ref, bias=None):
    rows, length = query.shape[0], keys.shape[0]
    blocks = rows // 128
    scores = dot_nt(stack_heads(query), keys)
    for head in range(2):
        if bias is not None:
            row_ids, key_ids, window = bias
            table = skew(window[head : head + 1], window.shape[1])
        for b in range(blocks):
            at = head * rows + b * 128
            part = scores[at : at + 128]
            if bias is not None:
                shift = (blocks - 1 - b) * 128
                allowed = key_ids <= row_ids[b * 128 : b * 128 + 128]
                part = jnp.where(allowed, part + table[:, shift : shift + length], MASKED)
            top = jnp.max(part, axis=-1, keepdims=True)
            raised = jnp.exp(part - top)
            share = 1.0 / jnp.sum(raised, axis=-1, keepdims=True)
            p_ref[at : at + 128, :] = (raised * share).astype(BF16)
    return merge_heads(dot(p_ref[...], values_ref[...]))


def bucket_onehot(buckets_ref, offsets_ref, place, rows, length):
    start = length - rows - place.shard * rows
    row = buckets_ref[...].reshape(1, 2 * length - 1)
    offsets_ref[...] = jnp.concatenate([jnp.zeros((1, 1), jnp.int32), row], axis=1)
    window = offsets_ref[:, pl.ds(pl.multiple_of(start, LANES), length + rows)]
    which = lax.broadcasted_iota(jnp.int32, (LANES, length + rows), 0)
    return jnp.where(window == which, 1.0, 0.0)


def forward_kernel(reps, shards, names, *refs):
    r = types.SimpleNamespace(**dict(zip(names, refs)))
    place = Place(reps, shards)
    rows, width = r.tok_in.shape
    length = r.tok.shape[0]
    pairs = width // LANES
    q = width // shards
    part = r.feed_in.shape[1] // width
    own = [r.self_query, r.self_keyval.at[0], r.self_keyval.at[1], r.self_output]
    own += [r.cross_query, r.cross_keyval.at[0], r.cross_keyval.at[1], r.cross_output]
    own += [r.feed_in.at[:, pl.ds(j * width, width)] for j in range(part)]
    own += [r.feed_out.at[pl.ds(j * q, q)] for j in range(part)]
    units = len(own)
    small = SmallSum(place, r.small_held, r.small_landed, r.small_send, r.small_recv)
    gather = Gather(place, r.whole, own, r.feed_out.shape[0], r.w_send, r.w_recv, r.w_own)
    tokens = Spread(place, r.tok_in, r.tok, r.t_send, r.t_recv, r.t_own)
    memories = Spread(place, r.enc_in, r.enc, r.e_send, r.e_recv, r.e_own)

    def weight(u):
        return r.whole[pl.ds(pl.multiple_of(u * width, width), width), :]

    def emit_weights(u, count):
        block = pl.ds(u * width, count * width)
        return pltpu.make_async_copy(r.whole.at[block], r.w_out.at[block], r.out_sem.at[u])

    def emit_kv(i):
        return pltpu.make_async_copy(r.kv.at[i], r.kv_out.at[i], r.out_sem.at[units + i])

    leaving = []

    def emit(src, dst):
        copy = pltpu.make_async_copy(src, dst, r.emit_sem.at[len(leaving)])
        copy.start()
        leaving.append(copy)

    emit_tok = pltpu.make_async_copy(r.tok_t, r.tok_out, r.out_sem.at[units + 4])
    emit_enc = pltpu.make_async_copy(r.enc_t, r.enc_out, r.out_sem.at[units + 5])

    def emit_p(which, i):
        slot = lax.rem(i, 2)
        return pltpu.make_async_copy(r.probs.at[slot], r.p_out.at[which, i], r.p_sem.at[slot])

    def gain(i):
        return r.small_held[2, i : i + 1, :width]

    shard = place.shard
    wide = r.small_held.shape[2]
    sub = lax.broadcasted_iota(jnp.int32, (8, wide), 0)
    padded = lambda a: jnp.concatenate([a, jnp.zeros((a.shape[0], wide - a.shape[1]), F32)], axis=1)
    shifted = lambda a, by: pltpu.roll(padded(a), shard * by, 1)
    ids = r.ids[...].astype(F32)
    gains = [gain_ref[...].astype(F32).reshape(1, q) for gain_ref in (r.norm_self, r.norm_cross, r.norm_feed)]
    mine = jnp.concatenate(gains + [jnp.zeros((5, q), F32)], axis=0)
    mine = jnp.where(sub == 3, 0.0, shifted(mine, q))
    mine = mine + jnp.where(sub == 3, shifted(jnp.broadcast_to(ids, (8, rows)), rows), 0.0)
    table = r.bucket_bias[...].astype(F32).T
    heads, cut = table.shape
    table = jnp.concatenate([table, jnp.zeros((16 - heads, cut), F32)], axis=0)
    r.small_held[0] = jnp.concatenate([mine, shifted(table, cut)], axis=0)
    r.row_ids[...] = jnp.broadcast_to(ids, (8, rows)).T[:, 0:1]
    enter(place)
    small.launch()
    line = [(gather, (u,)) for u in (1, 2, 0, 3)] + [(tokens, ())]
    line += [(gather, (u,)) for u in (5, 6)] + [(memories, ())]
    line += [(gather, (u,)) for u in [4, 7] + list(range(8, units))]
    pumped = [0]
    steps = ("relay_x", "relay_second", "relay_first")

    def issue(at):
        if at < len(line):
            line[at][0].issue(*line[at][1])

    def pump(at):
        for late, name in enumerate(steps):
            if 0 <= at - late < len(line):
                owner, u = line[at - late]
                if hasattr(owner, name):
                    getattr(owner, name)(*u)
            if late == 0:
                issue(at + LINE)

    def pump_to(end):
        while pumped[0] < end:
            pump(pumped[0])
            pumped[0] += 1

    def have(*wanted):
        last = max(line.index((gather, (u,))) for u in wanted)
        pump_to(last + len(steps))
        for u in wanted:
            gather.ready(u)

    for at in range(LINE):
        issue(at)
    small.step(0, 2)
    gathered = small.step(1, 2)
    r.small_out[...] = gathered
    table = gathered[8:24, :LANES].astype(BF16)
    biases = dot(table, bucket_onehot(r.buckets, r.offsets, place, rows, length).astype(BF16))
    for i in range(pairs):
        r.window[i] = biases[2 * i : 2 * i + 2]
    pump_to(5)
    tokens.ready()
    tokens.sent()

    def norm_rows(i, carry):
        at = pl.ds(pl.multiple_of(i * rows, 16), rows)
        values = r.tok[at, :].astype(F32)
        normed = (values * rms_scale(values) * gain(0)).astype(BF16)
        r.tok[at, :] = normed
        r.tok_t[:, pl.ds(pl.multiple_of(i * rows, LANES), rows)] = normed.T
        return carry

    lax.fori_loop(0, length // rows, norm_rows, 0)
    emit_tok.start()

    def project_pair(source, target, base):
        def step(i, carry):
            at = pl.ds(pl.multiple_of(i * rows, 16), rows)
            block = source[at, :]
            for which in range(2):
                out = dot(block, weight(base + which)).astype(BF16)
                for j in range(pairs):
                    r.kv[target + which, j, at, :] = out[:, j * LANES : (j + 1) * LANES]
            return carry

        lax.fori_loop(0, source.shape[0] // rows, step, 0)
        emit_kv(target).start()
        emit_kv(target + 1).start()

    def project_query(normed, u, which):
        out = dot(normed, weight(u)).astype(BF16)
        for j in range(pairs):
            r.queries[which, j] = out[:, j * LANES : (j + 1) * LANES]

    def attention(which, bias, relays):
        def pair(i, carry):
            @pl.when(i >= 2)
            def _():
                emit_p(which, i).wait()

            slot = lax.rem(i, 2)
            more = None
            if bias:
                more = (r.row_ids[...], r.small_held[2, 3:4, :length], r.window[i])
            r.low[which, i] = attend_pair(
                r.queries[which, i],
                r.kv[2 * which, i],
                r.kv.at[2 * which + 1, i],
                r.probs.at[slot],
                more,
            )
            emit_p(which, i).start()
            for step, end in relays:
                @pl.when(i == step)
                def _():
                    pump_to(end)

            return carry

        lax.fori_loop(0, pairs, pair, 0)
        emit_p(which, 0).wait()
        emit_p(which, 1).wait()
        low = [r.low[which, j].astype(BF16) for j in range(pairs)]
        low = jnp.concatenate(low, axis=1)
        r.low_t[which] = low.T
        emit(r.low.at[which], r.low_out.at[which])
        emit(r.low_t.at[which], r.low_t_out.at[which])
        emit(r.queries.at[which], r.q_out.at[which])
        return low

    have(1, 2)
    project_pair(r.tok, 0, 1)
    have(0)
    emit_weights(0, 3).start()
    mine = pl.ds(pl.multiple_of(place.shard * rows, 16), rows)
    project_query(r.tok[mine, :], 0, 0)
    low = attention(0, True, SELF_PUMPS)
    have(3)
    r.first[...] = r.tok_in[...].astype(F32) + dot(low, weight(3))
    emit(r.first, r.first_out)
    pump_to(8)
    memories.ready()

    def turn_rows(i, carry):
        at = pl.ds(pl.multiple_of(i * rows, LANES), rows)
        r.enc_t[:, at] = r.enc[at, :].T
        return carry

    lax.fori_loop(0, length // rows, turn_rows, 0)
    emit_enc.start()
    have(5, 6)
    project_pair(r.enc, 2, 5)
    have(4)
    first = r.first[...]
    normed = (first * rms_scale(first) * gain(1)).astype(BF16)
    r.normed2_t[...] = normed.T
    emit(r.normed2_t, r.normed2_out)
    project_query(normed, 4, 1)
    low = attention(1, False, CROSS_PUMPS)
    have(7)
    emit_weights(3, 5).start()
    r.second[...] = r.first[...] + dot(low, weight(7))
    emit(r.second, r.second_out)
    second = r.second[...]
    normed = (second * rms_scale(second) * gain(2)).astype(BF16)
    r.normed[...] = normed
    r.normed3_t[...] = normed.T
    emit(r.normed3_t, r.normed3_out)
    for j in range(part):
        have(8 + j)
        value, slope = gelu_parts(dot(r.normed[...], weight(8 + j)))
        value = value.astype(BF16)
        r.hidden[j] = value
        r.hidden_t[j * width : (j + 1) * width, :] = value.T
        r.slope[j] = slope
        block = pl.ds(j * width, width)
        emit(r.hidden_t.at[block], r.hidden_out.at[block])
        emit(r.slope.at[j], r.slope_out.at[j])
    have(*range(8 + part, units))
    emit_weights(8, units - 8).start()
    total = second
    for j in range(part):
        total = total + dot(r.hidden[j], weight(8 + part + j))
    r.result[...] = total.astype(BF16)
    for u in range(units):
        gather.sent(u)
    memories.sent()
    small.sent(2)
    for u, count in ((0, 3), (3, 5), (8, units - 8)):
        emit_weights(u, count).wait()
    for i in range(4):
        emit_kv(i).wait()
    emit_tok.wait()
    emit_enc.wait()
    for copy in leaving:
        copy.wait()


def forward(tokens, encoded, ids, buckets, gains, bucket_bias, shards_of, reps, shards):
    rows, width = tokens.shape
    length, memory = rows * shards, encoded.shape[0] * shards
    nx = shards // 2
    feed_in, feed_out = shards_of[-2:]
    hidden = feed_in.shape[1]
    units = 8 + 2 * (hidden // width)
    pairs = width // LANES
    small = (24, max(length, width))
    kept = lambda *shape, dtype=BF16: (pl.BlockSpec(memory_space=pl.ANY), jax.ShapeDtypeStruct(shape, dtype))
    near = lambda *shape, dtype=F32: (pl.BlockSpec(memory_space=pltpu.VMEM), jax.ShapeDtypeStruct(shape, dtype))
    outs = dict(
        result=near(rows, width, dtype=BF16),
        small_out=near(*small),
        first_out=kept(rows, width, dtype=F32),
        second_out=kept(rows, width, dtype=F32),
        low_out=kept(2, pairs, rows, LANES, dtype=F32),
        low_t_out=kept(2, width, rows),
        q_out=kept(2, pairs, rows, LANES),
        normed2_out=kept(width, rows),
        normed3_out=kept(width, rows),
        hidden_out=kept(hidden, rows),
        slope_out=kept(hidden // width, rows, width, dtype=F32),
        w_out=kept(units * width, width),
        kv_out=kept(4, pairs, length, LANES),
        tok_out=kept(width, length),
        enc_out=kept(width, memory),
        p_out=kept(2, pairs, 2 * rows, length),
    )
    scratch = dict(
        whole=pltpu.VMEM((units * width, width), BF16),
        tok=pltpu.VMEM((length, width), BF16),
        enc=pltpu.VMEM((memory, width), BF16),
        kv=pltpu.VMEM((4, pairs, length, LANES), BF16),
        window=pltpu.VMEM((pairs, 2, length + rows), F32),
        row_ids=pltpu.VMEM((rows, 1), F32),
        offsets=pltpu.VMEM((1, 2 * length), jnp.int32),
        probs=pltpu.VMEM((2, 2 * rows, length), BF16),
        first=pltpu.VMEM((rows, width), F32),
        second=pltpu.VMEM((rows, width), F32),
        low=pltpu.VMEM((2, pairs, rows, LANES), F32),
        low_t=pltpu.VMEM((2, width, rows), BF16),
        queries=pltpu.VMEM((2, pairs, rows, LANES), BF16),
        normed2_t=pltpu.VMEM((width, rows), BF16),
        normed3_t=pltpu.VMEM((width, rows), BF16),
        hidden_t=pltpu.VMEM((hidden, rows), BF16),
        slope=pltpu.VMEM((hidden // width, rows, width), F32),
        emit_sem=pltpu.SemaphoreType.DMA((10 + 2 * (hidden // width),)),
        normed=pltpu.VMEM((rows, width), BF16),
        hidden=pltpu.VMEM((hidden // width, rows, width), BF16),
        tok_t=pltpu.VMEM((width, length), BF16),
        enc_t=pltpu.VMEM((width, memory), BF16),
        p_sem=pltpu.SemaphoreType.DMA((2,)),
        out_sem=pltpu.SemaphoreType.DMA((units + 6,)),
    )
    scratch.update(zip(("small_held", "small_landed", "small_send", "small_recv"), SmallSum.scratch(nx, reps // 4, small)))
    scratch.update(zip(("w_send", "w_recv", "w_own"), Gather.scratch(units, nx)))
    scratch.update(zip(("t_send", "t_recv", "t_own"), Spread.scratch(nx)))
    scratch.update(zip(("e_send", "e_recv", "e_own"), Spread.scratch(nx)))
    shard_names = ["self_query", "self_keyval", "self_output", "cross_query", "cross_keyval", "cross_output", "feed_in", "feed_out"]
    near_names = ["tok_in", "enc_in", "ids", "buckets", "norm_self", "norm_cross", "norm_feed", "bucket_bias"]
    names = near_names + shard_names + list(outs) + list(scratch)
    made = pl.pallas_call(
        functools.partial(forward_kernel, reps, shards, tuple(names)),
        in_specs=[pl.BlockSpec(memory_space=pltpu.VMEM)] * 8 + [pl.BlockSpec(memory_space=pl.ANY)] * 8,
        out_specs=[spec for spec, _ in outs.values()],
        out_shape=[shape for _, shape in outs.values()],
        scratch_shapes=list(scratch.values()),
        compiler_params=pltpu.CompilerParams(
            collective_id=2, has_side_effects=True, vmem_limit_bytes=FUSED_LIMIT
        ),
    )(tokens, encoded, ids, buckets, *gains, bucket_bias, *shards_of)
    return types.SimpleNamespace(**dict(zip(outs, made)))


class RowSum:
    def __init__(self, place, parts, recv_a, recv_b, send, recv):
        self.place, self.parts, self.recv_a, self.recv_b = place, parts, recv_a, recv_b
        self.send, self.recv = send, recv

    @staticmethod
    def scratch(nx, width, rows):
        return [
            pltpu.VMEM((2, nx, width, rows), BF16),
            pltpu.VMEM((nx, width, rows), BF16),
            pltpu.VMEM((nx - 1, width, rows), BF16),
            pltpu.SemaphoreType.DMA((nx,)),
            pltpu.SemaphoreType.DMA((nx,)),
        ]

    def copy(self, which, src, dst, device):
        return remote(src, dst, self.send.at[which], self.recv.at[which], device)

    def to_core(self):
        p = self.place
        return self.copy(0, self.parts.at[1 - p.core], self.recv_a, p.other_core())

    def over_x(self, d):
        x, device = self.place.x_at(d)
        return self.copy(d, self.recv_a.at[x], self.recv_b.at[d - 1], device)

    def begin(self, total):
        rows = self.parts.shape[3]
        for s in range(2 * self.place.nx):
            self.parts[s % 2, s // 2] = total[:, s * rows : (s + 1) * rows].astype(BF16)
        self.to_core().start()

    def pass_x(self):
        self.to_core().wait_recv()
        self.recv_a[...] = added(self.recv_a[...], self.parts[self.place.core]).astype(BF16)
        for d in range(1, self.place.nx):
            self.over_x(d).start()

    def finish(self):
        p = self.place
        for d in range(1, p.nx):
            self.over_x(d).wait_recv()
        return added(self.recv_a[p.x], *[self.recv_b[d] for d in range(p.nx - 1)]).astype(F32)

    def sent(self):
        for d in range(1, self.place.nx):
            self.over_x(d).wait_send()


def attend_back_pair(query, keys, values, p_ref, output, grad, ds_ref, width=None):
    rows, length = query.shape[0], keys.shape[0]
    blocks = rows // 128
    grads, queries = stack_heads(grad), stack_heads(query)
    delta_wide = grad.astype(F32) * output
    d_weights = dot_nt(grads, values)
    windows = []
    for head in range(2):
        delta = jnp.sum(delta_wide * own_lanes(head == 0), axis=-1, keepdims=True)
        total = None
        for b in range(blocks):
            at = head * rows + b * 128
            part = p_ref[at : at + 128, :].astype(F32) * (
                d_weights[at : at + 128] - delta[b * 128 : b * 128 + 128]
            )
            ds_ref[at : at + 128, :] = part.astype(BF16)
            if width is not None:
                shift = (blocks - 1 - b) * 128
                pieces = [jnp.zeros((128, shift), F32)] if shift else []
                pieces.append(part)
                if width - shift - length:
                    pieces.append(jnp.zeros((128, width - shift - length), F32))
                placed = jnp.concatenate(pieces, axis=1)
                total = placed if total is None else total + placed
        if width is not None:
            windows.append(unskew(total, width))
    d_query = merge_heads(dot(ds_ref[...], keys)).astype(BF16)
    d_keys = dot(queries.T, ds_ref[...]).astype(BF16)
    d_values = dot(grads.T, p_ref[...]).astype(BF16)
    return d_query, d_keys, d_values, windows


BROUGHT = ("hidden_t", "normed3_t", "second", "low_t", "queries", "low", "first", "normed2_t")
REDUCTION = ("_parts", "_x", "_y", "_low", "_high", "_send", "_recv", "_own")


def late_units(units):
    return [n for n in LATE if n < units]


def backward_kernel(reps, shards, names, *refs):
    r = types.SimpleNamespace(**dict(zip(names, refs)))
    place = Place(reps, shards)
    rows, width = r.cotangent.shape
    length = r.enc_t.shape[1]
    pairs = width // LANES
    q = width // shards
    part = r.hidden_t.shape[0] // width
    units = 8 + 2 * part
    late = late_units(units)
    order = [n for n in range(units) if n not in late]
    reductions = [
        Reduction(place, x_first, names, r.fin, *(getattr(r, name + end) for end in REDUCTION))
        for x_first, names, name in ((True, order, "a"), (False, late, "b"))
    ]
    stages = len(reductions[0].copies)

    def owner(n):
        return (reductions[1], late.index(n)) if n in late else (reductions[0], order.index(n))

    small = SmallSum(place, r.small_held, r.small_landed, r.small_send, r.small_recv)
    sum_memory = RowSum(place, r.m_parts, r.m_a, r.m_b, r.m_send, r.m_recv)
    sum_tokens = RowSum(place, r.m_parts, r.t_a, r.t_b, r.t_send, r.t_recv)

    def gain(i):
        return r.gains[i : i + 1, :width]

    def load_weight(u, slot):
        block = pl.ds(u * width, width)
        return pltpu.make_async_copy(r.w_in.at[block], r.w.at[slot], r.w_sem.at[slot])

    ticks = [0]

    def slot_done(slot):
        while ticks[0] < TICKS.get(slot, 0):
            advance(ticks[0])
            ticks[0] += 1

    def load_slope(j):
        slot = j % 2
        return pltpu.make_async_copy(r.slope.at[j], r.slopes.at[slot], r.s_sem.at[slot])

    def load_kv(i, slot):
        return pltpu.make_async_copy(r.kv_in.at[i], r.kv.at[slot], r.kv_sem.at[slot])

    def load_p(which, i):
        slot = lax.rem(i, 2)
        return pltpu.make_async_copy(r.p_in.at[which, i], r.probs.at[slot], r.p_sem.at[slot])

    def load_t(source, which):
        return pltpu.make_async_copy(source, r.rows_t, r.t_sem.at[which])

    def away(n):
        return r.made.at[n % SLOTS, 1 - place.core]

    def fill(n, value):
        slot = n % SLOTS
        rest = value.shape[0] // shards
        half = width // 2
        for s in range(shards):
            for h in range(2):
                r.made[slot, s % 2, s // 2, h] = value[
                    s * rest : (s + 1) * rest, h * half : (h + 1) * half
                ].astype(BF16)
        red, u = owner(n)
        red.begin(u, away(n))

    def left(n):
        red, u = owner(n)
        red.over_core(u, away(n))[0].wait_send()

    def free(n):
        if n >= SLOTS:
            left(n - SLOTS)

    done_stages = {n: 0 for n in range(units)}
    started = [0]

    def set_out(end):
        while started[0] < min(end, len(order)):
            red, u = owner(order[started[0]])
            red.start(u, 0)
            started[0] += 1

    def take(n):
        red, u = owner(n)
        red.collect(u, away(n), r.made.at[n % SLOTS, place.core])
        if n in late:
            red.start(u, 0)
        elif order.index(n) < AHEAD:
            set_out(order.index(n) + 1)

    def move(n, upto):
        red, u = owner(n)
        while done_stages[n] < min(upto, stages):
            red.step(u, done_stages[n])
            done_stages[n] += 1

    def advance(t):
        for back in range(stages):
            at = t - back
            if 0 <= at < len(order):
                move(order[at], back + 1)
            if back == 0:
                set_out(t + 1 + (AHEAD if t < len(order) - CLOSE else 1))
        for i, n in enumerate(late):
            move(n, t - LATE_START[i])

    def bring(name):
        source, sem = getattr(r, name + "_in"), r.bring_sem.at[BROUGHT.index(name)]
        return pltpu.make_async_copy(source, getattr(r, name), sem)

    load_slope(0).start()
    for slot, u in enumerate((8, 8 + part)):
        load_weight(u, slot).start()
    for name in BROUGHT[:3]:
        bring(name).start()
    enter(place)
    for name in BROUGHT[3:]:
        bring(name).start()
    for slot in range(2):
        load_kv(2 + slot, slot).start()
        load_p(1, slot).start()
    load_t(r.enc_t, 0).start()
    r.acc[...] = jnp.zeros((rows, width), F32)

    bring("hidden_t").wait()
    for m in range(part):
        n = m
        free(n)
        value = jnp.concatenate(
            [
                dot(r.hidden_t[s * width + m * q : s * width + (m + 1) * q, :], r.cotangent[...])
                for s in range(shards)
            ],
            axis=0,
        )
        fill(n, value)
        if m >= 1:
            take(n - 1)
    take(part - 1)
    for j in range(part):
        slot = 2 * (j % 2)
        load_weight(8, slot).wait()
        load_weight(8 + part, slot + 1).wait()
        load_slope(j).wait()
        if j + 1 < part:
            load_slope(j + 1).start()
            load_weight(8 + j + 1, 2 - slot).start()
            load_weight(8 + part + j + 1, 3 - slot).start()
        if j == 0:
            bring("normed3_t").wait()
        grad_hidden = dot_nt(r.cotangent[...], r.w[slot + 1])
        grad = (grad_hidden * r.slopes[j % 2]).astype(BF16)
        free(part + j)
        fill(part + j, dot(r.normed3_t[...], grad))
        r.acc[...] += dot_nt(grad, r.w[slot])
        if j >= 1:
            take(part + j - 1)
    for slot, u in ((0, 7), (1, 5), (2, 6), (3, 4)):
        load_weight(u, slot).start()
    bring("second").wait()
    back, d_gain3 = rms_back(r.second[...], gain(2), r.acc[...])
    r.grad[...] = r.cotangent[...].astype(F32) + back
    take(2 * part - 1)
    slot_done(0)

    def attention(which, fold, first_slot):
        def pair(i, carry):
            slot = lax.rem(i, 2)
            load_p(which, i).wait()
            d_query, d_keys, d_values, windows = attend_back_pair(
                r.queries[which, i],
                r.kv[0, i],
                r.kv[1, i],
                r.probs.at[slot],
                r.low[which, i],
                r.grad_att[i],
                r.ds,
                length + rows if fold else None,
            )
            r.d_query[i] = d_query
            at = pl.ds(pl.multiple_of(i * LANES, LANES), LANES)
            r.dk_t[at, :] = d_keys
            r.dv_t[at, :] = d_values
            if fold:
                r.d_window[i] = jnp.concatenate(windows, axis=0)

            @pl.when(i + 2 < pairs)
            def _():
                load_p(which, i + 2).start()

            for step in range(pairs):
                if first_slot + step in TICKS:
                    @pl.when(i == step)
                    def _():
                        slot_done(first_slot + step)

            return carry

        lax.fori_loop(0, pairs, pair, 0)

    def spread_grad(value):
        for i in range(pairs):
            r.grad_att[i] = value[:, i * LANES : (i + 1) * LANES].astype(BF16)

    def joined_query():
        return jnp.concatenate([r.d_query[i] for i in range(pairs)], axis=1)

    for name in BROUGHT[3:]:
        bring(name).wait()
    n = 2 * part
    grad_low = r.grad[...].astype(BF16)
    free(n)
    fill(n, dot(r.low_t[1], grad_low))
    load_weight(7, 0).wait()
    spread_grad(dot_nt(grad_low, r.w[0]))
    load_weight(3, 0).start()
    take(n)
    for slot in range(2):
        load_kv(2 + slot, slot).wait()
    attention(1, False, 1)
    for slot in range(2):
        load_kv(slot, slot).start()
        load_p(0, slot).start()
    load_weight(5, 1).wait()
    load_weight(6, 2).wait()
    sum_memory.begin(dot(r.w[1], r.dk_t[...]) + dot(r.w[2], r.dv_t[...]))
    load_weight(1, 1).start()
    load_weight(2, 2).start()
    load_t(r.enc_t, 0).wait()
    free(n + 1)
    fill(n + 1, dot_nt(r.rows_t[...], r.dk_t[...]))
    sum_memory.pass_x()
    free(n + 2)
    fill(n + 2, dot_nt(r.rows_t[...], r.dv_t[...]))
    take(n + 1)
    slot_done(7)
    load_t(r.tok_t, 1).start()
    d_query = joined_query()
    load_weight(4, 3).wait()
    back, d_gain2 = rms_back(r.first[...], gain(1), dot_nt(d_query, r.w[3]))
    load_weight(0, 3).start()
    free(n + 3)
    fill(n + 3, dot(r.normed2_t[...], d_query))
    take(n + 2)
    r.grad[...] = r.grad[...] + back
    slot_done(8)

    grad_low = r.grad[...].astype(BF16)
    take(n + 3)
    free(n + 4)
    fill(n + 4, dot(r.low_t[0], grad_low))
    load_weight(3, 0).wait()
    spread_grad(dot_nt(grad_low, r.w[0]))
    take(n + 4)
    for slot in range(2):
        load_kv(slot, slot).wait()
    attention(0, True, 9)
    load_weight(1, 1).wait()
    load_weight(2, 2).wait()
    sum_memory.to_core().wait_send()
    sum_tokens.begin(dot(r.w[1], r.dk_t[...]) + dot(r.w[2], r.dv_t[...]))
    load_t(r.tok_t, 1).wait()
    free(n + 5)
    fill(n + 5, dot_nt(r.rows_t[...], r.dk_t[...]))
    sum_tokens.pass_x()
    free(n + 6)
    fill(n + 6, dot_nt(r.rows_t[...], r.dv_t[...]))
    take(n + 5)
    r.d_memory[...] = sum_memory.finish().T
    slot_done(15)
    d_query = joined_query()
    free(n + 7)
    mine = pl.ds(pl.multiple_of(place.shard * rows, LANES), rows)
    fill(n + 7, dot(r.rows_t[:, mine], d_query))
    take(n + 6)
    load_weight(0, 3).wait()
    r.acc[...] = dot_nt(d_query, r.w[3])
    windows = jnp.concatenate([r.d_window[i] for i in range(pairs)], axis=0)
    d_table = lax.dot_general(
        windows,
        bucket_onehot(r.buckets, r.offsets, place, rows, length),
        (((1,), (1,)), ((), ())),
        precision=lax.Precision.HIGHEST,
        preferred_element_type=F32,
    )
    take(n + 7)
    slot_done(16)
    for t in range(ticks[0], len(order) + stages):
        advance(t)
        if t == LAST_SUM:
            values = r.tokens[...].astype(F32)
            total = r.acc[...] + sum_tokens.finish().T
            back, d_gain1 = rms_back(values, gain(0), total)
            r.d_tokens[...] = r.grad[...] + back
            r.small_held[0] = jnp.zeros(r.small_held.shape[1:], F32)
            for i, d_gain in enumerate((d_gain1, d_gain2, d_gain3)):
                r.small_held[0, i : i + 1, :width] = d_gain
            r.small_held[0, 8 : 8 + 2 * pairs, :LANES] = d_table
            small.launch()
        elif LAST_SUM < t < LAST_SUM + 6:
            small.step(t - LAST_SUM - 1)
    for n in range(units):
        move(n, stages)
    r.small_out[...] = r.small_held[5]
    for n in range(units):
        if n >= units - SLOTS:
            left(n)
        red, u = owner(n)
        red.sent(u)
    small.sent()
    sum_tokens.to_core().wait_send()
    sum_memory.sent()
    sum_tokens.sent()


def backward(tokens, cotangent, buckets, held, reps, shards):
    rows, width = tokens.shape
    length = held.enc_out.shape[1]
    nx, nh = shards // 2, reps // 4
    pairs = width // LANES
    q, half = width // shards, width // 2
    units = held.w_out.shape[0] // width
    small = (24, width)
    kept = pl.BlockSpec(memory_space=pl.ANY)
    near = pl.BlockSpec(memory_space=pltpu.VMEM)
    arrays = (held.hidden_out, held.normed3_out, held.second_out, held.low_t_out)
    arrays += (held.q_out, held.low_out, held.first_out, held.normed2_out)
    brought = dict(zip(BROUGHT, arrays))
    ins = dict(
        tokens=(near, tokens),
        cotangent=(near, cotangent),
        buckets=(near, buckets),
        gains=(near, held.small_out),
        **{name + "_in": (kept, array) for name, array in brought.items()},
        slope=(kept, held.slope_out),
        tok_t=(kept, held.tok_out),
        enc_t=(kept, held.enc_out),
        w_in=(kept, held.w_out),
        kv_in=(kept, held.kv_out),
        p_in=(kept, held.p_out),
    )
    outs = dict(
        d_tokens=(near, jax.ShapeDtypeStruct((rows, width), F32)),
        d_memory=(near, jax.ShapeDtypeStruct((rows, width), F32)),
        small_out=(near, jax.ShapeDtypeStruct(small, F32)),
        fin=(kept, jax.ShapeDtypeStruct((units, 2, q, half), BF16)),
    )
    scratch = {name: pltpu.VMEM(array.shape, array.dtype) for name, array in brought.items()}
    scratch.update(
        bring_sem=pltpu.SemaphoreType.DMA((len(brought),)),
        w=pltpu.VMEM((4, width, width), BF16),
        kv=pltpu.VMEM((2, pairs, length, LANES), BF16),
        probs=pltpu.VMEM((2, 2 * rows, length), BF16),
        ds=pltpu.VMEM((2 * rows, length), BF16),
        rows_t=pltpu.VMEM((width, length), BF16),
        dk_t=pltpu.VMEM((width, length), BF16),
        dv_t=pltpu.VMEM((width, length), BF16),
        d_query=pltpu.VMEM((pairs, rows, LANES), BF16),
        grad_att=pltpu.VMEM((pairs, rows, LANES), BF16),
        offsets=pltpu.VMEM((1, 2 * length), jnp.int32),
        d_window=pltpu.VMEM((pairs, 2, length + rows), F32),
        acc=pltpu.VMEM((rows, width), F32),
        grad=pltpu.VMEM((rows, width), F32),
        made=pltpu.VMEM((SLOTS, 2, nx, 2, q, half), BF16),
        slopes=pltpu.VMEM((2, rows, width), F32),
        s_sem=pltpu.SemaphoreType.DMA((2,)),
        w_sem=pltpu.SemaphoreType.DMA((4,)),
        kv_sem=pltpu.SemaphoreType.DMA((2,)),
        p_sem=pltpu.SemaphoreType.DMA((2,)),
        t_sem=pltpu.SemaphoreType.DMA((2,)),
    )
    counts = {"a": units - len(late_units(units)), "b": len(late_units(units))}
    for name, count in counts.items():
        made_for = Reduction.scratch(count, name == "a", nx, nh, q, half)
        scratch.update(zip((name + end for end in REDUCTION), made_for))
    scratch.update(
        zip(("small_held", "small_landed", "small_send", "small_recv"), SmallSum.scratch(nx, nh, small))
    )
    for name in "mt":
        keys = (name + end for end in ("_parts", "_a", "_b", "_send", "_recv"))
        scratch.update(zip(keys, RowSum.scratch(nx, width, rows)))
    del scratch["t_parts"]
    names = tuple(list(ins) + list(outs) + list(scratch))
    made = pl.pallas_call(
        functools.partial(backward_kernel, reps, shards, names),
        in_specs=[spec for spec, _ in ins.values()],
        out_specs=[spec for spec, _ in outs.values()],
        out_shape=[shape for _, shape in outs.values()],
        scratch_shapes=list(scratch.values()),
        compiler_params=pltpu.CompilerParams(
            collective_id=3, has_side_effects=True, vmem_limit_bytes=FUSED_LIMIT
        ),
    )(*[value for _, value in ins.values()])
    return types.SimpleNamespace(**dict(zip(outs, made)))


def finish_kernel(squares, shards, names, *refs):
    r = types.SimpleNamespace(**dict(zip(names, refs)))
    step = pl.program_id(0)
    shard = lax.axis_index("shard")
    whole = lambda ref: jnp.concatenate([ref[0, 0], ref[0, 1]], axis=1).astype(F32)
    r.feed_in[...] = whole(r.fin_in)
    r.feed_out[...] = whole(r.fin_out)
    for source, group in zip((r.fin_cross, r.fin_self), squares):
        value = whole(source)
        for name, first, count in group:
            out = getattr(r, name)

            @pl.when((step >= first) & (step < first + count))
            def _():
                out[...] = value.reshape(out.shape)

    r.d_tokens[...] = r.tokens_in[...]
    r.d_memory[...] = r.memory_in[...]
    r.result[...] = r.result_in[...]

    @pl.when(step == 0)
    def _():
        small = r.small[...]
        width = small.shape[1]
        mine = lambda by: pltpu.roll(small, lax.rem(width - shard * by, width), 1)
        gains = mine(width // shards)
        for i, out in enumerate((r.norm_self, r.norm_cross, r.norm_feed)):
            out[...] = gains[i : i + 1, : width // shards].reshape(out.shape)
        cut, heads = r.bucket_bias.shape
        r.bucket_bias[...] = mine(cut)[8:24, :LANES].T[:cut, :heads]


def finish(made, result, table_shape, shards):
    units, _, q, half = made.fin.shape
    rows, width = made.d_tokens.shape
    steps = units // 4
    still = lambda *shape: pl.BlockSpec(shape, lambda n: (0,) * len(shape))
    line = pl.BlockSpec((rows // steps, width), lambda n: (n, 0))
    unit = lambda group: pl.BlockSpec((1, 2, q, half), lambda n: (group * steps + n, 0, 0, 0))
    pair = lambda first: pl.BlockSpec((1, q, width), lambda n: (jnp.where(n <= first, 0, 1), 0, 0))
    squares = (
        (("cross_output", 0, 1), ("cross_keyval", 1, 2), ("cross_query", 3, 1)),
        (("self_output", 0, 1), ("self_keyval", 1, 2), ("self_query", 3, 1)),
    )
    square = ((q, width), still(q, width))
    outs = dict(
        feed_in=((q, steps * width), pl.BlockSpec((q, width), lambda n: (0, n))),
        feed_out=((steps * q, width), pl.BlockSpec((q, width), lambda n: (n, 0))),
        cross_output=square,
        cross_keyval=((2, q, width), pair(1)),
        cross_query=square,
        self_output=square,
        self_keyval=((2, q, width), pair(1)),
        self_query=square,
        d_tokens=((rows, width), line),
        d_memory=((rows, width), line),
        result=((rows, width), line),
        norm_self=((q,), still(q)),
        norm_cross=((q,), still(q)),
        norm_feed=((q,), still(q)),
        bucket_bias=(table_shape, still(*table_shape)),
    )
    names = ("fin_in", "fin_out", "fin_cross", "fin_self", "tokens_in", "memory_in", "result_in", "small")
    done = pl.pallas_call(
        functools.partial(finish_kernel, squares, shards, names + tuple(outs)),
        grid=(steps,),
        in_specs=[unit(1), unit(0), unit(2), unit(3), line, line, line, still(*made.small_out.shape)],
        out_specs=[spec for _, spec in outs.values()],
        out_shape=[
            jax.ShapeDtypeStruct(shape, BF16 if name == "result" else F32)
            for name, (shape, _) in outs.items()
        ],
        compiler_params=pltpu.CompilerParams(vmem_limit_bytes=VMEM_LIMIT),
    )(*[made.fin] * 4, made.d_tokens, made.d_memory, result, made.small_out)
    return types.SimpleNamespace(**dict(zip(outs, done)))


def tiles_evenly(reps, shards, width):
    if reps % 4 or shards % 2 or width % shards:
        return False
    return (width // shards) % (8 * reps) == 0 and width % (4 * HD) == 0


def layer(
    tokens,
    encoded,
    block_ids,
    buckets,
    cotangent,
    norm_self,
    self_query,
    self_keyval,
    self_output,
    bucket_bias,
    norm_cross,
    cross_query,
    cross_keyval,
    cross_output,
    norm_feed,
    feed_in,
    feed_out,
):
    groups, positions, model_width = tokens.shape
    reps, shards = lax.axis_size("rep"), lax.axis_size("shard")
    length = (buckets.shape[0] + 1) // 2
    memory_local = encoded.shape[1]
    row_anchor = lax.axis_index("shard") * positions
    heads, bucket_count = bucket_bias.shape[0], bucket_bias.shape[1] * shards
    window_width = length + positions
    fused = tiles_evenly(reps, shards, model_width) and encoded.shape == tokens.shape
    fused = fused and feed_out.shape[0] == model_width
    fused = fused and feed_in.shape[1] == 4 * model_width and positions % LANES == 0
    if fused:
        gains = (norm_self, norm_cross, norm_feed)
        matrices = (self_query, self_keyval, self_output, cross_query, cross_keyval, cross_output)
        matrices += (feed_in, feed_out)
        held = forward(
            tokens[0], encoded[0], block_ids, buckets, gains, bucket_bias.T, matrices, reps, shards
        )
        made = backward(tokens[0], cotangent[0], buckets, held, reps, shards)
        out = finish(made, held.result, bucket_bias.T.shape, shards)
        return (
            out.result[None],
            out.d_tokens[None],
            out.d_memory[None],
            out.norm_self,
            out.self_query,
            out.self_keyval,
            out.self_output,
            out.bucket_bias.T,
            out.norm_cross,
            out.cross_query,
            out.cross_keyval,
            out.cross_output,
            out.norm_feed,
            out.feed_in,
            out.feed_out,
        )

    inputs = tokens[0].astype(F32)
    encoded_whole = gather(encoded[0])
    ids_whole = gather(block_ids[0])
    gains = gather(jnp.stack([norm_self, norm_cross, norm_feed]), 1).astype(F32)
    gain_first, gain_second, gain_third = gains[0:1], gains[1:2], gains[2:3]
    query_first, keyval_first, output_first, table = (
        gather(self_query),
        gather(self_keyval, 1),
        gather(self_output),
        gather(bucket_bias, 1),
    )
    query_second, keyval_second, output_second = (
        gather(cross_query),
        gather(cross_keyval, 1),
        gather(cross_output),
    )
    inner, outer = gather(feed_in), gather(feed_out)

    window_buckets = lax.dynamic_slice_in_dim(
        jnp.pad(buckets, (1, 0)), length - row_anchor - positions, window_width
    )
    onehot = window_buckets[None, :] == jnp.arange(bucket_count, dtype=jnp.int32)[:, None]
    window = dot(table, onehot.astype(BF16)).reshape(heads // 2, 2, window_width)

    normed_first = (inputs * rms_scale(inputs) * gain_first).astype(BF16)
    normed_whole = gather(normed_first)
    query = dot(normed_first, query_first).astype(BF16)
    keys = dot(normed_whole, keyval_first[0]).astype(BF16)
    values = dot(normed_whole, keyval_first[1]).astype(BF16)
    attended, weights = attend(
        query, keys, values, (block_ids[0][:, None], ids_whole[None, :], window)
    )
    low_first = attended.astype(BF16)
    first = inputs + dot(low_first, output_first)

    memory_keys = dot(encoded_whole, keyval_second[0]).astype(BF16)
    memory_values = dot(encoded_whole, keyval_second[1]).astype(BF16)
    normed_second = (first * rms_scale(first) * gain_second).astype(BF16)
    query_cross = dot(normed_second, query_second).astype(BF16)
    attended_cross, weights_cross = attend(query_cross, memory_keys, memory_values)
    low_second = attended_cross.astype(BF16)
    second = first + dot(low_second, output_second)

    normed_third = (second * rms_scale(second) * gain_third).astype(BF16)
    preact = dot(normed_third, inner)
    value, slope = gelu_parts(preact)
    hidden = value.astype(BF16)
    result = (second + dot(hidden, outer)).astype(BF16)

    grad_result = cotangent[0]
    d_outer = dot_tn(hidden, grad_result)
    grad_preact = (dot_nt(grad_result, outer) * slope).astype(BF16)
    d_inner = dot_tn(normed_third, grad_preact)
    back, d_gain_third = rms_back(second, gain_third, dot_nt(grad_preact, inner))
    grad_second = grad_result.astype(F32) + back

    grad_second_low = grad_second.astype(BF16)
    d_output_second = dot_tn(low_second, grad_second_low)
    grad_att = dot_nt(grad_second_low, output_second).astype(BF16)
    d_query, d_keys, d_values = attend_back(
        query_cross, memory_keys, memory_values, weights_cross, attended_cross, grad_att
    )
    d_keyval_second = jnp.stack(
        [dot_tn(encoded_whole, d_keys), dot_tn(encoded_whole, d_values)]
    )
    d_memory = scatter(dot_nt(d_keys, keyval_second[0]) + dot_nt(d_values, keyval_second[1]))
    d_query_second = dot_tn(normed_second, d_query)
    back, d_gain_second = rms_back(first, gain_second, dot_nt(d_query, query_second))
    grad_first = grad_second + back

    grad_first_low = grad_first.astype(BF16)
    d_output_first = dot_tn(low_first, grad_first_low)
    grad_att = dot_nt(grad_first_low, output_first).astype(BF16)
    d_query, d_keys, d_values, d_window = attend_back(
        query, keys, values, weights, attended, grad_att, window.shape
    )
    d_table = lax.dot_general(
        d_window.reshape(heads, window_width),
        onehot.astype(F32),
        (((1,), (1,)), ((), ())),
        precision=lax.Precision.HIGHEST,
    )
    d_keyval_first = jnp.stack([dot_tn(normed_whole, d_keys), dot_tn(normed_whole, d_values)])
    grad_normed = scatter(
        dot_nt(d_keys, keyval_first[0]) + dot_nt(d_values, keyval_first[1])
    ).astype(F32) + dot_nt(d_query, query_first)
    d_query_first = dot_tn(normed_first, d_query)
    back, d_gain_first = rms_back(inputs, gain_first, grad_normed)
    d_inputs = grad_first + back

    gains = [d_gain_first, d_gain_second, d_gain_third]
    squares = [d_query_first, d_output_first, d_query_second, d_output_second]
    pairs = [d_keyval_first, d_keyval_second]
    total = lambda a, axis=0: lax.psum(scatter(a, axis), "rep").astype(F32)
    gains = [total(gain[0]) for gain in gains]
    squares = [total(square) for square in squares]
    pairs = [total(pair, 1) for pair in pairs]
    d_table, d_inner, d_outer = total(d_table, 1), total(d_inner), total(d_outer)
    totals = (gains[0], squares[0], pairs[0], squares[1], d_table)
    totals += (gains[1], squares[2], pairs[1], squares[3], gains[2], d_inner, d_outer)
    return (result[None], d_inputs[None], d_memory.astype(F32)[None]) + totals


def solution(mesh):
    rows, line = P("rep", "shard", None), P("shard")
    matrix, pair, table = P("shard", None), P(None, "shard", None), P(None, "shard")
    weights = (line, matrix, pair, matrix, table, line, matrix, pair, matrix, line, matrix, matrix)
    return jax.shard_map(
        layer,
        mesh=mesh,
        in_specs=(rows, rows, P("rep", "shard"), P(), rows) + weights,
        out_specs=(rows, rows, rows) + weights,
        check_vma=False,
    )
```

```python
import functools
import types

import jax
import jax.numpy as jnp
from jax import lax
from jax.experimental import pallas as pl
from jax.experimental.pallas import tpu as pltpu
from jax.sharding import PartitionSpec as P

H = 12
HD = 64
LANES = 2 * HD
EPSILON = 1e-06
MASKED = -1e30
F32 = jnp.float32
BF16 = jnp.bfloat16
VMEM_LIMIT = 56 * 2**20
FUSED_LIMIT = 62 * 2**20
AHEAD = 2
CLOSE = 2
LAST_SUM = 12
TICKS = {0: 1, 2: 2, 5: 3, 7: 4, 8: 5, 10: 6, 12: 7, 14: 8, 15: 9, 16: 10}
LINE = 4
SELF_PUMPS = ((1, 6), (3, 7), (5, 8))
CROSS_PUMPS = ((1, 12), (3, 13), (5, 14))
QUARTERS = (0, 1, 2, 3)
LATE = (1, 3)
LATE_START = (-1, 1)
SLOTS = 4
LAG = 1
MESH = pl.DeviceIdType.MESH


def dot(a, b):
    return lax.dot_general(a, b, (((1,), (0,)), ((), ())), preferred_element_type=F32)


def dot_nt(a, b):
    return lax.dot_general(a, b, (((1,), (1,)), ((), ())), preferred_element_type=F32)


def dot_tn(a, b):
    return lax.dot_general(a, b, (((0,), (0,)), ((), ())), preferred_element_type=F32)


def rms_scale(values):
    return lax.rsqrt(jnp.mean(values * values, axis=-1, keepdims=True) + EPSILON)


def rms_back(values, gain, grad):
    scale = rms_scale(values)
    scaled = gain * grad
    mean = jnp.mean(scaled * values, axis=-1, keepdims=True)
    d_values = scale * scaled - values * (scale * scale * scale) * mean
    d_gain = jnp.sum(grad * values * scale, axis=0, keepdims=True)
    return d_values, d_gain


def gelu_parts(x):
    c = 0.7978845608028654
    t = jnp.tanh(c * (x + 0.044715 * (x * x * x)))
    value = 0.5 * x * (1.0 + t)
    slope = 0.5 * (1.0 + t) + 0.5 * x * (1.0 - t * t) * (c * (1.0 + 3.0 * 0.044715 * (x * x)))
    return value, slope


def own_lanes(first):
    lane = lax.broadcasted_iota(jnp.int32, (1, LANES), 1)
    mine = (lane < HD) if first else (lane >= HD)
    return jnp.where(mine, 1.0, 0.0)


def stack_heads(pair):
    one, two = own_lanes(True).astype(pair.dtype), own_lanes(False).astype(pair.dtype)
    return jnp.concatenate([pair * one, pair * two], axis=0)


def merge_heads(stacked):
    rows = stacked.shape[0] // 2
    return stacked[:rows] * own_lanes(True) + stacked[rows:] * own_lanes(False)


def skew(window, width):
    sub = lax.broadcasted_iota(jnp.int32, (8, width), 0)
    rows = jnp.broadcast_to(window, (8, width))
    for bit in (1, 2, 4):
        rows = jnp.where((sub & bit) != 0, pltpu.roll(rows, bit, 1), rows)
    return jnp.concatenate(
        [pltpu.roll(rows, (8 * g + width - 128) % width, 1) for g in range(16)], axis=0
    )


def unskew(total, width):
    sub = lax.broadcasted_iota(jnp.int32, (8, width), 0)
    rows = jnp.zeros((8, width), F32)
    for g in range(16):
        rows = rows + pltpu.roll(total[8 * g : 8 * g + 8], 128 - 8 * g, 1)
    for bit in (1, 2, 4):
        rows = jnp.where((sub & bit) != 0, pltpu.roll(rows, width - bit, 1), rows)
    return jnp.sum(rows, axis=0, keepdims=True)


def attend_kernel(biased, q_ref, k_ref, v_ref, *refs):
    if biased:
        row_ids, key_ids, window_ref, out_ref, p_ref = refs
    else:
        out_ref, p_ref = refs
    rows, length = q_ref.shape[0], k_ref.shape[0]
    blocks = rows // 128
    scores = dot_nt(stack_heads(q_ref[...]), k_ref[...])
    for head in range(2):
        if biased:
            width = window_ref.shape[2]
            table = skew(window_ref[0, head : head + 1, :], width)
        for b in range(blocks):
            at = head * rows + b * 128
            part = scores[at : at + 128]
            if biased:
                shift = (blocks - 1 - b) * 128
                allowed = key_ids[...] <= row_ids[b * 128 : b * 128 + 128, :]
                part = jnp.where(allowed, part + table[:, shift : shift + length], MASKED)
            top = jnp.max(part, axis=-1, keepdims=True)
            raised = jnp.exp(part - top)
            share = 1.0 / jnp.sum(raised, axis=-1, keepdims=True)
            p_ref[0, at : at + 128, :] = (raised * share).astype(BF16)
    out_ref[...] = merge_heads(dot(p_ref[0], v_ref[...]))


def attend_back_kernel(folded, q_ref, k_ref, v_ref, p_ref, out_ref, grad_ref, *refs):
    if folded:
        dq_ref, dk_ref, dv_ref, window_ref, ds_ref = refs
    else:
        dq_ref, dk_ref, dv_ref, ds_ref = refs
    rows, length = q_ref.shape[0], k_ref.shape[0]
    blocks = rows // 128
    grad = grad_ref[...]
    grads = stack_heads(grad)
    delta_wide = grad.astype(F32) * out_ref[...]
    d_weights = dot_nt(grads, v_ref[...])
    for head in range(2):
        if folded:
            width = window_ref.shape[2]
            total = jnp.zeros((128, width), F32)
        delta = jnp.sum(delta_wide * own_lanes(head == 0), axis=-1, keepdims=True)
        for b in range(blocks):
            at = head * rows + b * 128
            part = p_ref[0, at : at + 128, :].astype(F32) * (
                d_weights[at : at + 128] - delta[b * 128 : b * 128 + 128]
            )
            ds_ref[at : at + 128, :] = part.astype(BF16)
            if folded:
                shift = (blocks - 1 - b) * 128
                pieces = [part]
                if shift:
                    pieces = [jnp.zeros((128, shift), F32)] + pieces
                if width - shift - length:
                    pieces = pieces + [jnp.zeros((128, width - shift - length), F32)]
                total = total + jnp.concatenate(pieces, axis=1)
        if folded:
            window_ref[0, head : head + 1, :] = unskew(total, width)
    queries = stack_heads(q_ref[...])
    dq_ref[...] = merge_heads(dot(ds_ref[...], k_ref[...])).astype(BF16)
    dk_ref[...] = dot(queries.T, ds_ref[...]).T.astype(BF16)
    dv_ref[...] = dot(grads.T, p_ref[0]).T.astype(BF16)


def attend(query, keys, values, bias=None):
    rows, width = query.shape
    length = keys.shape[0]
    pairs = width // LANES
    column = lambda n: pl.BlockSpec((n, LANES), lambda i: (0, i))
    whole = lambda a: pl.BlockSpec(a.shape, lambda i: (0,) * a.ndim)
    operands, specs = [query, keys, values], [column(rows), column(length), column(length)]
    if bias is not None:
        row_ids, key_ids, window = bias
        operands += [row_ids, key_ids, window]
        specs += [
            whole(row_ids),
            whole(key_ids),
            pl.BlockSpec((1,) + window.shape[1:], lambda i: (i, 0, 0)),
        ]
    return pl.pallas_call(
        functools.partial(attend_kernel, bias is not None),
        grid=(pairs,),
        in_specs=specs,
        out_specs=[
            column(rows),
            pl.BlockSpec((1, 2 * rows, length), lambda i: (i, 0, 0)),
        ],
        out_shape=[
            jax.ShapeDtypeStruct((rows, width), F32),
            jax.ShapeDtypeStruct((pairs, 2 * rows, length), BF16),
        ],
        compiler_params=pltpu.CompilerParams(vmem_limit_bytes=VMEM_LIMIT),
        cost_estimate=pl.CostEstimate(
            flops=16 * rows * length * width,
            bytes_accessed=2 * pairs * 2 * rows * length,
            transcendentals=pairs * 2 * rows * length,
        ),
    )(*operands)


def attend_back(query, keys, values, weights, output, grad, window_shape=None):
    rows, width = query.shape
    length = keys.shape[0]
    pairs = width // LANES
    column = lambda n: pl.BlockSpec((n, LANES), lambda i: (0, i))
    out_specs = [column(rows), column(length), column(length)]
    out_shape = [
        jax.ShapeDtypeStruct((rows, width), BF16),
        jax.ShapeDtypeStruct((length, width), BF16),
        jax.ShapeDtypeStruct((length, width), BF16),
    ]
    if window_shape is not None:
        out_specs.append(pl.BlockSpec((1,) + window_shape[1:], lambda i: (i, 0, 0)))
        out_shape.append(jax.ShapeDtypeStruct(window_shape, F32))
    return pl.pallas_call(
        functools.partial(attend_back_kernel, window_shape is not None),
        grid=(pairs,),
        in_specs=[
            column(rows),
            column(length),
            column(length),
            pl.BlockSpec((1, 2 * rows, length), lambda i: (i, 0, 0)),
            column(rows),
            column(rows),
        ],
        out_specs=out_specs,
        out_shape=out_shape,
        scratch_shapes=[pltpu.VMEM((2 * rows, length), BF16)],
        compiler_params=pltpu.CompilerParams(vmem_limit_bytes=VMEM_LIMIT),
        cost_estimate=pl.CostEstimate(
            flops=32 * rows * length * width,
            bytes_accessed=2 * pairs * 2 * rows * length,
            transcendentals=0,
        ),
    )(query, keys, values, weights, output, grad)


def gather(values, axis=0):
    return lax.all_gather(values, "shard", axis=axis, tiled=True)


def scatter(values, axis=0):
    return lax.psum_scatter(values.astype(BF16), "shard", scatter_dimension=axis, tiled=True)


class Place:
    def __init__(self, reps, shards):
        self.nx, self.nh = shards // 2, reps // 4
        rep, shard = lax.axis_index("rep"), lax.axis_index("shard")
        self.rep, self.shard = rep, shard
        self.core, self.x = lax.rem(shard, 2), lax.div(shard, 2)
        self.y, z = lax.rem(rep, 2), lax.div(rep, 2)
        self.low, self.high = lax.rem(z, 2), lax.div(z, 2)

    def other_core(self):
        return (self.rep, self.x * 2 + 1 - self.core)

    def x_at(self, step):
        x = lax.rem(self.x + step, self.nx)
        return x, (self.rep, x * 2 + self.core)

    def other_y(self):
        return (self.rep + 1 - 2 * self.y, self.shard)

    def other_low(self):
        return (self.rep + 2 - 4 * self.low, self.shard)

    def high_at(self, step):
        high = lax.rem(self.high + step, self.nh)
        return high, (high * 4 + self.low * 2 + self.y, self.shard)

    def partners(self):
        found = [self.other_core(), self.other_y(), self.other_low()]
        found += [self.x_at(d)[1] for d in range(1, self.nx)]
        found += [self.high_at(d)[1] for d in range(1, self.nh)]
        return found


def enter(place):
    barrier = pltpu.get_barrier_semaphore()
    partners = place.partners()
    for device in partners:
        pl.semaphore_signal(barrier, inc=1, device_id=device, device_id_type=MESH)
    pl.semaphore_wait(barrier, len(partners))


def remote(src, dst, send, recv, device):
    return pltpu.make_async_remote_copy(
        src_ref=src, dst_ref=dst, send_sem=send, recv_sem=recv, device_id=device, device_id_type=MESH
    )


def added(*parts):
    if len(parts) == 2:
        return parts[0] + parts[1]
    total = parts[0].astype(F32)
    for part in parts[1:]:
        total = total + part.astype(F32)
    return total


class Reduction:
    def __init__(self, place, x_first, names, fin, parts, recv_x, recv_y, recv_low, recv_high, send, recv, own_sem):
        self.place, self.x_first, self.parts, self.fin = place, x_first, parts, fin
        self.names = names
        self.recv_x, self.recv_y, self.recv_low, self.recv_high = recv_x, recv_y, recv_low, recv_high
        self.send, self.recv, self.own_sem = send, recv, own_sem
        self.half = parts.shape[3] // 2
        self.rows = self.half // place.nh
        stages = [self.over_y, self.over_low, self.over_high]
        stages = [self.over_x] + stages if x_first else stages + [self.over_x]
        stages += [self.back_high, self.back_low, self.back_y]
        self.copies = stages
        self.adds = stages.index(self.back_high)

    @staticmethod
    def scratch(n, x_first, nx, nh, q, half):
        copies = 4 + nx + 2 * (nh - 1)
        wide = (n,) if x_first else (n, nx)
        x_part = (2, q) if x_first else (q // (2 * nh),)
        return [
            pltpu.VMEM((n, nx, 2, q, half), BF16),
            pltpu.VMEM((n, nx - 1) + x_part + (half,), BF16),
            pltpu.VMEM(wide + (q, half), BF16),
            pltpu.VMEM(wide + (q // 2, half), BF16),
            pltpu.VMEM((n, nh - 1) + wide[1:] + (q // (2 * nh), half), BF16),
            pltpu.SemaphoreType.DMA((n, copies)),
            pltpu.SemaphoreType.DMA((n, copies)),
            pltpu.SemaphoreType.DMA((n,)),
        ]

    def copy(self, u, which, src, dst, device):
        return remote(src, dst, self.send.at[u, which], self.recv.at[u, which], device)

    def low_rows(self, low):
        return pl.ds(pl.multiple_of(low * self.half, 16), self.half)

    def high_rows(self, high):
        at = self.place.low * self.half + high * self.rows
        return pl.ds(pl.multiple_of(at, 16), self.rows)

    def chips(self):
        return self.place.x if self.x_first else slice(None)

    def over_core(self, u, src):
        return [self.copy(u, 0, src, self.parts.at[u], self.place.other_core())]

    def over_x(self, u):
        p, out = self.place, []
        rest = () if self.x_first else (p.y, self.high_rows(p.high))
        for d in range(1, p.nx):
            x, device = p.x_at(d)
            src = self.parts.at[(u, x) + rest]
            out.append(self.copy(u, 2 + d, src, self.recv_x.at[u, d - 1], device))
        return out, (u, p.x) + rest, [self.recv_x.at[u, d] for d in range(p.nx - 1)]

    def over_y(self, u):
        p, chips = self.place, self.chips()
        src = self.parts.at[u, chips, 1 - p.y]
        copies = [self.copy(u, 1, src, self.recv_y.at[u], p.other_y())]
        return copies, (u, chips, p.y), [self.recv_y.at[u]]

    def over_low(self, u):
        p, chips = self.place, self.chips()
        src = self.parts.at[u, chips, p.y, self.low_rows(1 - p.low)]
        copies = [self.copy(u, 2 + p.nx, src, self.recv_low.at[u], p.other_low())]
        return copies, (u, chips, p.y, self.low_rows(p.low)), [self.recv_low.at[u]]

    def over_high(self, u):
        p, chips, out = self.place, self.chips(), []
        for d in range(1, p.nh):
            high, device = p.high_at(d)
            src = self.parts.at[u, chips, p.y, self.high_rows(high)]
            out.append(self.copy(u, 3 + p.nx + d, src, self.recv_high.at[u, d - 1], device))
        came = [self.recv_high.at[u, d] for d in range(p.nh - 1)]
        return out, (u, chips, p.y, self.high_rows(p.high)), came

    def piece(self, u):
        p = self.place
        rows = self.high_rows(p.high)
        return self.parts.at[u, p.x, p.y, rows], self.fin.at[self.names[u], p.y, rows]

    def keep(self, u):
        return pltpu.make_async_copy(*self.piece(u), self.own_sem.at[u])

    def back_high(self, u):
        p = self.place
        return [
            self.copy(u, 2 + p.nx + p.nh + d, *self.piece(u), p.high_at(d)[1])
            for d in range(1, p.nh)
        ]

    def back_low(self, u):
        p = self.place
        rows = self.fin.at[self.names[u], p.y, self.low_rows(p.low)]
        return [self.copy(u, 3 + p.nx, rows, rows, p.other_low())]

    def back_y(self, u):
        half = self.fin.at[self.names[u], self.place.y]
        return [self.copy(u, 2, half, half, self.place.other_y())]

    def begin(self, u, src):
        self.over_core(u, src)[0].start()

    def collect(self, u, src, own):
        self.over_core(u, src)[0].wait_recv()
        self.parts[u] = added(self.parts[u], own[...]).astype(BF16)

    def start(self, u, stage):
        if stage < len(self.copies):
            copies = self.copies[stage](u)
            for copy in copies[0] if stage < self.adds else copies:
                copy.start()

    def step(self, u, stage):
        if stage < self.adds:
            copies, stays, came = self.copies[stage](u)
            for copy in copies:
                copy.wait_recv()
            total = added(self.parts[stays], *[part[...] for part in came])
            self.parts[stays] = total.astype(BF16)
            if stage + 1 == self.adds:
                self.keep(u).start()
        else:
            for copy in self.copies[stage](u):
                copy.wait_recv()
            if stage == self.adds:
                self.keep(u).wait()
        self.start(u, stage + 1)

    def sent(self, u):
        for stage in range(len(self.copies)):
            copies = self.copies[stage](u)
            for copy in copies[0] if stage < self.adds else copies:
                copy.wait_send()


class SmallSum:
    def __init__(self, place, held, landed, send, recv):
        self.place, self.held, self.landed = place, held, landed
        self.send, self.recv = send, recv

    @staticmethod
    def scratch(nx, nh, shape):
        copies = 3 + nx - 1 + nh - 1
        return [
            pltpu.VMEM((6,) + shape, F32),
            pltpu.VMEM((copies,) + shape, F32),
            pltpu.SemaphoreType.DMA((copies,)),
            pltpu.SemaphoreType.DMA((copies,)),
        ]

    def copies(self, stage):
        p = self.place
        first, devices = [
            (0, [p.other_core()]),
            (3, [p.x_at(d)[1] for d in range(1, p.nx)]),
            (1, [p.other_y()]),
            (2, [p.other_low()]),
            (2 + p.nx, [p.high_at(d)[1] for d in range(1, p.nh)]),
        ][stage]
        return [
            remote(self.held.at[stage], self.landed.at[first + i], self.send.at[first + i], self.recv.at[first + i], device)
            for i, device in enumerate(devices)
        ], list(range(first, first + len(devices)))

    def begin(self, value):
        self.held[0] = value
        self.launch()

    def launch(self):
        for copy in self.copies(0)[0]:
            copy.start()

    def step(self, stage, stages=5):
        copies, slots = self.copies(stage)
        for copy in copies:
            copy.wait_recv()
        total = self.held[stage]
        for slot in slots:
            total = total + self.landed[slot]
        self.held[stage + 1] = total
        if stage + 1 < stages:
            for copy in self.copies(stage + 1)[0]:
                copy.start()
        return total

    def sent(self, stages=5):
        for stage in range(stages):
            for copy in self.copies(stage)[0]:
                copy.wait_send()


class Gather:
    def __init__(self, place, whole, own, hidden_rows, send, recv, own_sem):
        self.place, self.whole, self.own = place, whole, own
        self.send, self.recv, self.own_sem = send, recv, own_sem
        self.width = whole.shape[1]
        self.q = self.width // (2 * place.nx)
        self.square = len(own) - hidden_rows // self.q
        self.hidden_rows = hidden_rows

    @staticmethod
    def scratch(units, nx):
        copies = 1 + 8 * (nx - 1)
        return [
            pltpu.SemaphoreType.DMA((units, copies)),
            pltpu.SemaphoreType.DMA((units, copies)),
            pltpu.SemaphoreType.DMA((units,)),
        ]

    def cut(self, u, far_first, far_second=False):
        p = self.place
        first, second = (p.y, p.low) if u % 2 == 0 else (p.low, p.y)
        first = 1 - first if far_first else first
        second = 1 - second if far_second else second
        if u not in QUARTERS:
            return first * (self.q // 2)
        return (first * 2 + second) * (self.q // 4)

    def size(self, u):
        return self.q // 4 if u in QUARTERS else self.q // 2

    def first(self, u):
        return self.place.other_y() if u % 2 == 0 else self.place.other_low()

    def second(self, u):
        return self.place.other_low() if u % 2 == 0 else self.place.other_y()

    def part(self, u, shard, at=None):
        if u >= self.square:
            start = self.square * self.width + shard * self.hidden_rows
            start = start + (u - self.square) * self.q
        else:
            start = u * self.width + shard * self.q
        if at is None:
            return self.whole.at[pl.ds(pl.multiple_of(start, 16), self.q)]
        return self.whole.at[pl.ds(pl.multiple_of(start + at, 16), self.size(u))]

    def came(self, d):
        p = self.place
        return lax.rem(p.x + p.nx - d, p.nx) * 2 + p.core

    def copy(self, u, which, src, dst, device):
        return remote(src, dst, self.send.at[u, which], self.recv.at[u, which], device)

    def to_core(self, u):
        shard = self.place.shard
        return self.copy(u, 0, self.own[u], self.part(u, shard), self.place.other_core())

    def keep(self, u):
        return pltpu.make_async_copy(
            self.own[u], self.part(u, self.place.shard), self.own_sem.at[u]
        )

    def over_x(self, u, d):
        p = self.place
        at = self.cut(u, False)
        src = self.own[u].at[pl.ds(pl.multiple_of(at, 16), self.size(u))]
        return self.copy(u, 8 * d - 7, src, self.part(u, p.shard, at), p.x_at(d)[1])

    def on(self, u, d, which, far_first, far_second, device):
        here = self.part(u, self.came(d), self.cut(u, far_first, far_second))
        return self.copy(u, 8 * d - 7 + which, here, here, device)

    def onward(self, u, d, which):
        core, first, second = self.place.other_core(), self.first(u), self.second(u)
        far_first, far_second, device = (
            (False, False, first),
            (False, False, second),
            (False, False, core),
            (False, True, first),
            (False, True, core),
            (True, False, core),
            (True, True, core),
        )[which]
        return self.on(u, d, which + 1, far_first, far_second, device)

    def issue(self, u):
        for d in range(1, self.place.nx):
            self.over_x(u, d).start()
        self.to_core(u).start()
        self.keep(u).start()

    def relay_x(self, u):
        for d in range(1, self.place.nx):
            self.over_x(u, d).wait_recv()
            for which in (0, 1, 2) if u in QUARTERS else (0, 2):
                self.onward(u, d, which).start()

    def relay_second(self, u):
        for d in range(1, self.place.nx if u in QUARTERS else 1):
            self.onward(u, d, 1).wait_recv()
            self.onward(u, d, 3).start()
            self.onward(u, d, 4).start()

    def relay_first(self, u):
        for d in range(1, self.place.nx):
            self.onward(u, d, 0).wait_recv()
            self.onward(u, d, 5).start()
            if u in QUARTERS:
                self.onward(u, d, 3).wait_recv()
                self.onward(u, d, 6).start()

    def ready(self, u):
        self.keep(u).wait()
        self.to_core(u).wait_recv()
        for d in range(1, self.place.nx):
            for which in (2, 4, 5, 6) if u in QUARTERS else (2, 5):
                self.onward(u, d, which).wait_recv()

    def sent(self, u):
        self.to_core(u).wait_send()
        for d in range(1, self.place.nx):
            self.over_x(u, d).wait_send()
            for which in range(7) if u in QUARTERS else (0, 2, 5):
                self.onward(u, d, which).wait_send()


class Spread:
    def __init__(self, place, own, whole, send, recv, own_sem):
        self.place, self.own, self.whole = place, own, whole
        self.send, self.recv, self.own_sem = send, recv, own_sem
        self.count = own.shape[0]

    @staticmethod
    def scratch(nx):
        copies = 1 + 2 * (nx - 1)
        return [
            pltpu.SemaphoreType.DMA((copies,)),
            pltpu.SemaphoreType.DMA((copies,)),
            pltpu.SemaphoreType.DMA(()),
        ]

    def part(self, shard):
        return self.whole.at[pl.ds(pl.multiple_of(shard * self.count, 16), self.count)]

    def copy(self, which, src, dst, device):
        return remote(src, dst, self.send.at[which], self.recv.at[which], device)

    def to_core(self):
        return self.copy(0, self.own, self.part(self.place.shard), self.place.other_core())

    def over_x(self, d):
        p = self.place
        return self.copy(2 * d - 1, self.own, self.part(p.shard), p.x_at(d)[1])

    def on_core(self, d):
        p = self.place
        here = self.part(lax.rem(p.x + p.nx - d, p.nx) * 2 + p.core)
        return self.copy(2 * d, here, here, p.other_core())

    def keep(self):
        return pltpu.make_async_copy(self.own, self.part(self.place.shard), self.own_sem)

    def issue(self):
        for d in range(1, self.place.nx):
            self.over_x(d).start()
        self.to_core().start()
        self.keep().start()

    def relay_x(self):
        for d in range(1, self.place.nx):
            self.over_x(d).wait_recv()
            self.on_core(d).start()

    def ready(self):
        self.keep().wait()
        self.to_core().wait_recv()
        for d in range(1, self.place.nx):
            self.on_core(d).wait_recv()

    def sent(self):
        self.to_core().wait_send()
        for d in range(1, self.place.nx):
            self.over_x(d).wait_send()
            self.on_core(d).wait_send()


def attend_pair(query, keys, values_ref, p_ref, bias=None):
    rows, length = query.shape[0], keys.shape[0]
    blocks = rows // 128
    scores = dot_nt(stack_heads(query), keys)
    for head in range(2):
        if bias is not None:
            row_ids, key_ids, window = bias
            table = skew(window[head : head + 1], window.shape[1])
        for b in range(blocks):
            at = head * rows + b * 128
            part = scores[at : at + 128]
            if bias is not None:
                shift = (blocks - 1 - b) * 128
                allowed = key_ids <= row_ids[b * 128 : b * 128 + 128]
                part = jnp.where(allowed, part + table[:, shift : shift + length], MASKED)
            top = jnp.max(part, axis=-1, keepdims=True)
            raised = jnp.exp(part - top)
            share = 1.0 / jnp.sum(raised, axis=-1, keepdims=True)
            p_ref[at : at + 128, :] = (raised * share).astype(BF16)
    return merge_heads(dot(p_ref[...], values_ref[...]))


def bucket_onehot(buckets_ref, offsets_ref, place, rows, length):
    start = length - rows - place.shard * rows
    row = buckets_ref[...].reshape(1, 2 * length - 1)
    offsets_ref[...] = jnp.concatenate([jnp.zeros((1, 1), jnp.int32), row], axis=1)
    window = offsets_ref[:, pl.ds(pl.multiple_of(start, LANES), length + rows)]
    which = lax.broadcasted_iota(jnp.int32, (LANES, length + rows), 0)
    return jnp.where(window == which, 1.0, 0.0)


def forward_kernel(reps, shards, names, *refs):
    r = types.SimpleNamespace(**dict(zip(names, refs)))
    place = Place(reps, shards)
    rows, width = r.tok_in.shape
    length = r.tok.shape[0]
    pairs = width // LANES
    q = width // shards
    part = r.feed_in.shape[1] // width
    own = [r.self_query, r.self_keyval.at[0], r.self_keyval.at[1], r.self_output]
    own += [r.cross_query, r.cross_keyval.at[0], r.cross_keyval.at[1], r.cross_output]
    own += [r.feed_in.at[:, pl.ds(j * width, width)] for j in range(part)]
    own += [r.feed_out.at[pl.ds(j * q, q)] for j in range(part)]
    units = len(own)
    small = SmallSum(place, r.small_held, r.small_landed, r.small_send, r.small_recv)
    gather = Gather(place, r.whole, own, r.feed_out.shape[0], r.w_send, r.w_recv, r.w_own)
    tokens = Spread(place, r.tok_in, r.tok, r.t_send, r.t_recv, r.t_own)
    memories = Spread(place, r.enc_in, r.enc, r.e_send, r.e_recv, r.e_own)

    def weight(u):
        return r.whole[pl.ds(pl.multiple_of(u * width, width), width), :]

    def emit_weights(u, count):
        block = pl.ds(u * width, count * width)
        return pltpu.make_async_copy(r.whole.at[block], r.w_out.at[block], r.out_sem.at[u])

    def emit_kv(i):
        return pltpu.make_async_copy(r.kv.at[i], r.kv_out.at[i], r.out_sem.at[units + i])

    leaving = []

    def emit(src, dst):
        copy = pltpu.make_async_copy(src, dst, r.emit_sem.at[len(leaving)])
        copy.start()
        leaving.append(copy)

    emit_tok = pltpu.make_async_copy(r.tok_t, r.tok_out, r.out_sem.at[units + 4])
    emit_enc = pltpu.make_async_copy(r.enc_t, r.enc_out, r.out_sem.at[units + 5])

    def emit_p(which, i):
        slot = lax.rem(i, 2)
        return pltpu.make_async_copy(r.probs.at[slot], r.p_out.at[which, i], r.p_sem.at[slot])

    def gain(i):
        return r.small_held[2, i : i + 1, :width]

    shard = place.shard
    wide = r.small_held.shape[2]
    sub = lax.broadcasted_iota(jnp.int32, (8, wide), 0)
    padded = lambda a: jnp.concatenate([a, jnp.zeros((a.shape[0], wide - a.shape[1]), F32)], axis=1)
    shifted = lambda a, by: pltpu.roll(padded(a), shard * by, 1)
    ids = r.ids[...].astype(F32)
    gains = [gain_ref[...].astype(F32).reshape(1, q) for gain_ref in (r.norm_self, r.norm_cross, r.norm_feed)]
    mine = jnp.concatenate(gains + [jnp.zeros((5, q), F32)], axis=0)
    mine = jnp.where(sub == 3, 0.0, shifted(mine, q))
    mine = mine + jnp.where(sub == 3, shifted(jnp.broadcast_to(ids, (8, rows)), rows), 0.0)
    table = r.bucket_bias[...].astype(F32).T
    heads, cut = table.shape
    table = jnp.concatenate([table, jnp.zeros((16 - heads, cut), F32)], axis=0)
    r.small_held[0] = jnp.concatenate([mine, shifted(table, cut)], axis=0)
    r.row_ids[...] = jnp.broadcast_to(ids, (8, rows)).T[:, 0:1]
    enter(place)
    small.launch()
    line = [(gather, (u,)) for u in (1, 2, 0, 3)] + [(tokens, ())]
    line += [(gather, (u,)) for u in (5, 6)] + [(memories, ())]
    line += [(gather, (u,)) for u in [4, 7] + list(range(8, units))]
    pumped = [0]
    steps = ("relay_x", "relay_second", "relay_first")

    def issue(at):
        if at < len(line):
            line[at][0].issue(*line[at][1])

    def pump(at):
        for late, name in enumerate(steps):
            if 0 <= at - late < len(line):
                owner, u = line[at - late]
                if hasattr(owner, name):
                    getattr(owner, name)(*u)
            if late == 0:
                issue(at + LINE)

    def pump_to(end):
        while pumped[0] < end:
            pump(pumped[0])
            pumped[0] += 1

    def have(*wanted):
        last = max(line.index((gather, (u,))) for u in wanted)
        pump_to(last + len(steps))
        for u in wanted:
            gather.ready(u)

    for at in range(LINE):
        issue(at)
    small.step(0, 2)
    gathered = small.step(1, 2)
    r.small_out[...] = gathered
    table = gathered[8:24, :LANES].astype(BF16)
    biases = dot(table, bucket_onehot(r.buckets, r.offsets, place, rows, length).astype(BF16))
    for i in range(pairs):
        r.window[i] = biases[2 * i : 2 * i + 2]
    pump_to(5)
    tokens.ready()
    tokens.sent()

    def norm_rows(i, carry):
        at = pl.ds(pl.multiple_of(i * rows, 16), rows)
        values = r.tok[at, :].astype(F32)
        normed = (values * rms_scale(values) * gain(0)).astype(BF16)
        r.tok[at, :] = normed
        r.tok_t[:, pl.ds(pl.multiple_of(i * rows, LANES), rows)] = normed.T
        return carry

    lax.fori_loop(0, length // rows, norm_rows, 0)
    emit_tok.start()

    def project_pair(source, target, base):
        def step(i, carry):
            at = pl.ds(pl.multiple_of(i * rows, 16), rows)
            block = source[at, :]
            for which in range(2):
                out = dot(block, weight(base + which)).astype(BF16)
                for j in range(pairs):
                    r.kv[target + which, j, at, :] = out[:, j * LANES : (j + 1) * LANES]
            return carry

        lax.fori_loop(0, source.shape[0] // rows, step, 0)
        emit_kv(target).start()
        emit_kv(target + 1).start()

    def project_query(normed, u, which):
        out = dot(normed, weight(u)).astype(BF16)
        for j in range(pairs):
            r.queries[which, j] = out[:, j * LANES : (j + 1) * LANES]

    def attention(which, bias, relays):
        def pair(i, carry):
            @pl.when(i >= 2)
            def _():
                emit_p(which, i).wait()

            slot = lax.rem(i, 2)
            more = None
            if bias:
                more = (r.row_ids[...], r.small_held[2, 3:4, :length], r.window[i])
            r.low[which, i] = attend_pair(
                r.queries[which, i],
                r.kv[2 * which, i],
                r.kv.at[2 * which + 1, i],
                r.probs.at[slot],
                more,
            )
            emit_p(which, i).start()
            for step, end in relays:
                @pl.when(i == step)
                def _():
                    pump_to(end)

            return carry

        lax.fori_loop(0, pairs, pair, 0)
        emit_p(which, 0).wait()
        emit_p(which, 1).wait()
        low = [r.low[which, j].astype(BF16) for j in range(pairs)]
        low = jnp.concatenate(low, axis=1)
        r.low_t[which] = low.T
        emit(r.low.at[which], r.low_out.at[which])
        emit(r.low_t.at[which], r.low_t_out.at[which])
        emit(r.queries.at[which], r.q_out.at[which])
        return low

    have(1, 2)
    project_pair(r.tok, 0, 1)
    have(0)
    emit_weights(0, 3).start()
    mine = pl.ds(pl.multiple_of(place.shard * rows, 16), rows)
    project_query(r.tok[mine, :], 0, 0)
    low = attention(0, True, SELF_PUMPS)
    have(3)
    r.first[...] = r.tok_in[...].astype(F32) + dot(low, weight(3))
    emit(r.first, r.first_out)
    pump_to(8)
    memories.ready()

    def turn_rows(i, carry):
        at = pl.ds(pl.multiple_of(i * rows, LANES), rows)
        r.enc_t[:, at] = r.enc[at, :].T
        return carry

    lax.fori_loop(0, length // rows, turn_rows, 0)
    emit_enc.start()
    have(5, 6)
    project_pair(r.enc, 2, 5)
    have(4)
    first = r.first[...]
    normed = (first * rms_scale(first) * gain(1)).astype(BF16)
    r.normed2_t[...] = normed.T
    emit(r.normed2_t, r.normed2_out)
    project_query(normed, 4, 1)
    low = attention(1, False, CROSS_PUMPS)
    have(7)
    emit_weights(3, 5).start()
    r.second[...] = r.first[...] + dot(low, weight(7))
    emit(r.second, r.second_out)
    second = r.second[...]
    normed = (second * rms_scale(second) * gain(2)).astype(BF16)
    r.normed[...] = normed
    r.normed3_t[...] = normed.T
    emit(r.normed3_t, r.normed3_out)
    for j in range(part):
        have(8 + j)
        value, slope = gelu_parts(dot(r.normed[...], weight(8 + j)))
        value = value.astype(BF16)
        r.hidden[j] = value
        r.hidden_t[j * width : (j + 1) * width, :] = value.T
        r.slope[j] = slope
        block = pl.ds(j * width, width)
        emit(r.hidden_t.at[block], r.hidden_out.at[block])
        emit(r.slope.at[j], r.slope_out.at[j])
    have(*range(8 + part, units))
    emit_weights(8, units - 8).start()
    total = second
    for j in range(part):
        total = total + dot(r.hidden[j], weight(8 + part + j))
    r.result[...] = total.astype(BF16)
    for u in range(units):
        gather.sent(u)
    memories.sent()
    small.sent(2)
    for u, count in ((0, 3), (3, 5), (8, units - 8)):
        emit_weights(u, count).wait()
    for i in range(4):
        emit_kv(i).wait()
    emit_tok.wait()
    emit_enc.wait()
    for copy in leaving:
        copy.wait()


def forward(tokens, encoded, ids, buckets, gains, bucket_bias, shards_of, reps, shards):
    rows, width = tokens.shape
    length, memory = rows * shards, encoded.shape[0] * shards
    nx = shards // 2
    feed_in, feed_out = shards_of[-2:]
    hidden = feed_in.shape[1]
    units = 8 + 2 * (hidden // width)
    pairs = width // LANES
    small = (24, max(length, width))
    kept = lambda *shape, dtype=BF16: (pl.BlockSpec(memory_space=pl.ANY), jax.ShapeDtypeStruct(shape, dtype))
    near = lambda *shape, dtype=F32: (pl.BlockSpec(memory_space=pltpu.VMEM), jax.ShapeDtypeStruct(shape, dtype))
    outs = dict(
        result=near(rows, width, dtype=BF16),
        small_out=near(*small),
        first_out=kept(rows, width, dtype=F32),
        second_out=kept(rows, width, dtype=F32),
        low_out=kept(2, pairs, rows, LANES, dtype=F32),
        low_t_out=kept(2, width, rows),
        q_out=kept(2, pairs, rows, LANES),
        normed2_out=kept(width, rows),
        normed3_out=kept(width, rows),
        hidden_out=kept(hidden, rows),
        slope_out=kept(hidden // width, rows, width, dtype=F32),
        w_out=kept(units * width, width),
        kv_out=kept(4, pairs, length, LANES),
        tok_out=kept(width, length),
        enc_out=kept(width, memory),
        p_out=kept(2, pairs, 2 * rows, length),
    )
    scratch = dict(
        whole=pltpu.VMEM((units * width, width), BF16),
        tok=pltpu.VMEM((length, width), BF16),
        enc=pltpu.VMEM((memory, width), BF16),
        kv=pltpu.VMEM((4, pairs, length, LANES), BF16),
        window=pltpu.VMEM((pairs, 2, length + rows), F32),
        row_ids=pltpu.VMEM((rows, 1), F32),
        offsets=pltpu.VMEM((1, 2 * length), jnp.int32),
        probs=pltpu.VMEM((2, 2 * rows, length), BF16),
        first=pltpu.VMEM((rows, width), F32),
        second=pltpu.VMEM((rows, width), F32),
        low=pltpu.VMEM((2, pairs, rows, LANES), F32),
        low_t=pltpu.VMEM((2, width, rows), BF16),
        queries=pltpu.VMEM((2, pairs, rows, LANES), BF16),
        normed2_t=pltpu.VMEM((width, rows), BF16),
        normed3_t=pltpu.VMEM((width, rows), BF16),
        hidden_t=pltpu.VMEM((hidden, rows), BF16),
        slope=pltpu.VMEM((hidden // width, rows, width), F32),
        emit_sem=pltpu.SemaphoreType.DMA((10 + 2 * (hidden // width),)),
        normed=pltpu.VMEM((rows, width), BF16),
        hidden=pltpu.VMEM((hidden // width, rows, width), BF16),
        tok_t=pltpu.VMEM((width, length), BF16),
        enc_t=pltpu.VMEM((width, memory), BF16),
        p_sem=pltpu.SemaphoreType.DMA((2,)),
        out_sem=pltpu.SemaphoreType.DMA((units + 6,)),
    )
    scratch.update(zip(("small_held", "small_landed", "small_send", "small_recv"), SmallSum.scratch(nx, reps // 4, small)))
    scratch.update(zip(("w_send", "w_recv", "w_own"), Gather.scratch(units, nx)))
    scratch.update(zip(("t_send", "t_recv", "t_own"), Spread.scratch(nx)))
    scratch.update(zip(("e_send", "e_recv", "e_own"), Spread.scratch(nx)))
    shard_names = ["self_query", "self_keyval", "self_output", "cross_query", "cross_keyval", "cross_output", "feed_in", "feed_out"]
    near_names = ["tok_in", "enc_in", "ids", "buckets", "norm_self", "norm_cross", "norm_feed", "bucket_bias"]
    names = near_names + shard_names + list(outs) + list(scratch)
    made = pl.pallas_call(
        functools.partial(forward_kernel, reps, shards, tuple(names)),
        in_specs=[pl.BlockSpec(memory_space=pltpu.VMEM)] * 8 + [pl.BlockSpec(memory_space=pl.ANY)] * 8,
        out_specs=[spec for spec, _ in outs.values()],
        out_shape=[shape for _, shape in outs.values()],
        scratch_shapes=list(scratch.values()),
        compiler_params=pltpu.CompilerParams(
            collective_id=2, has_side_effects=True, vmem_limit_bytes=FUSED_LIMIT
        ),
    )(tokens, encoded, ids, buckets, *gains, bucket_bias, *shards_of)
    return types.SimpleNamespace(**dict(zip(outs, made)))


class RowSum:
    def __init__(self, place, parts, recv_a, recv_b, send, recv):
        self.place, self.parts, self.recv_a, self.recv_b = place, parts, recv_a, recv_b
        self.send, self.recv = send, recv

    @staticmethod
    def scratch(nx, width, rows):
        return [
            pltpu.VMEM((2, nx, width, rows), BF16),
            pltpu.VMEM((nx, width, rows), BF16),
            pltpu.VMEM((nx - 1, width, rows), BF16),
            pltpu.SemaphoreType.DMA((nx,)),
            pltpu.SemaphoreType.DMA((nx,)),
        ]

    def copy(self, which, src, dst, device):
        return remote(src, dst, self.send.at[which], self.recv.at[which], device)

    def to_core(self):
        p = self.place
        return self.copy(0, self.parts.at[1 - p.core], self.recv_a, p.other_core())

    def over_x(self, d):
        x, device = self.place.x_at(d)
        return self.copy(d, self.recv_a.at[x], self.recv_b.at[d - 1], device)

    def begin(self, total):
        rows = self.parts.shape[3]
        for s in range(2 * self.place.nx):
            self.parts[s % 2, s // 2] = total[:, s * rows : (s + 1) * rows].astype(BF16)
        self.to_core().start()

    def pass_x(self):
        self.to_core().wait_recv()
        self.recv_a[...] = added(self.recv_a[...], self.parts[self.place.core]).astype(BF16)
        for d in range(1, self.place.nx):
            self.over_x(d).start()

    def finish(self):
        p = self.place
        for d in range(1, p.nx):
            self.over_x(d).wait_recv()
        return added(self.recv_a[p.x], *[self.recv_b[d] for d in range(p.nx - 1)]).astype(F32)

    def sent(self):
        for d in range(1, self.place.nx):
            self.over_x(d).wait_send()


def attend_back_pair(query, keys, values, p_ref, output, grad, ds_ref, width=None):
    rows, length = query.shape[0], keys.shape[0]
    blocks = rows // 128
    grads, queries = stack_heads(grad), stack_heads(query)
    delta_wide = grad.astype(F32) * output
    d_weights = dot_nt(grads, values)
    windows = []
    for head in range(2):
        delta = jnp.sum(delta_wide * own_lanes(head == 0), axis=-1, keepdims=True)
        total = None
        for b in range(blocks):
            at = head * rows + b * 128
            part = p_ref[at : at + 128, :].astype(F32) * (
                d_weights[at : at + 128] - delta[b * 128 : b * 128 + 128]
            )
            ds_ref[at : at + 128, :] = part.astype(BF16)
            if width is not None:
                shift = (blocks - 1 - b) * 128
                pieces = [jnp.zeros((128, shift), F32)] if shift else []
                pieces.append(part)
                if width - shift - length:
                    pieces.append(jnp.zeros((128, width - shift - length), F32))
                placed = jnp.concatenate(pieces, axis=1)
                total = placed if total is None else total + placed
        if width is not None:
            windows.append(unskew(total, width))
    d_query = merge_heads(dot(ds_ref[...], keys)).astype(BF16)
    d_keys = dot(queries.T, ds_ref[...]).astype(BF16)
    d_values = dot(grads.T, p_ref[...]).astype(BF16)
    return d_query, d_keys, d_values, windows


BROUGHT = ("hidden_t", "normed3_t", "second", "low_t", "queries", "low", "first", "normed2_t")
REDUCTION = ("_parts", "_x", "_y", "_low", "_high", "_send", "_recv", "_own")


def late_units(units):
    return [n for n in LATE if n < units]


def backward_kernel(reps, shards, names, *refs):
    r = types.SimpleNamespace(**dict(zip(names, refs)))
    place = Place(reps, shards)
    rows, width = r.cotangent.shape
    length = r.enc_t.shape[1]
    pairs = width // LANES
    q = width // shards
    part = r.hidden_t.shape[0] // width
    units = 8 + 2 * part
    late = late_units(units)
    order = [n for n in range(units) if n not in late]
    reductions = [
        Reduction(place, x_first, names, r.fin, *(getattr(r, name + end) for end in REDUCTION))
        for x_first, names, name in ((True, order, "a"), (False, late, "b"))
    ]
    stages = len(reductions[0].copies)

    def owner(n):
        return (reductions[1], late.index(n)) if n in late else (reductions[0], order.index(n))

    small = SmallSum(place, r.small_held, r.small_landed, r.small_send, r.small_recv)
    sum_memory = RowSum(place, r.m_parts, r.m_a, r.m_b, r.m_send, r.m_recv)
    sum_tokens = RowSum(place, r.m_parts, r.t_a, r.t_b, r.t_send, r.t_recv)

    def gain(i):
        return r.gains[i : i + 1, :width]

    def load_weight(u, slot):
        block = pl.ds(u * width, width)
        return pltpu.make_async_copy(r.w_in.at[block], r.w.at[slot], r.w_sem.at[slot])

    ticks = [0]

    def slot_done(slot):
        while ticks[0] < TICKS.get(slot, 0):
            advance(ticks[0])
            ticks[0] += 1

    def load_slope(j):
        slot = j % 2
        return pltpu.make_async_copy(r.slope.at[j], r.slopes.at[slot], r.s_sem.at[slot])

    def load_kv(i, slot):
        return pltpu.make_async_copy(r.kv_in.at[i], r.kv.at[slot], r.kv_sem.at[slot])

    def load_p(which, i):
        slot = lax.rem(i, 2)
        return pltpu.make_async_copy(r.p_in.at[which, i], r.probs.at[slot], r.p_sem.at[slot])

    def load_t(source, which):
        return pltpu.make_async_copy(source, r.rows_t, r.t_sem.at[which])

    def away(n):
        return r.made.at[n % SLOTS, 1 - place.core]

    def fill(n, value):
        slot = n % SLOTS
        rest = value.shape[0] // shards
        half = width // 2
        for s in range(shards):
            for h in range(2):
                r.made[slot, s % 2, s // 2, h] = value[
                    s * rest : (s + 1) * rest, h * half : (h + 1) * half
                ].astype(BF16)
        red, u = owner(n)
        red.begin(u, away(n))

    def left(n):
        red, u = owner(n)
        red.over_core(u, away(n))[0].wait_send()

    def free(n):
        if n >= SLOTS:
            left(n - SLOTS)

    done_stages = {n: 0 for n in range(units)}
    started = [0]

    def set_out(end):
        while started[0] < min(end, len(order)):
            red, u = owner(order[started[0]])
            red.start(u, 0)
            started[0] += 1

    def take(n):
        red, u = owner(n)
        red.collect(u, away(n), r.made.at[n % SLOTS, place.core])
        if n in late:
            red.start(u, 0)
        elif order.index(n) < AHEAD:
            set_out(order.index(n) + 1)

    def move(n, upto):
        red, u = owner(n)
        while done_stages[n] < min(upto, stages):
            red.step(u, done_stages[n])
            done_stages[n] += 1

    def advance(t):
        for back in range(stages):
            at = t - back
            if 0 <= at < len(order):
                move(order[at], back + 1)
            if back == 0:
                set_out(t + 1 + (AHEAD if t < len(order) - CLOSE else 1))
        for i, n in enumerate(late):
            move(n, t - LATE_START[i])

    def bring(name):
        source, sem = getattr(r, name + "_in"), r.bring_sem.at[BROUGHT.index(name)]
        return pltpu.make_async_copy(source, getattr(r, name), sem)

    load_slope(0).start()
    for slot, u in enumerate((8, 8 + part)):
        load_weight(u, slot).start()
    for name in BROUGHT[:3]:
        bring(name).start()
    enter(place)
    for name in BROUGHT[3:]:
        bring(name).start()
    for slot in range(2):
        load_kv(2 + slot, slot).start()
        load_p(1, slot).start()
    load_t(r.enc_t, 0).start()
    r.acc[...] = jnp.zeros((rows, width), F32)

    bring("hidden_t").wait()
    for m in range(part):
        n = m
        free(n)
        value = jnp.concatenate(
            [
                dot(r.hidden_t[s * width + m * q : s * width + (m + 1) * q, :], r.cotangent[...])
                for s in range(shards)
            ],
            axis=0,
        )
        fill(n, value)
        if m >= 1:
            take(n - 1)
    take(part - 1)
    for j in range(part):
        slot = 2 * (j % 2)
        load_weight(8, slot).wait()
        load_weight(8 + part, slot + 1).wait()
        load_slope(j).wait()
        if j + 1 < part:
            load_slope(j + 1).start()
            load_weight(8 + j + 1, 2 - slot).start()
            load_weight(8 + part + j + 1, 3 - slot).start()
        if j == 0:
            bring("normed3_t").wait()
        grad_hidden = dot_nt(r.cotangent[...], r.w[slot + 1])
        grad = (grad_hidden * r.slopes[j % 2]).astype(BF16)
        free(part + j)
        fill(part + j, dot(r.normed3_t[...], grad))
        r.acc[...] += dot_nt(grad, r.w[slot])
        if j >= 1:
            take(part + j - 1)
    for slot, u in ((0, 7), (1, 5), (2, 6), (3, 4)):
        load_weight(u, slot).start()
    bring("second").wait()
    back, d_gain3 = rms_back(r.second[...], gain(2), r.acc[...])
    r.grad[...] = r.cotangent[...].astype(F32) + back
    take(2 * part - 1)
    slot_done(0)

    def attention(which, fold, first_slot):
        def pair(i, carry):
            slot = lax.rem(i, 2)
            load_p(which, i).wait()
            d_query, d_keys, d_values, windows = attend_back_pair(
                r.queries[which, i],
                r.kv[0, i],
                r.kv[1, i],
                r.probs.at[slot],
                r.low[which, i],
                r.grad_att[i],
                r.ds,
                length + rows if fold else None,
            )
            r.d_query[i] = d_query
            at = pl.ds(pl.multiple_of(i * LANES, LANES), LANES)
            r.dk_t[at, :] = d_keys
            r.dv_t[at, :] = d_values
            if fold:
                r.d_window[i] = jnp.concatenate(windows, axis=0)

            @pl.when(i + 2 < pairs)
            def _():
                load_p(which, i + 2).start()

            for step in range(pairs):
                if first_slot + step in TICKS:
                    @pl.when(i == step)
                    def _():
                        slot_done(first_slot + step)

            return carry

        lax.fori_loop(0, pairs, pair, 0)

    def spread_grad(value):
        for i in range(pairs):
            r.grad_att[i] = value[:, i * LANES : (i + 1) * LANES].astype(BF16)

    def joined_query():
        return jnp.concatenate([r.d_query[i] for i in range(pairs)], axis=1)

    for name in BROUGHT[3:]:
        bring(name).wait()
    n = 2 * part
    grad_low = r.grad[...].astype(BF16)
    free(n)
    fill(n, dot(r.low_t[1], grad_low))
    load_weight(7, 0).wait()
    spread_grad(dot_nt(grad_low, r.w[0]))
    load_weight(3, 0).start()
    take(n)
    for slot in range(2):
        load_kv(2 + slot, slot).wait()
    attention(1, False, 1)
    for slot in range(2):
        load_kv(slot, slot).start()
        load_p(0, slot).start()
    load_weight(5, 1).wait()
    load_weight(6, 2).wait()
    sum_memory.begin(dot(r.w[1], r.dk_t[...]) + dot(r.w[2], r.dv_t[...]))
    load_weight(1, 1).start()
    load_weight(2, 2).start()
    load_t(r.enc_t, 0).wait()
    free(n + 1)
    fill(n + 1, dot_nt(r.rows_t[...], r.dk_t[...]))
    sum_memory.pass_x()
    free(n + 2)
    fill(n + 2, dot_nt(r.rows_t[...], r.dv_t[...]))
    take(n + 1)
    slot_done(7)
    load_t(r.tok_t, 1).start()
    d_query = joined_query()
    load_weight(4, 3).wait()
    back, d_gain2 = rms_back(r.first[...], gain(1), dot_nt(d_query, r.w[3]))
    load_weight(0, 3).start()
    free(n + 3)
    fill(n + 3, dot(r.normed2_t[...], d_query))
    take(n + 2)
    r.grad[...] = r.grad[...] + back
    slot_done(8)

    grad_low = r.grad[...].astype(BF16)
    take(n + 3)
    free(n + 4)
    fill(n + 4, dot(r.low_t[0], grad_low))
    load_weight(3, 0).wait()
    spread_grad(dot_nt(grad_low, r.w[0]))
    take(n + 4)
    for slot in range(2):
        load_kv(slot, slot).wait()
    attention(0, True, 9)
    load_weight(1, 1).wait()
    load_weight(2, 2).wait()
    sum_memory.to_core().wait_send()
    sum_tokens.begin(dot(r.w[1], r.dk_t[...]) + dot(r.w[2], r.dv_t[...]))
    load_t(r.tok_t, 1).wait()
    free(n + 5)
    fill(n + 5, dot_nt(r.rows_t[...], r.dk_t[...]))
    sum_tokens.pass_x()
    free(n + 6)
    fill(n + 6, dot_nt(r.rows_t[...], r.dv_t[...]))
    take(n + 5)
    r.d_memory[...] = sum_memory.finish().T
    slot_done(15)
    d_query = joined_query()
    free(n + 7)
    mine = pl.ds(pl.multiple_of(place.shard * rows, LANES), rows)
    fill(n + 7, dot(r.rows_t[:, mine], d_query))
    take(n + 6)
    load_weight(0, 3).wait()
    r.acc[...] = dot_nt(d_query, r.w[3])
    windows = jnp.concatenate([r.d_window[i] for i in range(pairs)], axis=0)
    d_table = lax.dot_general(
        windows,
        bucket_onehot(r.buckets, r.offsets, place, rows, length),
        (((1,), (1,)), ((), ())),
        precision=lax.Precision.HIGHEST,
        preferred_element_type=F32,
    )
    take(n + 7)
    slot_done(16)
    for t in range(ticks[0], len(order) + stages):
        advance(t)
        if t == LAST_SUM:
            values = r.tokens[...].astype(F32)
            total = r.acc[...] + sum_tokens.finish().T
            back, d_gain1 = rms_back(values, gain(0), total)
            r.d_tokens[...] = r.grad[...] + back
            r.small_held[0] = jnp.zeros(r.small_held.shape[1:], F32)
            for i, d_gain in enumerate((d_gain1, d_gain2, d_gain3)):
                r.small_held[0, i : i + 1, :width] = d_gain
            r.small_held[0, 8 : 8 + 2 * pairs, :LANES] = d_table
            small.launch()
        elif LAST_SUM < t < LAST_SUM + 6:
            small.step(t - LAST_SUM - 1)
    for n in range(units):
        move(n, stages)
    r.small_out[...] = r.small_held[5]
    for n in range(units):
        if n >= units - SLOTS:
            left(n)
        red, u = owner(n)
        red.sent(u)
    small.sent()
    sum_tokens.to_core().wait_send()
    sum_memory.sent()
    sum_tokens.sent()


def backward(tokens, cotangent, buckets, held, reps, shards):
    rows, width = tokens.shape
    length = held.enc_out.shape[1]
    nx, nh = shards // 2, reps // 4
    pairs = width // LANES
    q, half = width // shards, width // 2
    units = held.w_out.shape[0] // width
    small = (24, width)
    kept = pl.BlockSpec(memory_space=pl.ANY)
    near = pl.BlockSpec(memory_space=pltpu.VMEM)
    arrays = (held.hidden_out, held.normed3_out, held.second_out, held.low_t_out)
    arrays += (held.q_out, held.low_out, held.first_out, held.normed2_out)
    brought = dict(zip(BROUGHT, arrays))
    ins = dict(
        tokens=(near, tokens),
        cotangent=(near, cotangent),
        buckets=(near, buckets),
        gains=(near, held.small_out),
        **{name + "_in": (kept, array) for name, array in brought.items()},
        slope=(kept, held.slope_out),
        tok_t=(kept, held.tok_out),
        enc_t=(kept, held.enc_out),
        w_in=(kept, held.w_out),
        kv_in=(kept, held.kv_out),
        p_in=(kept, held.p_out),
    )
    outs = dict(
        d_tokens=(near, jax.ShapeDtypeStruct((rows, width), F32)),
        d_memory=(near, jax.ShapeDtypeStruct((rows, width), F32)),
        small_out=(near, jax.ShapeDtypeStruct(small, F32)),
        fin=(kept, jax.ShapeDtypeStruct((units, 2, q, half), BF16)),
    )
    scratch = {name: pltpu.VMEM(array.shape, array.dtype) for name, array in brought.items()}
    scratch.update(
        bring_sem=pltpu.SemaphoreType.DMA((len(brought),)),
        w=pltpu.VMEM((4, width, width), BF16),
        kv=pltpu.VMEM((2, pairs, length, LANES), BF16),
        probs=pltpu.VMEM((2, 2 * rows, length), BF16),
        ds=pltpu.VMEM((2 * rows, length), BF16),
        rows_t=pltpu.VMEM((width, length), BF16),
        dk_t=pltpu.VMEM((width, length), BF16),
        dv_t=pltpu.VMEM((width, length), BF16),
        d_query=pltpu.VMEM((pairs, rows, LANES), BF16),
        grad_att=pltpu.VMEM((pairs, rows, LANES), BF16),
        offsets=pltpu.VMEM((1, 2 * length), jnp.int32),
        d_window=pltpu.VMEM((pairs, 2, length + rows), F32),
        acc=pltpu.VMEM((rows, width), F32),
        grad=pltpu.VMEM((rows, width), F32),
        made=pltpu.VMEM((SLOTS, 2, nx, 2, q, half), BF16),
        slopes=pltpu.VMEM((2, rows, width), F32),
        s_sem=pltpu.SemaphoreType.DMA((2,)),
        w_sem=pltpu.SemaphoreType.DMA((4,)),
        kv_sem=pltpu.SemaphoreType.DMA((2,)),
        p_sem=pltpu.SemaphoreType.DMA((2,)),
        t_sem=pltpu.SemaphoreType.DMA((2,)),
    )
    counts = {"a": units - len(late_units(units)), "b": len(late_units(units))}
    for name, count in counts.items():
        made_for = Reduction.scratch(count, name == "a", nx, nh, q, half)
        scratch.update(zip((name + end for end in REDUCTION), made_for))
    scratch.update(
        zip(("small_held", "small_landed", "small_send", "small_recv"), SmallSum.scratch(nx, nh, small))
    )
    for name in "mt":
        keys = (name + end for end in ("_parts", "_a", "_b", "_send", "_recv"))
        scratch.update(zip(keys, RowSum.scratch(nx, width, rows)))
    del scratch["t_parts"]
    names = tuple(list(ins) + list(outs) + list(scratch))
    made = pl.pallas_call(
        functools.partial(backward_kernel, reps, shards, names),
        in_specs=[spec for spec, _ in ins.values()],
        out_specs=[spec for spec, _ in outs.values()],
        out_shape=[shape for _, shape in outs.values()],
        scratch_shapes=list(scratch.values()),
        compiler_params=pltpu.CompilerParams(
            collective_id=3, has_side_effects=True, vmem_limit_bytes=FUSED_LIMIT
        ),
    )(*[value for _, value in ins.values()])
    return types.SimpleNamespace(**dict(zip(outs, made)))


def finish_kernel(squares, shards, names, *refs):
    r = types.SimpleNamespace(**dict(zip(names, refs)))
    step = pl.program_id(0)
    shard = lax.axis_index("shard")
    whole = lambda ref: jnp.concatenate([ref[0, 0], ref[0, 1]], axis=1).astype(F32)
    r.feed_in[...] = whole(r.fin_in)
    r.feed_out[...] = whole(r.fin_out)
    for source, group in zip((r.fin_cross, r.fin_self), squares):
        value = whole(source)
        for name, first, count in group:
            out = getattr(r, name)

            @pl.when((step >= first) & (step < first + count))
            def _():
                out[...] = value.reshape(out.shape)

    r.d_tokens[...] = r.tokens_in[...]
    r.d_memory[...] = r.memory_in[...]
    r.result[...] = r.result_in[...]

    @pl.when(step == 0)
    def _():
        small = r.small[...]
        width = small.shape[1]
        mine = lambda by: pltpu.roll(small, lax.rem(width - shard * by, width), 1)
        gains = mine(width // shards)
        for i, out in enumerate((r.norm_self, r.norm_cross, r.norm_feed)):
            out[...] = gains[i : i + 1, : width // shards].reshape(out.shape)
        cut, heads = r.bucket_bias.shape
        r.bucket_bias[...] = mine(cut)[8:24, :LANES].T[:cut, :heads]


def finish(made, result, table_shape, shards):
    units, _, q, half = made.fin.shape
    rows, width = made.d_tokens.shape
    steps = units // 4
    still = lambda *shape: pl.BlockSpec(shape, lambda n: (0,) * len(shape))
    line = pl.BlockSpec((rows // steps, width), lambda n: (n, 0))
    unit = lambda group: pl.BlockSpec((1, 2, q, half), lambda n: (group * steps + n, 0, 0, 0))
    pair = lambda first: pl.BlockSpec((1, q, width), lambda n: (jnp.where(n <= first, 0, 1), 0, 0))
    squares = (
        (("cross_output", 0, 1), ("cross_keyval", 1, 2), ("cross_query", 3, 1)),
        (("self_output", 0, 1), ("self_keyval", 1, 2), ("self_query", 3, 1)),
    )
    square = ((q, width), still(q, width))
    outs = dict(
        feed_in=((q, steps * width), pl.BlockSpec((q, width), lambda n: (0, n))),
        feed_out=((steps * q, width), pl.BlockSpec((q, width), lambda n: (n, 0))),
        cross_output=square,
        cross_keyval=((2, q, width), pair(1)),
        cross_query=square,
        self_output=square,
        self_keyval=((2, q, width), pair(1)),
        self_query=square,
        d_tokens=((rows, width), line),
        d_memory=((rows, width), line),
        result=((rows, width), line),
        norm_self=((q,), still(q)),
        norm_cross=((q,), still(q)),
        norm_feed=((q,), still(q)),
        bucket_bias=(table_shape, still(*table_shape)),
    )
    names = ("fin_in", "fin_out", "fin_cross", "fin_self", "tokens_in", "memory_in", "result_in", "small")
    done = pl.pallas_call(
        functools.partial(finish_kernel, squares, shards, names + tuple(outs)),
        grid=(steps,),
        in_specs=[unit(1), unit(0), unit(2), unit(3), line, line, line, still(*made.small_out.shape)],
        out_specs=[spec for _, spec in outs.values()],
        out_shape=[
            jax.ShapeDtypeStruct(shape, BF16 if name == "result" else F32)
            for name, (shape, _) in outs.items()
        ],
        compiler_params=pltpu.CompilerParams(vmem_limit_bytes=VMEM_LIMIT),
    )(*[made.fin] * 4, made.d_tokens, made.d_memory, result, made.small_out)
    return types.SimpleNamespace(**dict(zip(outs, done)))


def tiles_evenly(reps, shards, width):
    if reps % 4 or shards % 2 or width % shards:
        return False
    return (width // shards) % (8 * reps) == 0 and width % (4 * HD) == 0


def layer(
    tokens,
    encoded,
    block_ids,
    buckets,
    cotangent,
    norm_self,
    self_query,
    self_keyval,
    self_output,
    bucket_bias,
    norm_cross,
    cross_query,
    cross_keyval,
    cross_output,
    norm_feed,
    feed_in,
    feed_out,
):
    groups, positions, model_width = tokens.shape
    reps, shards = lax.axis_size("rep"), lax.axis_size("shard")
    length = (buckets.shape[0] + 1) // 2
    memory_local = encoded.shape[1]
    row_anchor = lax.axis_index("shard") * positions
    heads, bucket_count = bucket_bias.shape[0], bucket_bias.shape[1] * shards
    window_width = length + positions
    fused = tiles_evenly(reps, shards, model_width) and encoded.shape == tokens.shape
    fused = fused and feed_out.shape[0] == model_width
    fused = fused and feed_in.shape[1] == 4 * model_width and positions % LANES == 0
    if fused:
        gains = (norm_self, norm_cross, norm_feed)
        matrices = (self_query, self_keyval, self_output, cross_query, cross_keyval, cross_output)
        matrices += (feed_in, feed_out)
        held = forward(
            tokens[0], encoded[0], block_ids, buckets, gains, bucket_bias.T, matrices, reps, shards
        )
        made = backward(tokens[0], cotangent[0], buckets, held, reps, shards)
        out = finish(made, held.result, bucket_bias.T.shape, shards)
        return (
            out.result[None],
            out.d_tokens[None],
            out.d_memory[None],
            out.norm_self,
            out.self_query,
            out.self_keyval,
            out.self_output,
            out.bucket_bias.T,
            out.norm_cross,
            out.cross_query,
            out.cross_keyval,
            out.cross_output,
            out.norm_feed,
            out.feed_in,
            out.feed_out,
        )

    inputs = tokens[0].astype(F32)
    encoded_whole = gather(encoded[0])
    ids_whole = gather(block_ids[0])
    gains = gather(jnp.stack([norm_self, norm_cross, norm_feed]), 1).astype(F32)
    gain_first, gain_second, gain_third = gains[0:1], gains[1:2], gains[2:3]
    query_first, keyval_first, output_first, table = (
        gather(self_query),
        gather(self_keyval, 1),
        gather(self_output),
        gather(bucket_bias, 1),
    )
    query_second, keyval_second, output_second = (
        gather(cross_query),
        gather(cross_keyval, 1),
        gather(cross_output),
    )
    inner, outer = gather(feed_in), gather(feed_out)

    window_buckets = lax.dynamic_slice_in_dim(
        jnp.pad(buckets, (1, 0)), length - row_anchor - positions, window_width
    )
    onehot = window_buckets[None, :] == jnp.arange(bucket_count, dtype=jnp.int32)[:, None]
    window = dot(table, onehot.astype(BF16)).reshape(heads // 2, 2, window_width)

    normed_first = (inputs * rms_scale(inputs) * gain_first).astype(BF16)
    normed_whole = gather(normed_first)
    query = dot(normed_first, query_first).astype(BF16)
    keys = dot(normed_whole, keyval_first[0]).astype(BF16)
    values = dot(normed_whole, keyval_first[1]).astype(BF16)
    attended, weights = attend(
        query, keys, values, (block_ids[0][:, None], ids_whole[None, :], window)
    )
    low_first = attended.astype(BF16)
    first = inputs + dot(low_first, output_first)

    memory_keys = dot(encoded_whole, keyval_second[0]).astype(BF16)
    memory_values = dot(encoded_whole, keyval_second[1]).astype(BF16)
    normed_second = (first * rms_scale(first) * gain_second).astype(BF16)
    query_cross = dot(normed_second, query_second).astype(BF16)
    attended_cross, weights_cross = attend(query_cross, memory_keys, memory_values)
    low_second = attended_cross.astype(BF16)
    second = first + dot(low_second, output_second)

    normed_third = (second * rms_scale(second) * gain_third).astype(BF16)
    preact = dot(normed_third, inner)
    value, slope = gelu_parts(preact)
    hidden = value.astype(BF16)
    result = (second + dot(hidden, outer)).astype(BF16)

    grad_result = cotangent[0]
    d_outer = dot_tn(hidden, grad_result)
    grad_preact = (dot_nt(grad_result, outer) * slope).astype(BF16)
    d_inner = dot_tn(normed_third, grad_preact)
    back, d_gain_third = rms_back(second, gain_third, dot_nt(grad_preact, inner))
    grad_second = grad_result.astype(F32) + back

    grad_second_low = grad_second.astype(BF16)
    d_output_second = dot_tn(low_second, grad_second_low)
    grad_att = dot_nt(grad_second_low, output_second).astype(BF16)
    d_query, d_keys, d_values = attend_back(
        query_cross, memory_keys, memory_values, weights_cross, attended_cross, grad_att
    )
    d_keyval_second = jnp.stack(
        [dot_tn(encoded_whole, d_keys), dot_tn(encoded_whole, d_values)]
    )
    d_memory = scatter(dot_nt(d_keys, keyval_second[0]) + dot_nt(d_values, keyval_second[1]))
    d_query_second = dot_tn(normed_second, d_query)
    back, d_gain_second = rms_back(first, gain_second, dot_nt(d_query, query_second))
    grad_first = grad_second + back

    grad_first_low = grad_first.astype(BF16)
    d_output_first = dot_tn(low_first, grad_first_low)
    grad_att = dot_nt(grad_first_low, output_first).astype(BF16)
    d_query, d_keys, d_values, d_window = attend_back(
        query, keys, values, weights, attended, grad_att, window.shape
    )
    d_table = lax.dot_general(
        d_window.reshape(heads, window_width),
        onehot.astype(F32),
        (((1,), (1,)), ((), ())),
        precision=lax.Precision.HIGHEST,
    )
    d_keyval_first = jnp.stack([dot_tn(normed_whole, d_keys), dot_tn(normed_whole, d_values)])
    grad_normed = scatter(
        dot_nt(d_keys, keyval_first[0]) + dot_nt(d_values, keyval_first[1])
    ).astype(F32) + dot_nt(d_query, query_first)
    d_query_first = dot_tn(normed_first, d_query)
    back, d_gain_first = rms_back(inputs, gain_first, grad_normed)
    d_inputs = grad_first + back

    gains = [d_gain_first, d_gain_second, d_gain_third]
    squares = [d_query_first, d_output_first, d_query_second, d_output_second]
    pairs = [d_keyval_first, d_keyval_second]
    total = lambda a, axis=0: lax.psum(scatter(a, axis), "rep").astype(F32)
    gains = [total(gain[0]) for gain in gains]
    squares = [total(square) for square in squares]
    pairs = [total(pair, 1) for pair in pairs]
    d_table, d_inner, d_outer = total(d_table, 1), total(d_inner), total(d_outer)
    totals = (gains[0], squares[0], pairs[0], squares[1], d_table)
    totals += (gains[1], squares[2], pairs[1], squares[3], gains[2], d_inner, d_outer)
    return (result[None], d_inputs[None], d_memory.astype(F32)[None]) + totals


def solution(mesh):
    rows, line = P("rep", "shard", None), P("shard")
    matrix, pair, table = P("shard", None), P(None, "shard", None), P(None, "shard")
    weights = (line, matrix, pair, matrix, table, line, matrix, pair, matrix, line, matrix, matrix)
    return jax.shard_map(
        layer,
        mesh=mesh,
        in_specs=(rows, rows, P("rep", "shard"), P(), rows) + weights,
        out_specs=(rows, rows, rows) + weights,
        check_vma=False,
    )
```
